128 devices in a mesh: row: 16 (over z, y_hi, core), col: 8 (over y_lo, x).
Axes of the slice: x: 4, y: 4 (y_hi: 2, y_lo: 2; y = y_hi * 2 + y_lo), z: 4, core: 2. Of those that a mesh axis runs over, the one named last changes fastest.
Arguments:
- tokens: bfloat16 [1024, 6144], P('col', 'row'), may hold values from -160 to 160
- ln_gain: float32 [6144], P('row'), may hold values from 0.5 to 1.5
- w_up: bfloat16 [6144, 24576], P('row', 'col'), may hold values from -0.078125 to 0.078125
- w_down: bfloat16 [24576, 6144], P('col', 'row'), may hold values from -0.0390625 to 0.0390625
- proj: bfloat16 [6144, 256], P('row'), may hold values from -0.078125 to 0.078125
- conv_kernel: bfloat16 [3, 3, 256, 256], replicated, may hold values from -0.125 to 0.125
- head_weight: float32 [256], replicated, may hold values from -0.375 to 0.375
- depth_mm: int32 [16, 64], P('col'), may hold values from 1000 to 80000
- lidar_mask: int32 [16, 64], P('col'), may hold values from 0 to 1, as said below
Outputs:
- grad_up: float32 [6144, 24576], P('row', 'col')
- grad_down: float32 [24576, 6144], P('col', 'row')
- loss: float32 [], replicated
The draws below stay inside these ranges and needn't reach their ends.
Inputs may be any that keep to these rules, and one draw needn't show every extreme that they name: `lidar_mask`: at least one entry is 1.
All inputs are finite; a program needn't handle non-finite values.
Results may differ from the reference program's by a relative error of at most 0.04.
Values may be sent and summed in bfloat16 or wider, within the bound.
A program may use at most 128 MiB of HBM per device.

```python
import jax
import jax.numpy as jnp
from jax import lax

D = 6144
FF = 24576
F = 256
GW = 64
TOKENS = 1024
GH = 16
N_ROW = 16
N_COL = 8


def draw_tokens(key, part):
    key = jax.random.fold_in(key, 11)
    key_base, key_column = jax.random.split(key, 2)
    position = jnp.arange(D, dtype=jnp.float32) / D
    column = 0.5 * 3.0 ** position * jnp.exp(jax.random.uniform(key_column, (D,), jnp.float32, -0.7, 0.7))
    base = jnp.clip(jax.random.normal(key_base, (TOKENS, D), jnp.float32), -6.0, 6.0)
    return (base * column[None, :]).astype(jnp.bfloat16)


def draw_lidar_mask(key, part):
    key = jax.random.fold_in(key, 23)
    key_ticket, key_spot = jax.random.split(key, 2)
    ticket = jax.random.randint(key_ticket, (GH, GW), 0, 1000)
    level = 250 + 500 * jnp.arange(GH, dtype=jnp.int32) // max(GH - 1, 1)
    drawn = (ticket < level[:, None]).astype(jnp.int32)
    spot = jax.random.randint(key_spot, (), 0, GH * GW)
    forced = (jnp.arange(GH * GW, dtype=jnp.int32) == spot).astype(jnp.int32).reshape(GH, GW)
    return jnp.maximum(drawn, forced)


def draw_depth_mm(key, part):
    key = jax.random.fold_in(key, 37)
    lowest = 1000 + 39000 * jnp.arange(GH, dtype=jnp.int32) // max(GH - 1, 1)
    lower = jnp.broadcast_to(lowest[:, None], (GH, GW))
    return jax.random.randint(key, (GH, GW), lower, 2 * lower + 1)


def shard_levels(own_key, shape, cuts, smallest, top_value):
    factor_of, own = 1.0, jax.random.fold_in(own_key, 6)
    for axis_at, parts in cuts:
        steps = jnp.exp(jax.random.uniform(jax.random.fold_in(own, axis_at), (parts,), jnp.float32, smallest / len(cuts), top_value / len(cuts)))
        factor_of = factor_of * jnp.repeat(steps, shape[axis_at] // parts).reshape([-1 if axis == axis_at else 1 for axis in range(len(shape))])
    return factor_of


def scatter_about(rng, extent, scale, bound, cuts=(), held_as=jnp.bfloat16):
    values = scale * jax.random.normal(rng, extent, jnp.float32)
    if cuts:
        values = values * shard_levels(rng, extent, cuts, -0.22, 0.18)
    return jnp.clip(values, -bound, bound).astype(held_as)


def setup_inputs(seed: int = 0) -> dict:
    arg_keys = jax.random.split(jax.random.key(seed), 10)
    return {
        "tokens": draw_tokens(jax.random.fold_in(arg_keys[9], 71), 0),
        "ln_gain": jnp.clip(0.5 + 1.0 * jax.random.uniform(arg_keys[1], (D,), jnp.float32) ** shard_levels(arg_keys[1], (D,), ((0, 16),), -0.2, 0.2), 0.5, 1.5),
        "w_up": scatter_about(arg_keys[2], (D, FF), D ** -0.5, 0.078125, ((0, 16), (1, 8))),
        "w_down": scatter_about(arg_keys[3], (FF, D), FF ** -0.5, 0.0390625, ((0, 8), (1, 16))),
        "proj": scatter_about(arg_keys[4], (D, F), D ** -0.5, 0.078125, ((0, 16),)),
        "conv_kernel": scatter_about(arg_keys[5], (3, 3, F, F), (9 * F) ** -0.5, 0.125),
        "head_weight": scatter_about(arg_keys[6], (F,), F ** -0.5, 0.375, (), jnp.float32),
        "depth_mm": draw_depth_mm(jax.random.fold_in(arg_keys[9], 71), 0),
        "lidar_mask": draw_lidar_mask(jax.random.fold_in(arg_keys[9], 71), 0),
    }


variance_focus = 0.85
norm_eps = 1e-06

def normalize(values, first, second, gain, width):
    mean = first / width
    spread = second / width - mean * mean
    return (values - mean[:, None]) * lax.rsqrt(spread + norm_eps)[:, None] * gain[None, :]

def gelu_exact(values):
    return jax.nn.gelu(values, approximate=False)

def gelu_back(pre, cotangent):
    _, pull = jax.vjp(gelu_exact, pre)
    return pull(cotangent)[0]

def rounded(term):
    return lax.optimization_barrier(term.astype(jnp.bfloat16)).astype(jnp.float32)

def neighbours(field, offsets):
    height = field.shape[0] - 2
    across = field.shape[1] - 2
    return jnp.concatenate([field[a:a + height, b:b + across, :].reshape(height * across, -1) for a, b in offsets], axis=1)

def reference(tokens, ln_gain, w_up, w_down, proj, conv_kernel, head_weight, depth_mm, lidar_mask):
    xf = tokens.astype(jnp.float32)
    normed = normalize(xf, lax.optimization_barrier(jnp.sum(xf, 1)), lax.optimization_barrier(jnp.sum(xf * xf, 1)), ln_gain, D).astype(jnp.bfloat16)
    block = D // N_ROW
    pre = jnp.zeros((TOKENS, FF), jnp.float32)
    for index in range(N_ROW):
        pre = pre + rounded(jnp.dot(normed[:, index * block:(index + 1) * block], w_up[index * block:(index + 1) * block], preferred_element_type=jnp.float32))
    hidden = gelu_exact(pre).astype(jnp.bfloat16)
    hblock = FF // N_COL
    out = jnp.zeros((TOKENS, D), jnp.float32)
    for index in range(N_COL):
        out = out + rounded(jnp.dot(hidden[:, index * hblock:(index + 1) * hblock], w_down[index * hblock:(index + 1) * hblock], preferred_element_type=jnp.float32))
    mixed = (xf + out).astype(jnp.bfloat16)
    z = jnp.dot(mixed, proj, preferred_element_type=jnp.float32)
    forward_offsets = [(i, j) for i in range(3) for j in range(3)]
    backward_offsets = [(2 - i, 2 - j) for i in range(3) for j in range(3)]
    act = gelu_exact(z).astype(jnp.bfloat16).reshape(GH, GW, F)
    padded = jnp.pad(act, ((1, 1), (1, 1), (0, 0)))
    u = z + jnp.dot(neighbours(padded, forward_offsets), conv_kernel.reshape(9 * F, F), preferred_element_type=jnp.float32)
    pred = jnp.dot(u, head_weight, precision=lax.Precision.HIGHEST)
    valid = lidar_mask.reshape(-1).astype(jnp.float32)
    target = jnp.log(depth_mm.reshape(-1).astype(jnp.float32) * 0.001)
    err = valid * (pred - target)
    count = jnp.sum(valid)
    mean_err = jnp.sum(err) / count
    loss = jnp.sum(err * err) / count - variance_focus * mean_err * mean_err
    grad_pred = valid * (2.0 * err - 2.0 * variance_focus * mean_err)
    grad_u = grad_pred[:, None] * head_weight[None, :]
    grad_pad = jnp.pad(grad_u.astype(jnp.bfloat16).reshape(GH, GW, F), ((1, 1), (1, 1), (0, 0)))
    back_kernel = jnp.swapaxes(conv_kernel, 2, 3).reshape(9 * F, F)
    back_conv = jnp.dot(neighbours(grad_pad, backward_offsets), back_kernel, preferred_element_type=jnp.float32)
    grad_z = grad_u + gelu_back(z, back_conv)
    grad_mixed = jnp.dot(grad_z.astype(jnp.bfloat16), proj.T, preferred_element_type=jnp.float32).astype(jnp.bfloat16)
    grad_down = lax.dot_general(hidden, grad_mixed, (((0,), (0,)), ((), ())), preferred_element_type=jnp.float32)
    back = jnp.zeros((TOKENS, FF), jnp.float32)
    for index in range(N_ROW):
        back = back + rounded(lax.dot_general(grad_mixed[:, index * block:(index + 1) * block], w_down[:, index * block:(index + 1) * block], (((1,), (1,)), ((), ())), preferred_element_type=jnp.float32))
    grad_pre = gelu_back(pre, back).astype(jnp.bfloat16)
    grad_up = lax.dot_general(normed, grad_pre, (((0,), (0,)), ((), ())), preferred_element_type=jnp.float32)
    return (grad_up, grad_down, loss)
```

```python
import math

import jax
import jax.numpy as jnp
from jax import lax
from jax.experimental import pallas as pl
from jax.experimental.pallas import tpu as pltpu
from jax.sharding import PartitionSpec as P

MESH = pl.DeviceIdType.MESH
F32 = jnp.float32
BF16 = jnp.bfloat16

WIDTH = 6144
GW = 64
GH = 16
TOK = 1024
STRIP = 128
FEAT = 384
HID = 3072
HALF = 1536
OWN = 192
CH = 256
TA = 512
TB = TOK - TA
GA = TA + CH
FOCUS = 0.85
EPS = 1e-06

ROOT_HALF = math.sqrt(0.5)
DENSITY = 1.0 / math.sqrt(2.0 * math.pi)

N_SEMS = 192


def cdf(v):
    return 0.5 * (1.0 + lax.erf(v * ROOT_HALF))


def slope(v):
    return cdf(v) + v * (DENSITY * jnp.exp(-0.5 * v * v))


def tn(a, b):
    return lax.dot_general(a, b, (((0,), (0,)), ((), ())), preferred_element_type=F32)


def nt(a, b):
    return lax.dot_general(a, b, (((1,), (1,)), ((), ())), preferred_element_type=F32)


def mm(a, b):
    return jnp.dot(a, b, preferred_element_type=F32)


def step_kernel(
    tok_ref, gain_ref, wup_ref, wdn_hbm, proj_ref, conv_hbm, head_ref, depth_ref, mask_ref,
    nt_out, ga_out, gb_out, loss_ref,
    wdn, conv, xall, st_row, st_col, w_t, w_send, wd_peer, proj_peer, n_t, m_part, m_recv, m_own,
    p_a, p_b, a1, a2, a3, b1, b2, b3, pre, hid, der, zc, z1, z1_recv, z2, z2_recv, z3,
    pred_all, rows_buf, gz, ga_own, gb_own, send_sems, recv_sems, local_sems,
):
    row, col = lax.axis_index("row"), lax.axis_index("col")
    z, h, c = row // 4, lax.rem(row // 2, 2), lax.rem(row, 2)
    used = [0]

    def zz(dz):
        return lax.rem(z + dz + 4, 4)

    def hh(dh):
        return lax.rem(h + dh, 2)

    def at_row(dz, dh, dc):
        return {"row": zz(dz) * 4 + hh(dh) * 2 + lax.rem(c + dc, 2)}

    def at_col(dl, dx):
        return {"col": lax.rem(col // 4 + dl, 2) * 4 + lax.rem(lax.rem(col, 4) + dx, 4)}

    def remote(src, dst, device):
        at = used[0]
        used[0] += 1
        copy = pltpu.make_async_remote_copy(
            src_ref=src, dst_ref=dst, send_sem=send_sems.at[at], recv_sem=recv_sems.at[at],
            device_id=device, device_id_type=MESH,
        )
        copy.start()
        sent.append(copy)
        return copy

    sent = []
    row_peers = [
        (dz, dh, dc) for dz in (2, 1, 3, 0) for dh in (1, 0) for dc in (1, 0) if (dz, dh, dc) != (0, 0, 0)
    ]
    chip_peers = [(dz, dh) for dz in (2, 1, 3, 0) for dh in (1, 0) if (dz, dh) != (0, 0)]
    col_peers = [(dl, dx) for dl in (1, 0) for dx in (2, 1, 3, 0) if (dl, dx) != (0, 0)]
    partner = at_row(0, 0, 1)
    here = z * 2 + h
    other = 1 - c

    barrier = pltpu.get_barrier_semaphore()
    for peer in row_peers:
        pl.semaphore_signal(barrier, inc=1, device_id=at_row(*peer), device_id_type=MESH)
    for peer in col_peers:
        pl.semaphore_signal(barrier, inc=1, device_id=at_col(*peer), device_id_type=MESH)

    wdn_copy = pltpu.make_async_copy(wdn_hbm, wdn, local_sems.at[0])
    wdn_copy.start()
    first_channel = pl.multiple_of(c * 128 + here * 16, 16)
    conv_copy = pltpu.make_async_copy(
        conv_hbm.at[:, pl.ds(first_channel, 16), :], conv, local_sems.at[1]
    )
    conv_copy.start()

    x_t = tok_ref[...].astype(F32).T
    xall[col] = x_t.astype(BF16)
    st_row[row] = jnp.concatenate(
        [
            jnp.sum(x_t, 0, keepdims=True),
            jnp.sum(x_t * x_t, 0, keepdims=True),
            jnp.zeros((6, STRIP), F32),
        ],
        axis=0,
    )
    pl.semaphore_wait(barrier, len(row_peers) + len(col_peers))

    stat_copies = [remote(st_row.at[row], st_row.at[row], at_row(*peer)) for peer in row_peers]
    token_copies = [remote(xall.at[col], xall.at[col], at_col(*peer)) for peer in col_peers]
    wdn_copy.wait()
    to_peer = pl.multiple_of(other * HALF, HALF)
    wd_copy = remote(wdn.at[pl.ds(to_peer, HALF)], wd_peer, partner)
    proj_copy = remote(proj_ref, proj_peer, partner)

    feature_at = pl.multiple_of(c * FEAT, 128)

    @pl.loop(0, HALF // 128)
    def _(i):
        at = pl.multiple_of(to_peer + i * 128, 128)
        w_send[pl.ds(pl.multiple_of(i * 128, 128), 128), :] = wup_ref[:, pl.ds(at, 128)].T

    w_copy = remote(w_send, w_t.at[:, pl.ds(feature_at, FEAT)], partner)

    for copy in stat_copies:
        copy.wait_recv()
    total = st_row[0]
    for index in range(1, 16):
        total = total + st_row[index]
    mean = total[0:1] / WIDTH
    spread = total[1:2] / WIDTH - mean * mean
    depth = depth_ref[...].astype(F32)
    seen = mask_ref[...].astype(F32)
    st_col[col] = jnp.concatenate(
        [
            mean,
            lax.rsqrt(spread + EPS),
            jnp.concatenate([seen[0:1], seen[1:2]], axis=1),
            jnp.log(jnp.concatenate([depth[0:1], depth[1:2]], axis=1) * 0.001),
            jnp.zeros((4, STRIP), F32),
        ],
        axis=0,
    )
    norm_copies = [remote(st_col.at[col], st_col.at[col], at_col(*peer)) for peer in col_peers]

    own_half = pl.multiple_of(c * HALF, HALF)

    @pl.loop(0, HALF // 128)
    def _(i):
        at = pl.multiple_of(own_half + i * 128, 128)
        w_t[pl.ds(pl.multiple_of(i * 128, 128), 128), pl.ds(feature_at, FEAT)] = wup_ref[:, pl.ds(at, 128)].T

    wd_copy.wait_recv()
    proj_copy.wait_recv()

    @pl.loop(0, 8)
    def _(k):
        at = pl.multiple_of(k * OWN, 64)
        m_part[k] = (
            mm(wdn[pl.ds(own_half + at, OWN), :], proj_ref[...]) + mm(wd_peer[pl.ds(at, OWN), :], proj_peer[...])
        ).astype(BF16)

    m_copies = []
    for index, (dz, dh) in enumerate(chip_peers):
        m_copies.append(
            remote(m_part.at[zz(dz) * 2 + hh(dh)], m_recv.at[index], at_row(dz, dh, 0))
        )

    gain = jnp.broadcast_to(gain_ref[...], (STRIP, FEAT)).T
    for copy in norm_copies:
        copy.wait_recv()
    for copy in token_copies:
        copy.wait_recv()

    for index in range(8):
        stats = st_col[index]
        n_t[pl.ds(feature_at, FEAT), index * STRIP : (index + 1) * STRIP] = (
            (xall[index].astype(F32) - stats[0:1]) * stats[1:2] * gain
        ).astype(BF16)
    n_own = n_t.at[pl.ds(feature_at, FEAT)]
    n_copy = remote(n_own, n_own, partner)
    n_out_copy = pltpu.make_async_copy(n_own, nt_out, local_sems.at[2])
    n_out_copy.start()
    w_copy.wait_recv()
    n_copy.wait_recv()

    a_copies, b_copies = {}, {}

    def project(dz):
        base = pl.multiple_of(zz(dz) * 2 * OWN, 2 * OWN)

        @pl.loop(0, TOK // 256)
        def _(t):
            at = pl.multiple_of(t * 256, 256)
            both = mm(w_t[pl.ds(base, 2 * OWN), :], n_t[:, pl.ds(at, 256)]).astype(BF16)

            @pl.when(t < TA // 256)
            def _():
                p_a[zz(dz), 0, :, pl.ds(at, 256)] = both[:OWN]
                p_a[zz(dz), 1, :, pl.ds(at, 256)] = both[OWN:]

            @pl.when(t >= TA // 256)
            def _():
                at_b = pl.multiple_of(jnp.maximum(at - TA, 0), 256)
                p_b[zz(dz), 0, :, pl.ds(at_b, 256)] = both[:OWN]
                p_b[zz(dz), 1, :, pl.ds(at_b, 256)] = both[OWN:]

    up, down, flip = at_row(1, 0, 0), at_row(3, 0, 0), at_row(0, 1, 0)
    for dz in (2, 1, 3, 0):
        project(dz)
        b_copies[dz] = remote(p_b.at[zz(dz), 1 - h], b1.at[zz(dz)], flip)
        if dz == 2:
            a_up = remote(p_a.at[zz(2), 0], a1.at[0], up)
            a_down = remote(p_a.at[zz(2), 1], a1.at[1], down)

    def add(into, more):
        into[...] = (into[...].astype(F32) + more[...].astype(F32)).astype(BF16)

    a_up.wait_recv()
    add(p_a.at[zz(1), 0], a1.at[0])
    a_up2 = remote(p_a.at[zz(1)], a2.at[0], up)
    a_down.wait_recv()
    add(p_a.at[zz(3), 1], a1.at[1])
    a_down2 = remote(p_a.at[zz(3)], a2.at[1], down)

    b_copies[2].wait_recv()
    add(p_b.at[zz(2), h], b1.at[zz(2)])
    b_up = remote(p_b.at[zz(2), h, 0:96], b2.at[0], up)
    b_down = remote(p_b.at[zz(2), h, 96:192], b2.at[1], down)
    b_copies[1].wait_recv()
    add(p_b.at[zz(1), h], b1.at[zz(1)])
    b_copies[3].wait_recv()
    add(p_b.at[zz(3), h], b1.at[zz(3)])

    a_up2.wait_recv()
    a_down2.wait_recv()
    p_a[z, 1 - h] = (
        p_a[z, 1 - h].astype(F32) + a2[0, 1 - h].astype(F32) + a2[1, 1 - h].astype(F32)
    ).astype(BF16)
    a_flip = remote(p_a.at[z, 1 - h], a3, flip)

    b_up.wait_recv()
    add(p_b.at[zz(1), h, 0:96], b2.at[0])
    b_up2 = remote(p_b.at[zz(1), h], b3.at[0], up)
    b_down.wait_recv()
    add(p_b.at[zz(3), h, 96:192], b2.at[1])
    b_down2 = remote(p_b.at[zz(3), h], b3.at[1], down)

    for copy in m_copies:
        copy.wait_recv()
    m_sum = m_part[here].astype(F32)
    for index in range(7):
        m_sum = m_sum + m_recv[index].astype(F32)
    m_own[...] = m_sum.astype(BF16)
    x_proj = tn(proj_ref[...], xall[col])

    conv_copy.wait()
    head = head_ref[...]
    taps = [jnp.sum(conv[k].astype(F32) * head, axis=1, keepdims=True) for k in range(9)]
    lane = lax.broadcasted_iota(jnp.int32, (16, CH), 1)
    sub = lax.broadcasted_iota(jnp.int32, (16, CH), 0)
    head_col = jnp.sum(jnp.where(lane == sub + first_channel, head, 0.0), axis=1, keepdims=True)

    b_copies[0].wait_recv()
    a_flip.wait_recv()
    pre[:, :TA] = (
        p_a[z, h].astype(F32) + a2[0, h].astype(F32) + a2[1, h].astype(F32) + a3[...].astype(F32)
    )
    b_up2.wait_recv()
    b_down2.wait_recv()
    pre[:, TA:] = (
        p_b[z, h].astype(F32) + b1[z].astype(F32) + b3[0].astype(F32) + b3[1].astype(F32)
    )

    @pl.loop(0, TOK // 128)
    def _(t):
        at = pl.ds(pl.multiple_of(t * 128, 128), 128)
        value = pre[:, at]
        hid[:, at] = (value * cdf(value)).astype(BF16)

    @pl.loop(0, TOK // 256)
    def _(t):
        at = pl.ds(pl.multiple_of(t * 256, 256), 256)
        zc[:, at] = tn(m_own[...], hid[:, at])

    strip = pl.ds(pl.multiple_of(col * STRIP, STRIP), STRIP)
    zc[:, strip] = zc[:, strip] + x_proj

    z1[...] = zc[pl.ds(pl.multiple_of(other * 128, 128), 128), :].astype(BF16)
    z1_copy = remote(z1, z1_recv, partner)

    @pl.loop(0, TOK // 128)
    def _(t):
        at = pl.ds(pl.multiple_of(t * 128, 128), 128)
        der[:, at] = slope(pre[:, at])

    z1_copy.wait_recv()
    z2[...] = (
        zc[pl.ds(pl.multiple_of(c * 128, 128), 128), :] + z1_recv[...].astype(F32)
    ).astype(BF16)
    z2_copies = []
    for index, (dz, dh) in enumerate(chip_peers):
        at = pl.multiple_of((zz(dz) * 2 + hh(dh)) * 16, 16)
        z2_copies.append(remote(z2.at[pl.ds(at, 16)], z2_recv.at[index], at_row(dz, dh, 0)))
    part = z2[pl.ds(pl.multiple_of(here * 16, 16), 16), :].astype(F32)
    for index, copy in enumerate(z2_copies):
        copy.wait_recv()
        part = part + z2_recv[index].astype(F32)
    z3[col] = part.astype(BF16)
    z3_copies = [remote(z3.at[col], z3.at[col], at_col(*peer)) for peer in col_peers]
    for copy in z3_copies:
        copy.wait_recv()
    field = z3[0].astype(F32)
    for index in range(1, 8):
        field = field + z3[index].astype(F32)

    token = lax.broadcasted_iota(jnp.int32, (1, TOK), 1)
    line, place = token >> 6, token & (GW - 1)

    def moved(values, di, dj):
        shift = di * GW + dj
        if shift:
            values = pltpu.roll(values, (-shift) % TOK, 1)
        inside = (
            (line + di >= 0) & (line + di < GH) & (place + dj >= 0) & (place + dj < GW)
        )
        return jnp.where(inside, values, 0.0)

    act = (field * cdf(field)).astype(BF16).astype(F32)
    pred = jnp.sum(field * head_col, axis=0, keepdims=True)
    for k in range(9):
        pred = pred + moved(jnp.sum(act * taps[k], axis=0, keepdims=True), k // 3 - 1, k % 3 - 1)
    for index in range(8):
        rows_buf[index : index + 1, :] = pred[:, index * STRIP : (index + 1) * STRIP]
    pred_all[row] = rows_buf[...]
    pred_copies = [remote(pred_all.at[row], pred_all.at[row], at_row(*peer)) for peer in row_peers]
    field_slope = slope(field)
    valid = jnp.concatenate([st_col[index][2:3] for index in range(8)], axis=0)
    target = jnp.concatenate([st_col[index][3:4] for index in range(8)], axis=0)
    for copy in pred_copies:
        copy.wait_recv()
    pred = pred_all[0]
    for index in range(1, 16):
        pred = pred + pred_all[index]

    err = valid * (pred - target)

    def whole(values):
        return jnp.sum(jnp.sum(values, axis=1, keepdims=True), axis=0, keepdims=True)

    count = whole(valid)
    mean_err = whole(err) / count
    loss_ref[...] = jnp.broadcast_to(
        whole(err * err) / count - FOCUS * mean_err * mean_err, loss_ref.shape
    )
    grad_pred = valid * (2.0 * err - 2.0 * FOCUS * mean_err)
    grad_pred = jnp.concatenate([grad_pred[index : index + 1] for index in range(8)], axis=1)
    back = jnp.zeros((16, TOK), F32)
    for k in range(9):
        back = back + taps[k] * moved(grad_pred, 1 - k // 3, 1 - k % 3)
    mine = pl.ds(first_channel, 16)
    gz[mine, :] = (grad_pred * head_col + field_slope * back).astype(BF16)

    gz_copies = [
        remote(gz.at[mine], gz.at[mine], at_row(dz, dh, 0)) for dz, dh in chip_peers
    ]
    gz_pair = [remote(gz.at[mine], gz.at[mine], partner)]
    for (dz, dh), copy in zip(chip_peers, gz_copies):
        copy.wait_recv()
        came = gz.at[pl.ds(pl.multiple_of(c * 128 + (zz(-dz) * 2 + hh(dh)) * 16, 16), 16)]
        gz_pair.append(remote(came, came, partner))
    for copy in gz_pair:
        copy.wait_recv()

    @pl.loop(0, TOK // 256)
    def _(t):
        at = pl.multiple_of(t * 256, 256)
        lanes = pl.ds(at, 256)
        grad = (mm(m_own[...], gz[:, lanes]) * der[:, lanes]).astype(BF16)

        @pl.when(t < TA // 256)
        def _():
            ga_own[:, lanes] = grad

        @pl.when(t >= TA // 256)
        def _():
            gb_own[:, pl.ds(pl.multiple_of(jnp.maximum(at - TA, 0), 256), 256)] = grad

    ga_own[:, TA:] = nt(hid[...], gz[...]).astype(BF16)

    def slot(dz, dh):
        return c * 8 + zz(dz) * 2 + hh(dh)

    mine_a, mine_b = ga_out.at[slot(0, 0)], gb_out.at[slot(0, 0)]
    own_copies = [
        pltpu.make_async_copy(ga_own, mine_a, local_sems.at[3]),
        pltpu.make_async_copy(gb_own, mine_b, local_sems.at[4]),
    ]
    fa = remote(ga_own, mine_a, flip)
    bu = remote(gb_own, mine_b, up)
    bd = remote(gb_own, mine_b, down)
    fb = remote(gb_own, mine_b, flip)
    au = remote(ga_own, mine_a, up)
    ad = remote(ga_own, mine_a, down)
    for copy in own_copies:
        copy.start()
    pair = [remote(ga_own, mine_a, partner), remote(gb_own, mine_b, partner)]

    def send(buf, dz, dh, device, rows=None):
        ref = buf.at[slot(dz, dh)] if rows is None else buf.at[slot(dz, dh), rows[0] : rows[1]]
        return remote(ref, ref, device)

    top, low = (0, 96), (96, 192)
    bu.wait_recv()
    bu2 = send(gb_out, 3, 0, up, top)
    f_m = send(gb_out, 3, 0, flip)
    pair.append(send(gb_out, 3, 0, partner))
    bd.wait_recv()
    bd2 = send(gb_out, 1, 0, down, low)
    f_p = send(gb_out, 1, 0, flip)
    pair.append(send(gb_out, 1, 0, partner))
    fa.wait_recv()
    fau = send(ga_out, 0, 1, up)
    fad = send(ga_out, 0, 1, down)
    pair.append(send(ga_out, 0, 1, partner))
    fb.wait_recv()
    pair.append(send(gb_out, 0, 1, partner))
    bu2.wait_recv()
    f_top = send(gb_out, 2, 0, flip, top)
    pair.append(send(gb_out, 2, 0, partner, top))
    bd2.wait_recv()
    f_low = send(gb_out, 2, 0, flip, low)
    pair.append(send(gb_out, 2, 0, partner, low))
    au.wait_recv()
    au2 = send(ga_out, 3, 0, up)
    pair.append(send(ga_out, 3, 0, partner))
    ad.wait_recv()
    pair.append(send(ga_out, 1, 0, partner))
    f_m.wait_recv()
    pair.append(send(gb_out, 3, 1, partner))
    fad.wait_recv()
    fad2 = send(ga_out, 1, 1, down)
    pair.append(send(ga_out, 1, 1, partner))
    fau.wait_recv()
    pair.append(send(ga_out, 3, 1, partner))
    f_p.wait_recv()
    pair.append(send(gb_out, 1, 1, partner))
    f_top.wait_recv()
    pair.append(send(gb_out, 2, 1, partner, top))
    f_low.wait_recv()
    pair.append(send(gb_out, 2, 1, partner, low))
    au2.wait_recv()
    pair.append(send(ga_out, 2, 0, partner))
    fad2.wait_recv()
    pair.append(send(ga_out, 2, 1, partner))
    for copy in pair:
        copy.wait_recv()
    for copy in own_copies:
        copy.wait()
    n_out_copy.wait()
    for copy in sent:
        copy.wait_send()


def weight_kernel(n_ref, ga_ref, gb_ref, proj_ref, up_ref, down_ref):
    part_a = ga_ref[...].reshape(2 * OWN, GA)
    part_b = gb_ref[...].reshape(2 * OWN, TB)
    up_ref[...] = nt(n_ref[:, :TA], part_a[:, :TA]) + nt(n_ref[:, TA:], part_b)
    down_ref[...] = nt(part_a[:, TA:], proj_ref[...])


def on_device(tokens, ln_gain, w_up, w_down, proj, conv_kernel, head_weight, depth_mm, lidar_mask):
    vmem = pl.BlockSpec(memory_space=pltpu.VMEM)
    anywhere = pl.BlockSpec(memory_space=pl.ANY)
    normed, grads_a, grads_b, loss = pl.pallas_call(
        step_kernel,
        name="mlp_step",
        out_shape=[
            jax.ShapeDtypeStruct((FEAT, TOK), BF16),
            jax.ShapeDtypeStruct((16, OWN, GA), BF16),
            jax.ShapeDtypeStruct((16, OWN, TB), BF16),
            jax.ShapeDtypeStruct((8, 128), F32),
        ],
        in_specs=[vmem, vmem, vmem, anywhere, vmem, anywhere, vmem, vmem, vmem],
        out_specs=[anywhere, anywhere, anywhere, vmem],
        scratch_shapes=[
            pltpu.VMEM((HID, FEAT), BF16),
            pltpu.VMEM((9, 16, CH), BF16),
            pltpu.VMEM((8, FEAT, STRIP), BF16),
            pltpu.VMEM((16, 8, STRIP), F32),
            pltpu.VMEM((8, 8, STRIP), F32),
            pltpu.VMEM((HALF, 2 * FEAT), BF16),
            pltpu.VMEM((HALF, FEAT), BF16),
            pltpu.VMEM((HALF, FEAT), BF16),
            pltpu.VMEM((FEAT, CH), BF16),
            pltpu.VMEM((2 * FEAT, TOK), BF16),
            pltpu.VMEM((8, OWN, CH), BF16),
            pltpu.VMEM((7, OWN, CH), BF16),
            pltpu.VMEM((OWN, CH), BF16),
            pltpu.VMEM((4, 2, OWN, TA), BF16),
            pltpu.VMEM((4, 2, OWN, TB), BF16),
            pltpu.VMEM((2, OWN, TA), BF16),
            pltpu.VMEM((2, 2, OWN, TA), BF16),
            pltpu.VMEM((OWN, TA), BF16),
            pltpu.VMEM((4, OWN, TB), BF16),
            pltpu.VMEM((2, OWN // 2, TB), BF16),
            pltpu.VMEM((2, OWN, TB), BF16),
            pltpu.VMEM((OWN, TOK), F32),
            pltpu.VMEM((OWN, TOK), BF16),
            pltpu.VMEM((OWN, TOK), F32),
            pltpu.VMEM((CH, TOK), F32),
            pltpu.VMEM((128, TOK), BF16),
            pltpu.VMEM((128, TOK), BF16),
            pltpu.VMEM((128, TOK), BF16),
            pltpu.VMEM((7, 16, TOK), BF16),
            pltpu.VMEM((8, 16, TOK), BF16),
            pltpu.VMEM((16, 8, STRIP), F32),
            pltpu.VMEM((8, STRIP), F32),
            pltpu.VMEM((CH, TOK), BF16),
            pltpu.VMEM((OWN, GA), BF16),
            pltpu.VMEM((OWN, TB), BF16),
            pltpu.SemaphoreType.DMA((N_SEMS,)),
            pltpu.SemaphoreType.DMA((N_SEMS,)),
            pltpu.SemaphoreType.DMA((5,)),
        ],
        compiler_params=pltpu.CompilerParams(
            collective_id=0, has_side_effects=True, vmem_limit_bytes=50 * 2**20
        ),
        cost_estimate=pl.CostEstimate(flops=4 * 10**9, bytes_accessed=16 * 2**20, transcendentals=10**6),
    )(
        tokens,
        ln_gain.reshape(1, FEAT),
        w_up,
        w_down,
        proj,
        conv_kernel.reshape(9, CH, CH),
        head_weight.reshape(1, CH),
        depth_mm,
        lidar_mask,
    )
    grad_up, grad_down = pl.pallas_call(
        weight_kernel,
        name="weight_grads",
        grid=(8,),
        out_shape=[
            jax.ShapeDtypeStruct((FEAT, HID), F32),
            jax.ShapeDtypeStruct((HID, FEAT), F32),
        ],
        in_specs=[
            pl.BlockSpec((FEAT, TOK), lambda j: (0, 0)),
            pl.BlockSpec((2, OWN, GA), lambda j: (j, 0, 0)),
            pl.BlockSpec((2, OWN, TB), lambda j: (j, 0, 0)),
            pl.BlockSpec((FEAT, CH), lambda j: (0, 0)),
        ],
        out_specs=[
            pl.BlockSpec((FEAT, 2 * OWN), lambda j: (0, j)),
            pl.BlockSpec((2 * OWN, FEAT), lambda j: (j, 0)),
        ],
        compiler_params=pltpu.CompilerParams(vmem_limit_bytes=32 * 2**20),
        cost_estimate=pl.CostEstimate(flops=3 * 10**9, bytes_accessed=18 * 2**20, transcendentals=0),
    )(normed, grads_a, grads_b, proj)
    return (grad_up, grad_down, loss[0, 0])


def solution(mesh):
    return jax.shard_map(
        on_device,
        mesh=mesh,
        in_specs=(
            P("col", "row"),
            P("row"),
            P("row", "col"),
            P("col", "row"),
            P("row", None),
            P(),
            P(),
            P("col", None),
            P("col", None),
        ),
        out_specs=(P("row", "col"), P("col", "row"), P()),
        check_vma=False,
    )
```

```python
import math

import jax
import jax.numpy as jnp
from jax import lax
from jax.experimental import pallas as pl
from jax.experimental.pallas import tpu as pltpu
from jax.sharding import PartitionSpec as P

MESH = pl.DeviceIdType.MESH
F32 = jnp.float32
BF16 = jnp.bfloat16

WIDTH = 6144
GW = 64
GH = 16
TOK = 1024
STRIP = 128
FEAT = 384
HID = 3072
HALF = 1536
OWN = 192
CH = 256
TA = 512
TB = TOK - TA
GA = TA + CH
FOCUS = 0.85
EPS = 1e-06

ROOT_HALF = math.sqrt(0.5)
DENSITY = 1.0 / math.sqrt(2.0 * math.pi)

N_SEMS = 192


def cdf(v):
    return 0.5 * (1.0 + lax.erf(v * ROOT_HALF))


def slope(v):
    return cdf(v) + v * (DENSITY * jnp.exp(-0.5 * v * v))


def tn(a, b):
    return lax.dot_general(a, b, (((0,), (0,)), ((), ())), preferred_element_type=F32)


def nt(a, b):
    return lax.dot_general(a, b, (((1,), (1,)), ((), ())), preferred_element_type=F32)


def mm(a, b):
    return jnp.dot(a, b, preferred_element_type=F32)


def step_kernel(
    tok_hbm, gain_ref, wup_hbm, wdn_hbm, proj_hbm, conv_hbm, head_ref, depth_hbm, mask_hbm,
    nt_out, gp_out, gh_out, loss_ref,
    tok_ref, wup_ref, wdn, proj_ref, conv, depth_ref, mask_ref,
    xall, st_row, st_col, w_t, w_send, wd_peer, proj_peer, n_t, m_sum, m_part, m_recv, m_own,
    p_a, p_b, a1, a2, a3, b1, b2, b3, pre, hid, zc, z1, z1_recv, z2, z2_recv, z3,
    pred_all, rows_buf, gz, ga, gb, gh_own, send_sems, recv_sems, local_sems, out_sems,
):
    row, col = lax.axis_index("row"), lax.axis_index("col")
    z, h, c = row // 4, lax.rem(row // 2, 2), lax.rem(row, 2)
    used = [0]

    def zz(dz):
        return lax.rem(z + dz + 4, 4)

    def hh(dh):
        return lax.rem(h + dh, 2)

    def at_row(dz, dh, dc):
        return {"row": zz(dz) * 4 + hh(dh) * 2 + lax.rem(c + dc, 2)}

    def at_col(dl, dx):
        return {"col": lax.rem(col // 4 + dl, 2) * 4 + lax.rem(lax.rem(col, 4) + dx, 4)}

    def remote(src, dst, device):
        at = used[0]
        used[0] += 1
        copy = pltpu.make_async_remote_copy(
            src_ref=src, dst_ref=dst, send_sem=send_sems.at[at], recv_sem=recv_sems.at[at],
            device_id=device, device_id_type=MESH,
        )
        copy.start()
        sent.append(copy)
        return copy

    def slot(dz, dh):
        return c * 8 + zz(dz) * 2 + hh(dh)

    sent = []
    row_peers = [
        (dz, dh, dc) for dz in (2, 1, 3, 0) for dh in (1, 0) for dc in (1, 0) if (dz, dh, dc) != (0, 0, 0)
    ]
    chip_peers = [(dz, dh) for dz in (2, 1, 3, 0) for dh in (1, 0) if (dz, dh) != (0, 0)]
    col_peers = [(dl, dx) for dl in (1, 0) for dx in (2, 1, 3, 0) if (dl, dx) != (0, 0)]
    partner = at_row(0, 0, 1)
    here = z * 2 + h
    other = 1 - c

    barrier = pltpu.get_barrier_semaphore()
    for peer in row_peers:
        pl.semaphore_signal(barrier, inc=1, device_id=at_row(*peer), device_id_type=MESH)
    for peer in col_peers:
        pl.semaphore_signal(barrier, inc=1, device_id=at_col(*peer), device_id_type=MESH)

    started = []

    def local(src, dst):
        copy = pltpu.make_async_copy(src, dst, local_sems.at[len(started)])
        copy.start()
        started.append(copy)
        return copy

    first_channel = pl.multiple_of(c * 128 + here * 16, 16)
    tok_copy = local(tok_hbm, tok_ref)
    proj_in = local(proj_hbm, proj_ref)
    wdn_copy = local(wdn_hbm, wdn)
    wup_copy = local(wup_hbm, wup_ref)
    depth_copy = local(depth_hbm, depth_ref)
    mask_copy = local(mask_hbm, mask_ref)
    conv_copy = local(conv_hbm.at[:, pl.ds(first_channel, 16), :], conv)

    tok_copy.wait()
    x_t = tok_ref[...].astype(F32).T
    xall[col] = x_t.astype(BF16)
    st_row[row] = jnp.concatenate(
        [
            jnp.sum(x_t, 0, keepdims=True),
            jnp.sum(x_t * x_t, 0, keepdims=True),
            jnp.zeros((6, STRIP), F32),
        ],
        axis=0,
    )
    own_half = pl.multiple_of(c * HALF, HALF)
    to_peer = pl.multiple_of(other * HALF, HALF)
    proj_in.wait()
    wdn_copy.wait()

    @pl.loop(0, 8)
    def _(k):
        m_sum[k] = mm(wdn[pl.ds(pl.multiple_of(own_half + k * OWN, 64), OWN), :], proj_ref[...])

    pl.semaphore_wait(barrier, len(row_peers) + len(col_peers))

    stat_copies = [remote(st_row.at[row], st_row.at[row], at_row(*peer)) for peer in row_peers]
    token_copies = [remote(xall.at[col], xall.at[col], at_col(*peer)) for peer in col_peers]
    wd_copy = remote(wdn.at[pl.ds(to_peer, HALF)], wd_peer, partner)
    proj_copy = remote(proj_ref, proj_peer, partner)

    feature_at = pl.multiple_of(c * FEAT, 128)
    wup_copy.wait()

    @pl.loop(0, HALF // 128)
    def _(i):
        at = pl.multiple_of(to_peer + i * 128, 128)
        w_send[pl.ds(pl.multiple_of(i * 128, 128), 128), :] = wup_ref[:, pl.ds(at, 128)].T

    w_copy = remote(w_send, w_t.at[:, pl.ds(feature_at, FEAT)], partner)

    for copy in stat_copies:
        copy.wait_recv()
    total = st_row[0]
    for index in range(1, 16):
        total = total + st_row[index]
    mean = total[0:1] / WIDTH
    spread = total[1:2] / WIDTH - mean * mean
    depth_copy.wait()
    mask_copy.wait()
    depth = depth_ref[...].astype(F32)
    seen = mask_ref[...].astype(F32)
    st_col[col] = jnp.concatenate(
        [
            mean,
            lax.rsqrt(spread + EPS),
            jnp.concatenate([seen[0:1], seen[1:2]], axis=1),
            jnp.log(jnp.concatenate([depth[0:1], depth[1:2]], axis=1) * 0.001),
            jnp.zeros((4, STRIP), F32),
        ],
        axis=0,
    )
    norm_copies = [remote(st_col.at[col], st_col.at[col], at_col(*peer)) for peer in col_peers]

    wd_copy.wait_recv()
    proj_copy.wait_recv()

    @pl.loop(0, 8)
    def _(k):
        more = mm(wd_peer[pl.ds(pl.multiple_of(k * OWN, 64), OWN), :], proj_peer[...])
        m_part[k] = (m_sum[k] + more).astype(BF16)

    m_copies = []
    for index, (dz, dh) in enumerate(chip_peers):
        m_copies.append(
            remote(m_part.at[zz(dz) * 2 + hh(dh)], m_recv.at[index], at_row(dz, dh, 0))
        )

    @pl.loop(0, HALF // 128)
    def _(i):
        at = pl.multiple_of(own_half + i * 128, 128)
        w_t[pl.ds(pl.multiple_of(i * 128, 128), 128), pl.ds(feature_at, FEAT)] = wup_ref[:, pl.ds(at, 128)].T

    gain = jnp.broadcast_to(gain_ref[...].reshape(1, FEAT), (STRIP, FEAT)).T
    for copy in norm_copies:
        copy.wait_recv()
    for copy in token_copies:
        copy.wait_recv()

    n_copies = []
    for first in (0, 4):
        for index in range(first, first + 4):
            stats = st_col[index]
            n_t[pl.ds(feature_at, FEAT), index * STRIP : (index + 1) * STRIP] = (
                (xall[index].astype(F32) - stats[0:1]) * stats[1:2] * gain
            ).astype(BF16)
        half = n_t.at[pl.ds(feature_at, FEAT), first * STRIP : (first + 4) * STRIP]
        n_copies.append(remote(half, half, partner))
    local(n_t.at[pl.ds(feature_at, FEAT)], nt_out)
    w_copy.wait_recv()

    a_copies, b_copies = {}, {}

    def project(dz, into, first):
        base = pl.multiple_of(zz(dz) * 2 * OWN, 2 * OWN)

        @pl.loop(0, into.shape[3] // 256)
        def _(t):
            at = pl.multiple_of(t * 256, 256)
            both = mm(
                w_t[pl.ds(base, 2 * OWN), :], n_t[:, pl.ds(pl.multiple_of(first + at, 256), 256)]
            ).astype(BF16)
            into[zz(dz), 0, :, pl.ds(at, 256)] = both[:OWN]
            into[zz(dz), 1, :, pl.ds(at, 256)] = both[OWN:]

    up, down, flip = at_row(1, 0, 0), at_row(3, 0, 0), at_row(0, 1, 0)
    n_copies[0].wait_recv()
    project(2, p_a, 0)
    a_up = remote(p_a.at[zz(2), 0], a1.at[0], up)
    a_down = remote(p_a.at[zz(2), 1], a1.at[1], down)
    n_copies[1].wait_recv()
    for dz in (2, 1, 3, 0):
        project(dz, p_b, TA)
        b_copies[dz] = remote(p_b.at[zz(dz), 1 - h], b1.at[zz(dz)], flip)
    for dz in (1, 3, 0):
        project(dz, p_a, 0)

    def add(into, more):
        into[...] = (into[...].astype(F32) + more[...].astype(F32)).astype(BF16)

    a_up.wait_recv()
    add(p_a.at[zz(1), 0], a1.at[0])
    a_up2 = remote(p_a.at[zz(1)], a2.at[0], up)
    a_down.wait_recv()
    add(p_a.at[zz(3), 1], a1.at[1])
    a_down2 = remote(p_a.at[zz(3)], a2.at[1], down)

    b_copies[2].wait_recv()
    add(p_b.at[zz(2), h], b1.at[zz(2)])
    b_up = remote(p_b.at[zz(2), h, 0:96], b2.at[0], up)
    b_down = remote(p_b.at[zz(2), h, 96:192], b2.at[1], down)
    b_copies[1].wait_recv()
    add(p_b.at[zz(1), h], b1.at[zz(1)])
    b_copies[3].wait_recv()
    add(p_b.at[zz(3), h], b1.at[zz(3)])

    a_up2.wait_recv()
    a_down2.wait_recv()
    p_a[z, 1 - h] = (
        p_a[z, 1 - h].astype(F32) + a2[0, 1 - h].astype(F32) + a2[1, 1 - h].astype(F32)
    ).astype(BF16)
    a_flip = remote(p_a.at[z, 1 - h], a3, flip)

    b_up.wait_recv()
    add(p_b.at[zz(1), h, 0:96], b2.at[0])
    b_up2 = remote(p_b.at[zz(1), h], b3.at[0], up)
    b_down.wait_recv()
    add(p_b.at[zz(3), h, 96:192], b2.at[1])
    b_down2 = remote(p_b.at[zz(3), h], b3.at[1], down)

    for copy in m_copies:
        copy.wait_recv()
    total = m_part[here].astype(F32)
    for index in range(7):
        total = total + m_recv[index].astype(F32)
    m_own[...] = total.astype(BF16)
    ga[slot(0, 0), :, TA:] = m_own[...]
    x_proj = tn(proj_ref[...], xall[col])

    conv_copy.wait()
    head = head_ref[...]
    taps = [jnp.sum(conv[k].astype(F32) * head, axis=1, keepdims=True) for k in range(9)]
    lane = lax.broadcasted_iota(jnp.int32, (16, CH), 1)
    sub = lax.broadcasted_iota(jnp.int32, (16, CH), 0)
    head_col = jnp.sum(jnp.where(lane == sub + first_channel, head, 0.0), axis=1, keepdims=True)

    b_copies[0].wait_recv()
    a_flip.wait_recv()
    pre[:, :TA] = (
        p_a[z, h].astype(F32) + a2[0, h].astype(F32) + a2[1, h].astype(F32) + a3[...].astype(F32)
    )
    b_up2.wait_recv()
    b_down2.wait_recv()
    pre[:, TA:] = (
        p_b[z, h].astype(F32) + b1[z].astype(F32) + b3[0].astype(F32) + b3[1].astype(F32)
    )

    @pl.loop(0, TOK // 128)
    def _(t):
        at = pl.ds(pl.multiple_of(t * 128, 128), 128)
        value = pre[:, at]
        hid[:, at] = (value * cdf(value)).astype(BF16)

    @pl.loop(0, TOK // 256)
    def _(t):
        at = pl.ds(pl.multiple_of(t * 256, 256), 256)
        zc[:, at] = tn(m_own[...], hid[:, at])

    strip = pl.ds(pl.multiple_of(col * STRIP, STRIP), STRIP)
    zc[:, strip] = zc[:, strip] + x_proj

    z1[...] = zc[pl.ds(pl.multiple_of(other * 128, 128), 128), :].astype(BF16)
    z1_copy = remote(z1, z1_recv, partner)

    bulk_from = len(sent)
    mine_a, mine_b = ga.at[slot(0, 0)], gb.at[slot(0, 0)]
    pair = []

    def send(buf, dz, dh, device, rows=None):
        ref = buf.at[slot(dz, dh)] if rows is None else buf.at[slot(dz, dh), rows[0] : rows[1]]
        return remote(ref, ref, device)

    top, low = (0, 96), (96, 192)

    @pl.loop(0, TB // 128)
    def _(t):
        at = pl.ds(pl.multiple_of(t * 128, 128), 128)
        mine_b[:, at] = slope(pre[:, pl.ds(pl.multiple_of(TA + t * 128, 128), 128)]).astype(BF16)

    bu = send(gb, 0, 0, up)
    bd = send(gb, 0, 0, down)
    pair.append(send(gb, 0, 0, partner))

    @pl.loop(0, TA // 128)
    def _(t):
        at = pl.ds(pl.multiple_of(t * 128, 128), 128)
        mine_a[:, at] = slope(pre[:, at]).astype(BF16)

    fa = send(ga, 0, 0, flip)
    pair.append(send(ga, 0, 0, partner))

    z1_copy.wait_recv()
    z2[...] = (
        zc[pl.ds(pl.multiple_of(c * 128, 128), 128), :] + z1_recv[...].astype(F32)
    ).astype(BF16)
    z2_copies = []
    for index, (dz, dh) in enumerate(chip_peers):
        at = pl.multiple_of((zz(dz) * 2 + hh(dh)) * 16, 16)
        z2_copies.append(remote(z2.at[pl.ds(at, 16)], z2_recv.at[index], at_row(dz, dh, 0)))
    fb = send(gb, 0, 0, flip)
    au = send(ga, 0, 0, up)
    ad = send(ga, 0, 0, down)
    bu.wait_recv()
    bu2 = send(gb, 3, 0, up, top)
    f_m = send(gb, 3, 0, flip)
    pair.append(send(gb, 3, 0, partner))
    bd.wait_recv()
    bd2 = send(gb, 1, 0, down, low)
    f_p = send(gb, 1, 0, flip)
    pair.append(send(gb, 1, 0, partner))
    part = z2[pl.ds(pl.multiple_of(here * 16, 16), 16), :].astype(F32)
    for index, copy in enumerate(z2_copies):
        copy.wait_recv()
        part = part + z2_recv[index].astype(F32)
    z3[col] = part.astype(BF16)
    z3_copies = [remote(z3.at[col], z3.at[col], at_col(*peer)) for peer in col_peers]
    fa.wait_recv()
    fau = send(ga, 0, 1, up)
    fad = send(ga, 0, 1, down)
    pair.append(send(ga, 0, 1, partner))
    for copy in z3_copies:
        copy.wait_recv()
    field = z3[0].astype(F32)
    for index in range(1, 8):
        field = field + z3[index].astype(F32)

    token = lax.broadcasted_iota(jnp.int32, (1, TOK), 1)
    line, place = token >> 6, token & (GW - 1)

    def moved(values, di, dj):
        shift = di * GW + dj
        if shift:
            values = pltpu.roll(values, (-shift) % TOK, 1)
        inside = (
            (line + di >= 0) & (line + di < GH) & (place + dj >= 0) & (place + dj < GW)
        )
        return jnp.where(inside, values, 0.0)

    act = (field * cdf(field)).astype(BF16).astype(F32)
    pred = jnp.sum(field * head_col, axis=0, keepdims=True)
    for k in range(9):
        pred = pred + moved(jnp.sum(act * taps[k], axis=0, keepdims=True), k // 3 - 1, k % 3 - 1)
    for index in range(8):
        rows_buf[index : index + 1, :] = pred[:, index * STRIP : (index + 1) * STRIP]
    pred_all[row] = rows_buf[...]
    pred_copies = [remote(pred_all.at[row], pred_all.at[row], at_row(*peer)) for peer in row_peers]
    fb.wait_recv()
    pair.append(send(gb, 0, 1, partner))
    bu2.wait_recv()
    f_top = send(gb, 2, 0, flip, top)
    pair.append(send(gb, 2, 0, partner, top))
    bd2.wait_recv()
    f_low = send(gb, 2, 0, flip, low)
    pair.append(send(gb, 2, 0, partner, low))
    au.wait_recv()
    au2 = send(ga, 3, 0, up)
    pair.append(send(ga, 3, 0, partner))
    ad.wait_recv()
    pair.append(send(ga, 1, 0, partner))
    field_slope = slope(field)
    valid = jnp.concatenate([st_col[index][2:3] for index in range(8)], axis=0)
    target = jnp.concatenate([st_col[index][3:4] for index in range(8)], axis=0)
    for copy in pred_copies:
        copy.wait_recv()
    pred = pred_all[0]
    for index in range(1, 16):
        pred = pred + pred_all[index]

    err = valid * (pred - target)

    def whole(values):
        return jnp.sum(jnp.sum(values, axis=1, keepdims=True), axis=0, keepdims=True)

    count = whole(valid)
    mean_err = whole(err) / count
    loss_ref[0, 0] = jnp.sum(whole(err * err) / count - FOCUS * mean_err * mean_err)
    grad_pred = valid * (2.0 * err - 2.0 * FOCUS * mean_err)
    grad_pred = jnp.concatenate([grad_pred[index : index + 1] for index in range(8)], axis=1)
    back = jnp.zeros((16, TOK), F32)
    for k in range(9):
        back = back + taps[k] * moved(grad_pred, 1 - k // 3, 1 - k % 3)
    mine = pl.ds(first_channel, 16)
    gz[mine, :] = (grad_pred * head_col + field_slope * back).astype(BF16)

    gz_copies = [
        remote(gz.at[mine], gz.at[mine], at_row(dz, dh, 0)) for dz, dh in chip_peers
    ]
    gz_pair = [remote(gz.at[mine], gz.at[mine], partner)]
    f_m.wait_recv()
    pair.append(send(gb, 3, 1, partner))
    fad.wait_recv()
    fad2 = send(ga, 1, 1, down)
    pair.append(send(ga, 1, 1, partner))
    fau.wait_recv()
    pair.append(send(ga, 3, 1, partner))
    f_p.wait_recv()
    pair.append(send(gb, 1, 1, partner))
    for (dz, dh), copy in zip(chip_peers, gz_copies):
        copy.wait_recv()
        came = gz.at[pl.ds(pl.multiple_of(c * 128 + (zz(-dz) * 2 + hh(dh)) * 16, 16), 16)]
        gz_pair.append(remote(came, came, partner))
    for copy in gz_pair:
        copy.wait_recv()

    gh_own[...] = nt(hid[...], gz[...]).astype(BF16)
    local(gh_own, gh_out.at[slot(0, 0)])
    bulk_to = len(sent)
    gh_copies = [
        remote(gh_own, gh_out.at[slot(0, 0)], at_row(dz, dh, 0)) for dz, dh in chip_peers
    ]
    gh_pair = [remote(gh_own, gh_out.at[slot(0, 0)], partner)]
    bulk_end = len(sent)
    f_top.wait_recv()
    pair.append(send(gb, 2, 1, partner, top))
    f_low.wait_recv()
    pair.append(send(gb, 2, 1, partner, low))
    au2.wait_recv()
    pair.append(send(ga, 2, 0, partner))
    fad2.wait_recv()
    pair.append(send(ga, 2, 1, partner))
    for copy in pair:
        copy.wait_recv()
    bulk = sent[bulk_from:bulk_to] + sent[bulk_end:]
    for copy in bulk:
        copy.wait_send()

    @pl.loop(0, 16)
    def _(k):
        weights = ga[k, :, TA:]
        ga[k, :, :TA] = (mm(weights, gz[:, :TA]) * ga[k, :, :TA].astype(F32)).astype(BF16)
        gb[k] = (mm(weights, gz[:, TA:]) * gb[k].astype(F32)).astype(BF16)
        pltpu.make_async_copy(ga.at[k, :, :TA], gp_out.at[k, :, :TA], out_sems.at[0, k]).start()
        pltpu.make_async_copy(gb.at[k], gp_out.at[k, :, TA:], out_sems.at[1, k]).start()

    for (dz, dh), copy in zip(chip_peers, gh_copies):
        copy.wait_recv()
        came = gh_out.at[slot(-dz, dh)]
        gh_pair.append(remote(came, came, partner))
    for copy in gh_pair:
        copy.wait_recv()

    @pl.loop(0, 16)
    def _(k):
        pltpu.make_async_copy(ga.at[k, :, :TA], gp_out.at[k, :, :TA], out_sems.at[0, k]).wait()
        pltpu.make_async_copy(gb.at[k], gp_out.at[k, :, TA:], out_sems.at[1, k]).wait()

    for copy in started[-2:]:
        copy.wait()
    for copy in sent:
        if not any(copy is other_copy for other_copy in bulk):
            copy.wait_send()


def weight_kernel(n_ref, gp_ref, gh_ref, proj_ref, up_ref, down_ref):
    up_ref[...] = nt(n_ref[...], gp_ref[...].reshape(2 * OWN, TOK))
    down_ref[...] = nt(gh_ref[...].reshape(2 * OWN, CH), proj_ref[...])


def on_device(tokens, ln_gain, w_up, w_down, proj, conv_kernel, head_weight, depth_mm, lidar_mask):
    vmem = pl.BlockSpec(memory_space=pltpu.VMEM)
    anywhere = pl.BlockSpec(memory_space=pl.ANY)
    normed, grad_pre, grad_hidden, loss = pl.pallas_call(
        step_kernel,
        name="mlp_step",
        out_shape=[
            jax.ShapeDtypeStruct((FEAT, TOK), BF16),
            jax.ShapeDtypeStruct((16, OWN, TOK), BF16),
            jax.ShapeDtypeStruct((16, OWN, CH), BF16),
            jax.ShapeDtypeStruct((1, 1), F32),
        ],
        in_specs=[
            anywhere, vmem, anywhere, anywhere, anywhere, anywhere, vmem, anywhere, anywhere,
        ],
        out_specs=[anywhere, anywhere, anywhere, pl.BlockSpec(memory_space=pltpu.SMEM)],
        scratch_shapes=[
            pltpu.VMEM((STRIP, FEAT), BF16),
            pltpu.VMEM((FEAT, HID), BF16),
            pltpu.VMEM((HID, FEAT), BF16),
            pltpu.VMEM((FEAT, CH), BF16),
            pltpu.VMEM((9, 16, CH), BF16),
            pltpu.VMEM((2, GW), jnp.int32),
            pltpu.VMEM((2, GW), jnp.int32),
            pltpu.VMEM((8, FEAT, STRIP), BF16),
            pltpu.VMEM((16, 8, STRIP), F32),
            pltpu.VMEM((8, 8, STRIP), F32),
            pltpu.VMEM((HALF, 2 * FEAT), BF16),
            pltpu.VMEM((HALF, FEAT), BF16),
            pltpu.VMEM((HALF, FEAT), BF16),
            pltpu.VMEM((FEAT, CH), BF16),
            pltpu.VMEM((2 * FEAT, TOK), BF16),
            pltpu.VMEM((8, OWN, CH), F32),
            pltpu.VMEM((8, OWN, CH), BF16),
            pltpu.VMEM((7, OWN, CH), BF16),
            pltpu.VMEM((OWN, CH), BF16),
            pltpu.VMEM((4, 2, OWN, TA), BF16),
            pltpu.VMEM((4, 2, OWN, TB), BF16),
            pltpu.VMEM((2, OWN, TA), BF16),
            pltpu.VMEM((2, 2, OWN, TA), BF16),
            pltpu.VMEM((OWN, TA), BF16),
            pltpu.VMEM((4, OWN, TB), BF16),
            pltpu.VMEM((2, OWN // 2, TB), BF16),
            pltpu.VMEM((2, OWN, TB), BF16),
            pltpu.VMEM((OWN, TOK), F32),
            pltpu.VMEM((OWN, TOK), BF16),
            pltpu.VMEM((CH, TOK), F32),
            pltpu.VMEM((128, TOK), BF16),
            pltpu.VMEM((128, TOK), BF16),
            pltpu.VMEM((128, TOK), BF16),
            pltpu.VMEM((7, 16, TOK), BF16),
            pltpu.VMEM((8, 16, TOK), BF16),
            pltpu.VMEM((16, 8, STRIP), F32),
            pltpu.VMEM((8, STRIP), F32),
            pltpu.VMEM((CH, TOK), BF16),
            pltpu.VMEM((16, OWN, GA), BF16),
            pltpu.VMEM((16, OWN, TB), BF16),
            pltpu.VMEM((OWN, CH), BF16),
            pltpu.SemaphoreType.DMA((N_SEMS,)),
            pltpu.SemaphoreType.DMA((N_SEMS,)),
            pltpu.SemaphoreType.DMA((9,)),
            pltpu.SemaphoreType.DMA((2, 16)),
        ],
        compiler_params=pltpu.CompilerParams(
            collective_id=0, has_side_effects=True, vmem_limit_bytes=60 * 2**20
        ),
        cost_estimate=pl.CostEstimate(flops=6 * 10**9, bytes_accessed=16 * 2**20, transcendentals=10**6),
    )(
        tokens, ln_gain, w_up, w_down, proj, conv_kernel.reshape(9, CH, CH),
        head_weight.reshape(1, CH), depth_mm, lidar_mask,
    )
    grad_up, grad_down = pl.pallas_call(
        weight_kernel,
        name="weight_grads",
        grid=(8,),
        out_shape=[
            jax.ShapeDtypeStruct((FEAT, HID), F32),
            jax.ShapeDtypeStruct((HID, FEAT), F32),
        ],
        in_specs=[
            pl.BlockSpec((FEAT, TOK), lambda j: (0, 0)),
            pl.BlockSpec((2, OWN, TOK), lambda j: (j, 0, 0)),
            pl.BlockSpec((2, OWN, CH), lambda j: (j, 0, 0)),
            pl.BlockSpec((FEAT, CH), lambda j: (0, 0)),
        ],
        out_specs=[
            pl.BlockSpec((FEAT, 2 * OWN), lambda j: (0, j)),
            pl.BlockSpec((2 * OWN, FEAT), lambda j: (j, 0)),
        ],
        compiler_params=pltpu.CompilerParams(vmem_limit_bytes=60 * 2**20),
        cost_estimate=pl.CostEstimate(flops=3 * 10**9, bytes_accessed=18 * 2**20, transcendentals=0),
    )(normed, grad_pre, grad_hidden, proj)
    return (grad_up, grad_down, loss.reshape(()))


def solution(mesh):
    return jax.shard_map(
        on_device,
        mesh=mesh,
        in_specs=(
            P("col", "row"),
            P("row"),
            P("row", "col"),
            P("col", "row"),
            P("row", None),
            P(),
            P(),
            P("col", None),
            P("col", None),
        ),
        out_specs=(P("row", "col"), P("col", "row"), P()),
        check_vma=False,
    )
```

```python
import math

import jax
import jax.numpy as jnp
from jax import lax
from jax.experimental import pallas as pl
from jax.experimental.pallas import tpu as pltpu
from jax.sharding import PartitionSpec as P

MESH = pl.DeviceIdType.MESH
F32 = jnp.float32
BF16 = jnp.bfloat16

WIDTH = 6144
GW = 64
GH = 16
TOK = 1024
STRIP = 128
FEAT = 384
HID = 3072
HALF = 1536
OWN = 192
CH = 256
TA = 512
TB = TOK - TA
GA = TA + CH
FOCUS = 0.85
EPS = 1e-06

ROOT_HALF = math.sqrt(0.5)
DENSITY = 1.0 / math.sqrt(2.0 * math.pi)

N_SEMS = 192


def cdf(v):
    return 0.5 * (1.0 + lax.erf(v * ROOT_HALF))


def slope(v):
    return cdf(v) + v * (DENSITY * jnp.exp(-0.5 * v * v))


def tn(a, b):
    return lax.dot_general(a, b, (((0,), (0,)), ((), ())), preferred_element_type=F32)


def nt(a, b):
    return lax.dot_general(a, b, (((1,), (1,)), ((), ())), preferred_element_type=F32)


def mm(a, b):
    return jnp.dot(a, b, preferred_element_type=F32)


def step_kernel(
    tok_hbm, gain_ref, wup_hbm, wdn_hbm, proj_hbm, conv_hbm, head_ref, depth_hbm, mask_hbm,
    nt_out, gp_out, gh_out, loss_ref,
    tok_ref, wup_ref, wdn, proj_ref, conv, depth_ref, mask_ref,
    xall, st_row, st_col, w_t, w_send, wd_peer, proj_peer, n_t, m_sum, m_part, m_recv, m_own,
    p_a, p_b, a1, a2, a3, b1, b2, b3, pre, hid, zc, z1, z1_recv, z2, z2_recv, z3,
    taps, field, field_slope, shifted, pred_all, rows_buf, gz, ga, gb, gh_own, send_sems, recv_sems, local_sems, out_sems,
):
    row, col = lax.axis_index("row"), lax.axis_index("col")
    z, h, c = row // 4, lax.rem(row // 2, 2), lax.rem(row, 2)
    used = [0]

    def zz(dz):
        return lax.rem(z + dz + 4, 4)

    def hh(dh):
        return lax.rem(h + dh, 2)

    def at_row(dz, dh, dc):
        return {"row": zz(dz) * 4 + hh(dh) * 2 + lax.rem(c + dc, 2)}

    def at_col(dl, dx):
        return {"col": lax.rem(col // 4 + dl, 2) * 4 + lax.rem(lax.rem(col, 4) + dx, 4)}

    def remote(src, dst, device):
        at = used[0]
        used[0] += 1
        copy = pltpu.make_async_remote_copy(
            src_ref=src, dst_ref=dst, send_sem=send_sems.at[at], recv_sem=recv_sems.at[at],
            device_id=device, device_id_type=MESH,
        )
        copy.start()
        sent.append(copy)
        return copy

    def slot(dz, dh):
        return c * 8 + zz(dz) * 2 + hh(dh)

    def own_rows(dz, dh):
        return pl.ds(pl.multiple_of(slot(dz, dh) * OWN, 64), OWN)

    sent = []
    row_peers = [
        (dz, dh, dc) for dz in (2, 1, 3, 0) for dh in (1, 0) for dc in (1, 0) if (dz, dh, dc) != (0, 0, 0)
    ]
    chip_peers = [(dz, dh) for dz in (2, 1, 3, 0) for dh in (1, 0) if (dz, dh) != (0, 0)]
    col_peers = [(dl, dx) for dl in (1, 0) for dx in (2, 1, 3, 0) if (dl, dx) != (0, 0)]
    partner = at_row(0, 0, 1)
    here = z * 2 + h
    other = 1 - c

    barrier = pltpu.get_barrier_semaphore()
    for peer in row_peers:
        pl.semaphore_signal(barrier, inc=1, device_id=at_row(*peer), device_id_type=MESH)
    for peer in col_peers:
        pl.semaphore_signal(barrier, inc=1, device_id=at_col(*peer), device_id_type=MESH)

    started = []

    def local(src, dst):
        copy = pltpu.make_async_copy(src, dst, local_sems.at[len(started)])
        copy.start()
        started.append(copy)
        return copy

    first_channel = pl.multiple_of(c * 128, 128)
    tok_copy = local(tok_hbm, tok_ref)
    proj_in = local(proj_hbm, proj_ref)
    wdn_copy = local(wdn_hbm, wdn)
    wup_copy = local(wup_hbm, wup_ref)
    depth_copy = local(depth_hbm, depth_ref)
    mask_copy = local(mask_hbm, mask_ref)
    conv_copy = local(conv_hbm.at[:, pl.ds(first_channel, 128), :], conv)

    tok_copy.wait()
    x_t = tok_ref[...].astype(F32).T
    xall[col] = x_t.astype(BF16)
    st_row[row] = jnp.concatenate(
        [
            jnp.sum(x_t, 0, keepdims=True),
            jnp.sum(x_t * x_t, 0, keepdims=True),
            jnp.zeros((6, STRIP), F32),
        ],
        axis=0,
    )
    own_half = pl.multiple_of(c * HALF, HALF)
    to_peer = pl.multiple_of(other * HALF, HALF)
    proj_in.wait()
    wdn_copy.wait()

    @pl.loop(0, 8)
    def _(k):
        m_sum[k] = mm(wdn[pl.ds(pl.multiple_of(own_half + k * OWN, 64), OWN), :], proj_ref[...])

    pl.semaphore_wait(barrier, len(row_peers) + len(col_peers))

    stat_copies = [remote(st_row.at[row], st_row.at[row], at_row(*peer)) for peer in row_peers]
    across = remote(xall.at[col], xall.at[col], at_col(1, 0))
    token_copies = [remote(xall.at[col], xall.at[col], at_col(0, dx)) for dx in (2, 1, 3)]
    wd_copy = remote(wdn.at[pl.ds(to_peer, HALF)], wd_peer, partner)
    proj_copy = remote(proj_ref, proj_peer, partner)

    feature_at = pl.multiple_of(c * FEAT, 128)
    wup_copy.wait()

    @pl.loop(0, HALF // 128)
    def _(i):
        at = pl.multiple_of(to_peer + i * 128, 128)
        w_send[pl.ds(pl.multiple_of(i * 128, 128), 128), :] = wup_ref[:, pl.ds(at, 128)].T

    across.wait_recv()
    came = xall.at[lax.rem(col + 4, 8)]
    token_copies += [remote(came, came, at_col(0, dx)) for dx in (2, 1, 3)]
    w_copy = remote(w_send, w_t.at[:, pl.ds(feature_at, FEAT)], partner)

    for copy in stat_copies:
        copy.wait_recv()
    total = st_row[0]
    for index in range(1, 16):
        total = total + st_row[index]
    mean = total[0:1] / WIDTH
    spread = total[1:2] / WIDTH - mean * mean
    depth_copy.wait()
    mask_copy.wait()
    depth = depth_ref[...].astype(F32)
    seen = mask_ref[...].astype(F32)
    st_col[col] = jnp.concatenate(
        [
            mean,
            lax.rsqrt(spread + EPS),
            jnp.concatenate([seen[0:1], seen[1:2]], axis=1),
            jnp.log(jnp.concatenate([depth[0:1], depth[1:2]], axis=1) * 0.001),
            jnp.zeros((4, STRIP), F32),
        ],
        axis=0,
    )
    norm_copies = [remote(st_col.at[col], st_col.at[col], at_col(*peer)) for peer in col_peers]

    wd_copy.wait_recv()
    proj_copy.wait_recv()

    @pl.loop(0, 8)
    def _(k):
        more = mm(wd_peer[pl.ds(pl.multiple_of(k * OWN, 64), OWN), :], proj_peer[...])
        m_part[k] = (m_sum[k] + more).astype(BF16)

    m_copies = []
    for index, (dz, dh) in enumerate(chip_peers):
        m_copies.append(
            remote(m_part.at[zz(dz) * 2 + hh(dh)], m_recv.at[index], at_row(dz, dh, 0))
        )

    @pl.loop(0, HALF // 128)
    def _(i):
        at = pl.multiple_of(own_half + i * 128, 128)
        w_t[pl.ds(pl.multiple_of(i * 128, 128), 128), pl.ds(feature_at, FEAT)] = wup_ref[:, pl.ds(at, 128)].T

    gain = jnp.broadcast_to(gain_ref[...].reshape(1, FEAT), (STRIP, FEAT)).T
    for copy in norm_copies:
        copy.wait_recv()
    for copy in token_copies:
        copy.wait_recv()

    n_copies = []
    for first in (0, 4):
        for index in range(first, first + 4):
            stats = st_col[index]
            n_t[pl.ds(feature_at, FEAT), index * STRIP : (index + 1) * STRIP] = (
                (xall[index].astype(F32) - stats[0:1]) * stats[1:2] * gain
            ).astype(BF16)
        half = n_t.at[pl.ds(feature_at, FEAT), first * STRIP : (first + 4) * STRIP]
        n_copies.append(remote(half, half, partner))
    local(n_t.at[pl.ds(feature_at, FEAT)], nt_out)
    w_copy.wait_recv()

    a_copies, b_copies = {}, {}

    def project(dz, into, first):
        base = pl.multiple_of(zz(dz) * 2 * OWN, 2 * OWN)

        @pl.loop(0, into.shape[3] // 256)
        def _(t):
            at = pl.multiple_of(t * 256, 256)
            both = mm(
                w_t[pl.ds(base, 2 * OWN), :], n_t[:, pl.ds(pl.multiple_of(first + at, 256), 256)]
            ).astype(BF16)
            into[zz(dz), 0, :, pl.ds(at, 256)] = both[:OWN]
            into[zz(dz), 1, :, pl.ds(at, 256)] = both[OWN:]

    up, down, flip = at_row(1, 0, 0), at_row(3, 0, 0), at_row(0, 1, 0)
    n_copies[0].wait_recv()
    project(2, p_a, 0)
    a_up = remote(p_a.at[zz(2), 0], a1.at[0], up)
    a_down = remote(p_a.at[zz(2), 1], a1.at[1], down)
    n_copies[1].wait_recv()
    for dz in (2, 1, 3, 0):
        project(dz, p_b, TA)
        b_copies[dz] = remote(p_b.at[zz(dz), 1 - h], b1.at[zz(dz)], flip)
    for dz in (1, 3, 0):
        project(dz, p_a, 0)

    def add(into, more):
        into[...] = (into[...].astype(F32) + more[...].astype(F32)).astype(BF16)

    a_up.wait_recv()
    add(p_a.at[zz(1), 0], a1.at[0])
    a_up2 = remote(p_a.at[zz(1)], a2.at[0], up)
    a_down.wait_recv()
    add(p_a.at[zz(3), 1], a1.at[1])
    a_down2 = remote(p_a.at[zz(3)], a2.at[1], down)

    b_copies[2].wait_recv()
    add(p_b.at[zz(2), h], b1.at[zz(2)])
    b_up = remote(p_b.at[zz(2), h, 0:96], b2.at[0], up)
    b_down = remote(p_b.at[zz(2), h, 96:192], b2.at[1], down)
    b_copies[1].wait_recv()
    add(p_b.at[zz(1), h], b1.at[zz(1)])
    b_copies[3].wait_recv()
    add(p_b.at[zz(3), h], b1.at[zz(3)])

    a_up2.wait_recv()
    a_down2.wait_recv()
    p_a[z, 1 - h] = (
        p_a[z, 1 - h].astype(F32) + a2[0, 1 - h].astype(F32) + a2[1, 1 - h].astype(F32)
    ).astype(BF16)
    a_flip = remote(p_a.at[z, 1 - h], a3, flip)

    b_up.wait_recv()
    add(p_b.at[zz(1), h, 0:96], b2.at[0])
    b_up2 = remote(p_b.at[zz(1), h], b3.at[0], up)
    b_down.wait_recv()
    add(p_b.at[zz(3), h, 96:192], b2.at[1])
    b_down2 = remote(p_b.at[zz(3), h], b3.at[1], down)

    for copy in m_copies:
        copy.wait_recv()
    total = m_part[here].astype(F32)
    for index in range(7):
        total = total + m_recv[index].astype(F32)
    m_own[...] = total.astype(BF16)
    ga[slot(0, 0), :, TA:] = m_own[...]
    x_proj = tn(proj_ref[...], xall[col])

    conv_copy.wait()
    head = head_ref[...]
    for k in range(9):
        taps[k] = jnp.broadcast_to(
            jnp.sum(conv[k].astype(F32) * head, axis=1, keepdims=True), (128, 128)
        )
    lane = lax.broadcasted_iota(jnp.int32, (128, CH), 1)
    sub = lax.broadcasted_iota(jnp.int32, (128, CH), 0)
    taps[9] = jnp.broadcast_to(
        jnp.sum(jnp.where(lane == sub + first_channel, head, 0.0), axis=1, keepdims=True), (128, 128)
    )

    b_copies[0].wait_recv()
    a_flip.wait_recv()
    pre[:, :TA] = (
        p_a[z, h].astype(F32) + a2[0, h].astype(F32) + a2[1, h].astype(F32) + a3[...].astype(F32)
    )
    b_up2.wait_recv()
    b_down2.wait_recv()
    pre[:, TA:] = (
        p_b[z, h].astype(F32) + b1[z].astype(F32) + b3[0].astype(F32) + b3[1].astype(F32)
    )

    @pl.loop(0, TOK // 128)
    def _(t):
        at = pl.ds(pl.multiple_of(t * 128, 128), 128)
        value = pre[:, at]
        hid[:, at] = (value * cdf(value)).astype(BF16)

    @pl.loop(0, TOK // 256)
    def _(t):
        at = pl.ds(pl.multiple_of(t * 256, 256), 256)
        zc[:, at] = tn(m_own[...], hid[:, at])

    strip = pl.ds(pl.multiple_of(col * STRIP, STRIP), STRIP)
    zc[:, strip] = zc[:, strip] + x_proj

    z1[...] = zc[pl.ds(pl.multiple_of(other * 128, 128), 128), :].astype(BF16)
    z1_copy = remote(z1, z1_recv, partner)

    bulk_from = len(sent)
    mine_a, mine_b = ga.at[slot(0, 0)], gb.at[slot(0, 0)]
    pair = []

    def send(buf, dz, dh, device, rows=None):
        ref = buf.at[slot(dz, dh)] if rows is None else buf.at[slot(dz, dh), rows[0] : rows[1]]
        return remote(ref, ref, device)

    top, low = (0, 96), (96, 192)

    @pl.loop(0, TB // 128)
    def _(t):
        at = pl.ds(pl.multiple_of(t * 128, 128), 128)
        mine_b[:, at] = slope(pre[:, pl.ds(pl.multiple_of(TA + t * 128, 128), 128)]).astype(BF16)

    @pl.loop(0, TA // 128)
    def _(t):
        at = pl.ds(pl.multiple_of(t * 128, 128), 128)
        mine_a[:, at] = slope(pre[:, at]).astype(BF16)

    z1_copy.wait_recv()
    z2[...] = (
        zc[pl.ds(pl.multiple_of(c * 128, 128), 128), :] + z1_recv[...].astype(F32)
    ).astype(BF16)
    z2_copies = []
    for index, (dz, dh) in enumerate(chip_peers):
        at = pl.multiple_of((zz(dz) * 2 + hh(dh)) * 16, 16)
        z2_copies.append(remote(z2.at[pl.ds(at, 16)], z2_recv.at[index], at_row(dz, dh, 0)))
    bu = send(gb, 0, 0, up)
    bd = send(gb, 0, 0, down)
    fa = send(ga, 0, 0, flip)
    pair.append(send(gb, 0, 0, partner))
    pair.append(send(ga, 0, 0, partner))
    mine = pl.ds(pl.multiple_of(here * 16, 16), 16)
    part = z2[mine, :].astype(F32)
    for index, copy in enumerate(z2_copies):
        copy.wait_recv()
        part = part + z2_recv[index].astype(F32)
    z3[col] = part.astype(BF16)
    z3_copies = [remote(z3.at[col], z3.at[col], at_col(*peer)) for peer in col_peers]
    au = send(ga, 0, 0, up)
    ad = send(ga, 0, 0, down)
    fb = send(gb, 0, 0, flip)
    bu.wait_recv()
    bu2 = send(gb, 3, 0, up, top)
    pair.append(send(gb, 3, 0, partner))
    bd.wait_recv()
    bd2 = send(gb, 1, 0, down, low)
    pair.append(send(gb, 1, 0, partner))
    for copy in z3_copies:
        copy.wait_recv()
    total = z3[0].astype(F32)
    for index in range(1, 8):
        total = total + z3[index].astype(F32)
    field[mine, :] = total.astype(BF16)
    z4_copies = [
        remote(field.at[mine], field.at[mine], at_row(dz, dh, 0)) for dz, dh in chip_peers
    ]
    f_m = send(gb, 3, 0, flip)
    f_p = send(gb, 1, 0, flip)
    fa.wait_recv()
    fau = send(ga, 0, 1, up)
    fad = send(ga, 0, 1, down)
    pair.append(send(ga, 0, 1, partner))
    fb.wait_recv()
    pair.append(send(gb, 0, 1, partner))
    for copy in z4_copies:
        copy.wait_recv()

    token = lax.broadcasted_iota(jnp.int32, (1, TOK), 1)
    line, place = token >> 6, token & (GW - 1)

    def moved(values, di, dj):
        shift = di * GW + dj
        if shift:
            values = pltpu.roll(values, (-shift) % TOK, 1)
        inside = (
            (line + di >= 0) & (line + di < GH) & (place + dj >= 0) & (place + dj < GW)
        )
        return jnp.where(inside, values, 0.0)

    @pl.loop(0, TOK // 128)
    def _(t):
        at = pl.ds(pl.multiple_of(t * 128, 128), 128)
        value = field[:, at].astype(F32)
        act = (value * cdf(value)).astype(BF16).astype(F32)
        for k in range(9):
            shifted[k : k + 1, at] = jnp.sum(act * taps[k], axis=0, keepdims=True)
        shifted[9:10, at] = jnp.sum(value * taps[9], axis=0, keepdims=True)

    pred = shifted[9:10, :]
    for k in range(9):
        pred = pred + moved(shifted[k : k + 1, :], k // 3 - 1, k % 3 - 1)
    for index in range(8):
        rows_buf[index : index + 1, :] = pred[:, index * STRIP : (index + 1) * STRIP]
    pred_all[c] = rows_buf[...]
    pred_copy = remote(pred_all.at[c], pred_all.at[c], partner)
    bu2.wait_recv()
    f_top = send(gb, 2, 0, flip, top)
    pair.append(send(gb, 2, 0, partner, top))
    bd2.wait_recv()
    f_low = send(gb, 2, 0, flip, low)
    pair.append(send(gb, 2, 0, partner, low))
    au.wait_recv()
    au2 = send(ga, 3, 0, up)
    pair.append(send(ga, 3, 0, partner))
    ad.wait_recv()
    pair.append(send(ga, 1, 0, partner))

    @pl.loop(0, TOK // 128)
    def _(t):
        at = pl.ds(pl.multiple_of(t * 128, 128), 128)
        field_slope[:, at] = slope(field[:, at].astype(F32))

    valid = jnp.concatenate([st_col[index][2:3] for index in range(8)], axis=0)
    target = jnp.concatenate([st_col[index][3:4] for index in range(8)], axis=0)
    pred_copy.wait_recv()
    err = valid * (pred_all[0] + pred_all[1] - target)

    def whole(values):
        return jnp.sum(jnp.sum(values, axis=1, keepdims=True), axis=0, keepdims=True)

    count = whole(valid)
    mean_err = whole(err) / count
    loss_ref[0, 0] = jnp.sum(whole(err * err) / count - FOCUS * mean_err * mean_err)
    grad_pred = valid * (2.0 * err - 2.0 * FOCUS * mean_err)
    grad_pred = jnp.concatenate([grad_pred[index : index + 1] for index in range(8)], axis=1)
    for k in range(9):
        shifted[k : k + 1, :] = moved(grad_pred, 1 - k // 3, 1 - k % 3)
    shifted[9:10, :] = grad_pred

    @pl.loop(0, TOK // 128)
    def _(t):
        at = pl.ds(pl.multiple_of(t * 128, 128), 128)
        back = taps[0] * shifted[0:1, at]
        for k in range(1, 9):
            back = back + taps[k] * shifted[k : k + 1, at]
        gz[pl.ds(first_channel, 128), at] = (
            taps[9] * shifted[9:10, at] + field_slope[:, at] * back
        ).astype(BF16)

    half_z = gz.at[pl.ds(first_channel, 128)]
    gz_copy = remote(half_z, half_z, partner)

    second_channel = pl.multiple_of(other * 128, 128)
    gh_own[:, pl.ds(first_channel, 128)] = nt(hid[...], half_z[...]).astype(BF16)
    gz_copy.wait_recv()
    gh_own[:, pl.ds(second_channel, 128)] = nt(
        hid[...], gz[pl.ds(second_channel, 128), :]
    ).astype(BF16)
    local(gh_own, gh_out.at[own_rows(0, 0)])
    bulk_to = len(sent)
    gh_copies = [
        remote(gh_own, gh_out.at[own_rows(0, 0)], at_row(dz, dh, 0)) for dz, dh in chip_peers
    ]
    gh_pair = [remote(gh_own, gh_out.at[own_rows(0, 0)], partner)]
    bulk_end = len(sent)
    f_m.wait_recv()
    pair.append(send(gb, 3, 1, partner))
    fad.wait_recv()
    fad2 = send(ga, 1, 1, down)
    pair.append(send(ga, 1, 1, partner))
    fau.wait_recv()
    pair.append(send(ga, 3, 1, partner))
    f_p.wait_recv()
    pair.append(send(gb, 1, 1, partner))
    f_top.wait_recv()
    pair.append(send(gb, 2, 1, partner, top))
    f_low.wait_recv()
    pair.append(send(gb, 2, 1, partner, low))
    au2.wait_recv()
    pair.append(send(ga, 2, 0, partner))
    fad2.wait_recv()
    pair.append(send(ga, 2, 1, partner))
    for copy in pair:
        copy.wait_recv()
    bulk = sent[bulk_from:bulk_to] + sent[bulk_end:]
    for copy in bulk:
        copy.wait_send()

    @pl.loop(0, 16)
    def _(k):
        weights = ga[k, :, TA:]
        ga[k, :, :TA] = (mm(weights, gz[:, :TA]) * ga[k, :, :TA].astype(F32)).astype(BF16)
        gb[k] = (mm(weights, gz[:, TA:]) * gb[k].astype(F32)).astype(BF16)
        pltpu.make_async_copy(ga.at[k, :, :TA], gp_out.at[pl.ds(pl.multiple_of(k * OWN, 64), OWN), :TA], out_sems.at[0, k]).start()
        pltpu.make_async_copy(gb.at[k], gp_out.at[pl.ds(pl.multiple_of(k * OWN, 64), OWN), TA:], out_sems.at[1, k]).start()

    for (dz, dh), copy in zip(chip_peers, gh_copies):
        copy.wait_recv()
        came = gh_out.at[own_rows(-dz, dh)]
        gh_pair.append(remote(came, came, partner))
    for copy in gh_pair:
        copy.wait_recv()

    @pl.loop(0, 16)
    def _(k):
        pltpu.make_async_copy(ga.at[k, :, :TA], gp_out.at[pl.ds(pl.multiple_of(k * OWN, 64), OWN), :TA], out_sems.at[0, k]).wait()
        pltpu.make_async_copy(gb.at[k], gp_out.at[pl.ds(pl.multiple_of(k * OWN, 64), OWN), TA:], out_sems.at[1, k]).wait()

    for copy in started[-2:]:
        copy.wait()
    for copy in sent:
        if not any(copy is other_copy for other_copy in bulk):
            copy.wait_send()


def weight_kernel(n_ref, gp_ref, gh_ref, proj_ref, up_ref, down_ref):
    up_ref[...] = nt(n_ref[...], gp_ref[...])
    down_ref[...] = nt(gh_ref[...], proj_ref[...])


def on_device(tokens, ln_gain, w_up, w_down, proj, conv_kernel, head_weight, depth_mm, lidar_mask):
    vmem = pl.BlockSpec(memory_space=pltpu.VMEM)
    anywhere = pl.BlockSpec(memory_space=pl.ANY)
    normed, grad_pre, grad_hidden, loss = pl.pallas_call(
        step_kernel,
        name="mlp_step",
        out_shape=[
            jax.ShapeDtypeStruct((FEAT, TOK), BF16),
            jax.ShapeDtypeStruct((HID, TOK), BF16),
            jax.ShapeDtypeStruct((HID, CH), BF16),
            jax.ShapeDtypeStruct((1, 1), F32),
        ],
        in_specs=[
            anywhere, vmem, anywhere, anywhere, anywhere, anywhere, vmem, anywhere, anywhere,
        ],
        out_specs=[anywhere, anywhere, anywhere, pl.BlockSpec(memory_space=pltpu.SMEM)],
        scratch_shapes=[
            pltpu.VMEM((STRIP, FEAT), BF16),
            pltpu.VMEM((FEAT, HID), BF16),
            pltpu.VMEM((HID, FEAT), BF16),
            pltpu.VMEM((FEAT, CH), BF16),
            pltpu.VMEM((9, 128, CH), BF16),
            pltpu.VMEM((2, GW), jnp.int32),
            pltpu.VMEM((2, GW), jnp.int32),
            pltpu.VMEM((8, FEAT, STRIP), BF16),
            pltpu.VMEM((16, 8, STRIP), F32),
            pltpu.VMEM((8, 8, STRIP), F32),
            pltpu.VMEM((HALF, 2 * FEAT), BF16),
            pltpu.VMEM((HALF, FEAT), BF16),
            pltpu.VMEM((HALF, FEAT), BF16),
            pltpu.VMEM((FEAT, CH), BF16),
            pltpu.VMEM((2 * FEAT, TOK), BF16),
            pltpu.VMEM((8, OWN, CH), F32),
            pltpu.VMEM((8, OWN, CH), BF16),
            pltpu.VMEM((7, OWN, CH), BF16),
            pltpu.VMEM((OWN, CH), BF16),
            pltpu.VMEM((4, 2, OWN, TA), BF16),
            pltpu.VMEM((4, 2, OWN, TB), BF16),
            pltpu.VMEM((2, OWN, TA), BF16),
            pltpu.VMEM((2, 2, OWN, TA), BF16),
            pltpu.VMEM((OWN, TA), BF16),
            pltpu.VMEM((4, OWN, TB), BF16),
            pltpu.VMEM((2, OWN // 2, TB), BF16),
            pltpu.VMEM((2, OWN, TB), BF16),
            pltpu.VMEM((OWN, TOK), F32),
            pltpu.VMEM((OWN, TOK), BF16),
            pltpu.VMEM((CH, TOK), F32),
            pltpu.VMEM((128, TOK), BF16),
            pltpu.VMEM((128, TOK), BF16),
            pltpu.VMEM((128, TOK), BF16),
            pltpu.VMEM((7, 16, TOK), BF16),
            pltpu.VMEM((8, 16, TOK), BF16),
            pltpu.VMEM((10, 128, 128), F32),
            pltpu.VMEM((128, TOK), BF16),
            pltpu.VMEM((128, TOK), F32),
            pltpu.VMEM((16, TOK), F32),
            pltpu.VMEM((2, 8, STRIP), F32),
            pltpu.VMEM((8, STRIP), F32),
            pltpu.VMEM((CH, TOK), BF16),
            pltpu.VMEM((16, OWN, GA), BF16),
            pltpu.VMEM((16, OWN, TB), BF16),
            pltpu.VMEM((OWN, CH), BF16),
            pltpu.SemaphoreType.DMA((N_SEMS,)),
            pltpu.SemaphoreType.DMA((N_SEMS,)),
            pltpu.SemaphoreType.DMA((9,)),
            pltpu.SemaphoreType.DMA((2, 16)),
        ],
        compiler_params=pltpu.CompilerParams(
            collective_id=0, has_side_effects=True, vmem_limit_bytes=60 * 2**20
        ),
        cost_estimate=pl.CostEstimate(flops=6 * 10**9, bytes_accessed=16 * 2**20, transcendentals=10**6),
    )(
        tokens, ln_gain, w_up, w_down, proj, conv_kernel.reshape(9, CH, CH),
        head_weight.reshape(1, CH), depth_mm, lidar_mask,
    )
    grad_up, grad_down = pl.pallas_call(
        weight_kernel,
        name="weight_grads",
        grid=(HID // 512,),
        out_shape=[
            jax.ShapeDtypeStruct((FEAT, HID), F32),
            jax.ShapeDtypeStruct((HID, FEAT), F32),
        ],
        in_specs=[
            pl.BlockSpec((FEAT, TOK), lambda j: (0, 0)),
            pl.BlockSpec((512, TOK), lambda j: (j, 0)),
            pl.BlockSpec((512, CH), lambda j: (j, 0)),
            pl.BlockSpec((FEAT, CH), lambda j: (0, 0)),
        ],
        out_specs=[
            pl.BlockSpec((FEAT, 512), lambda j: (0, j)),
            pl.BlockSpec((512, FEAT), lambda j: (j, 0)),
        ],
        compiler_params=pltpu.CompilerParams(vmem_limit_bytes=60 * 2**20),
        cost_estimate=pl.CostEstimate(flops=3 * 10**9, bytes_accessed=18 * 2**20, transcendentals=0),
    )(normed, grad_pre, grad_hidden, proj)
    return (grad_up, grad_down, loss.reshape(()))


def solution(mesh):
    return jax.shard_map(
        on_device,
        mesh=mesh,
        in_specs=(
            P("col", "row"),
            P("row"),
            P("row", "col"),
            P("col", "row"),
            P("row", None),
            P(),
            P(),
            P("col", None),
            P("col", None),
        ),
        out_specs=(P("row", "col"), P("col", "row"), P()),
        check_vma=False,
    )
```

```python
import math

import jax
import jax.numpy as jnp
from jax import lax
from jax.experimental import pallas as pl
from jax.experimental.pallas import tpu as pltpu
from jax.sharding import PartitionSpec as P

MESH = pl.DeviceIdType.MESH
F32 = jnp.float32
BF16 = jnp.bfloat16

WIDTH = 6144
GW = 64
GH = 16
TOK = 1024
STRIP = 128
FEAT = 384
HID = 3072
HALF = 1536
OWN = 192
CH = 256
TA = 512
TB = TOK - TA
FOCUS = 0.85
EPS = 1e-06

ROOT_HALF = math.sqrt(0.5)
DENSITY = 1.0 / math.sqrt(2.0 * math.pi)

N_SEMS = 192


def cdf(v):
    return 0.5 * (1.0 + lax.erf(v * ROOT_HALF))


def slope(v):
    return cdf(v) + v * (DENSITY * jnp.exp(-0.5 * v * v))


def tn(a, b):
    return lax.dot_general(a, b, (((0,), (0,)), ((), ())), preferred_element_type=F32)


def nt(a, b):
    return lax.dot_general(a, b, (((1,), (1,)), ((), ())), preferred_element_type=F32)


def mm(a, b):
    return jnp.dot(a, b, preferred_element_type=F32)


def step_kernel(
    tok_hbm, gain_ref, wup_hbm, wdn_hbm, proj_hbm, conv_hbm, head_ref, depth_hbm, mask_hbm,
    nt_out, gp_out, gh_out, loss_ref,
    tok_ref, wup_ref, wdn, proj_ref, conv, depth_ref, mask_ref,
    xall, st_row, st_col, w_t, w_send, wd_peer, proj_peer, n_t, m_sum, m_part, m_recv, m_own,
    p_a, p_b, a1, a2, a3, b1, b2, b3, pre, hid, zc, z1, z1_recv, z2, z2_recv, z3,
    taps, field, field_slope, shifted, pred_all, rows_buf, gz, gm, ga, gb, gh_own, send_sems, recv_sems, local_sems, out_sems,
):
    row, col = lax.axis_index("row"), lax.axis_index("col")
    z, h, c = row // 4, lax.rem(row // 2, 2), lax.rem(row, 2)
    used = [0]

    def zz(dz):
        return lax.rem(z + dz + 4, 4)

    def hh(dh):
        return lax.rem(h + dh, 2)

    def at_row(dz, dh, dc):
        return {"row": zz(dz) * 4 + hh(dh) * 2 + lax.rem(c + dc, 2)}

    def at_col(dl, dx):
        return {"col": lax.rem(col // 4 + dl, 2) * 4 + lax.rem(lax.rem(col, 4) + dx, 4)}

    def remote(src, dst, device):
        at = used[0]
        used[0] += 1
        copy = pltpu.make_async_remote_copy(
            src_ref=src, dst_ref=dst, send_sem=send_sems.at[at], recv_sem=recv_sems.at[at],
            device_id=device, device_id_type=MESH,
        )
        copy.start()
        sent.append(copy)
        return copy

    def slot(dz, dh):
        return c * 8 + zz(dz) * 2 + hh(dh)

    def own_rows(dz, dh):
        return pl.ds(pl.multiple_of(slot(dz, dh) * OWN, 64), OWN)

    sent = []
    row_peers = [
        (dz, dh, dc) for dz in (2, 1, 3, 0) for dh in (1, 0) for dc in (1, 0) if (dz, dh, dc) != (0, 0, 0)
    ]
    chip_peers = [(dz, dh) for dz in (2, 1, 3, 0) for dh in (1, 0) if (dz, dh) != (0, 0)]
    col_peers = [(dl, dx) for dl in (1, 0) for dx in (2, 1, 3, 0) if (dl, dx) != (0, 0)]
    partner = at_row(0, 0, 1)
    here = z * 2 + h
    other = 1 - c

    barrier = pltpu.get_barrier_semaphore()
    for peer in row_peers:
        pl.semaphore_signal(barrier, inc=1, device_id=at_row(*peer), device_id_type=MESH)
    for peer in col_peers:
        pl.semaphore_signal(barrier, inc=1, device_id=at_col(*peer), device_id_type=MESH)

    started = []

    def local(src, dst):
        copy = pltpu.make_async_copy(src, dst, local_sems.at[len(started)])
        copy.start()
        started.append(copy)
        return copy

    first_channel = pl.multiple_of(c * 128, 128)
    tok_copy = local(tok_hbm, tok_ref)
    proj_in = local(proj_hbm, proj_ref)
    wdn_copy = local(wdn_hbm, wdn)
    wup_copy = local(wup_hbm, wup_ref)
    depth_copy = local(depth_hbm, depth_ref)
    mask_copy = local(mask_hbm, mask_ref)
    conv_copy = local(conv_hbm.at[:, pl.ds(first_channel, 128), :], conv)

    tok_copy.wait()
    x_t = tok_ref[...].astype(F32).T
    xall[col] = x_t.astype(BF16)
    st_row[row] = jnp.concatenate(
        [
            jnp.sum(x_t, 0, keepdims=True),
            jnp.sum(x_t * x_t, 0, keepdims=True),
            jnp.zeros((6, STRIP), F32),
        ],
        axis=0,
    )
    own_half = pl.multiple_of(c * HALF, HALF)
    to_peer = pl.multiple_of(other * HALF, HALF)
    pl.semaphore_wait(barrier, len(row_peers) + len(col_peers))

    stat_copies = [remote(st_row.at[row], st_row.at[row], at_row(*peer)) for peer in row_peers]
    across = remote(xall.at[col], xall.at[col], at_col(1, 0))
    token_copies = [remote(xall.at[col], xall.at[col], at_col(0, dx)) for dx in (2, 1, 3)]
    proj_in.wait()
    wdn_copy.wait()
    wd_copy = remote(wdn.at[pl.ds(to_peer, HALF)], wd_peer, partner)
    proj_copy = remote(proj_ref, proj_peer, partner)

    @pl.loop(0, 8)
    def _(k):
        m_sum[k] = mm(wdn[pl.ds(pl.multiple_of(own_half + k * OWN, 64), OWN), :], proj_ref[...])

    across.wait_recv()
    came = xall.at[lax.rem(col + 4, 8)]
    token_copies += [remote(came, came, at_col(0, dx)) for dx in (2, 1, 3)]

    wd_copy.wait_recv()
    proj_copy.wait_recv()

    @pl.loop(0, 8)
    def _(k):
        more = mm(wd_peer[pl.ds(pl.multiple_of(k * OWN, 64), OWN), :], proj_peer[...])
        m_part[k] = (m_sum[k] + more).astype(BF16)

    m_copies = []
    for index, (dz, dh) in enumerate(chip_peers):
        m_copies.append(
            remote(m_part.at[zz(dz) * 2 + hh(dh)], m_recv.at[index], at_row(dz, dh, 0))
        )

    for copy in stat_copies:
        copy.wait_recv()
    total = st_row[0]
    for index in range(1, 16):
        total = total + st_row[index]
    mean = total[0:1] / WIDTH
    spread = total[1:2] / WIDTH - mean * mean
    depth_copy.wait()
    mask_copy.wait()
    depth = depth_ref[...].astype(F32)
    seen = mask_ref[...].astype(F32)
    st_col[col] = jnp.concatenate(
        [
            mean,
            lax.rsqrt(spread + EPS),
            jnp.concatenate([seen[0:1], seen[1:2]], axis=1),
            jnp.log(jnp.concatenate([depth[0:1], depth[1:2]], axis=1) * 0.001),
            jnp.zeros((4, STRIP), F32),
        ],
        axis=0,
    )
    norm_copies = [remote(st_col.at[col], st_col.at[col], at_col(*peer)) for peer in col_peers]

    feature_at = pl.multiple_of(c * FEAT, 128)
    wup_copy.wait()

    @pl.loop(0, HALF // 128)
    def _(i):
        at = pl.multiple_of(to_peer + i * 128, 128)
        w_send[pl.ds(pl.multiple_of(i * 128, 128), 128), :] = wup_ref[:, pl.ds(at, 128)].T

    w_copy = remote(w_send, w_t.at[:, pl.ds(feature_at, FEAT)], partner)

    @pl.loop(0, HALF // 128)
    def _(i):
        at = pl.multiple_of(own_half + i * 128, 128)
        w_t[pl.ds(pl.multiple_of(i * 128, 128), 128), pl.ds(feature_at, FEAT)] = wup_ref[:, pl.ds(at, 128)].T

    gain = jnp.broadcast_to(gain_ref[...].reshape(1, FEAT), (STRIP, FEAT)).T
    for copy in norm_copies:
        copy.wait_recv()
    for copy in token_copies:
        copy.wait_recv()

    n_copies = []
    for first in (0, 4):
        for index in range(first, first + 4):
            stats = st_col[index]
            n_t[pl.ds(feature_at, FEAT), index * STRIP : (index + 1) * STRIP] = (
                (xall[index].astype(F32) - stats[0:1]) * stats[1:2] * gain
            ).astype(BF16)
        half = n_t.at[pl.ds(feature_at, FEAT), first * STRIP : (first + 4) * STRIP]
        n_copies.append(remote(half, half, partner))
    local(n_t.at[pl.ds(feature_at, FEAT)], nt_out)
    w_copy.wait_recv()

    a_copies, b_copies = {}, {}

    def project(dz, into, first):
        base = pl.multiple_of(zz(dz) * 2 * OWN, 2 * OWN)

        @pl.loop(0, into.shape[3] // 256)
        def _(t):
            at = pl.multiple_of(t * 256, 256)
            both = mm(
                w_t[pl.ds(base, 2 * OWN), :], n_t[:, pl.ds(pl.multiple_of(first + at, 256), 256)]
            ).astype(BF16)
            into[zz(dz), 0, :, pl.ds(at, 256)] = both[:OWN]
            into[zz(dz), 1, :, pl.ds(at, 256)] = both[OWN:]

    up, down, flip = at_row(1, 0, 0), at_row(3, 0, 0), at_row(0, 1, 0)
    n_copies[0].wait_recv()
    project(2, p_a, 0)
    a_up = remote(p_a.at[zz(2), 0], a1.at[0], up)
    a_down = remote(p_a.at[zz(2), 1], a1.at[1], down)
    n_copies[1].wait_recv()
    for dz in (2, 1, 3, 0):
        project(dz, p_b, TA)
        b_copies[dz] = remote(p_b.at[zz(dz), 1 - h], b1.at[zz(dz)], flip)
    for dz in (1, 3, 0):
        project(dz, p_a, 0)

    def add(into, more):
        into[...] = (into[...].astype(F32) + more[...].astype(F32)).astype(BF16)

    a_up.wait_recv()
    add(p_a.at[zz(1), 0], a1.at[0])
    a_up2 = remote(p_a.at[zz(1)], a2.at[0], up)
    a_down.wait_recv()
    add(p_a.at[zz(3), 1], a1.at[1])
    a_down2 = remote(p_a.at[zz(3)], a2.at[1], down)

    b_copies[2].wait_recv()
    add(p_b.at[zz(2), h], b1.at[zz(2)])
    b_up = remote(p_b.at[zz(2), h, 0:96], b2.at[0], up)
    b_down = remote(p_b.at[zz(2), h, 96:192], b2.at[1], down)
    b_copies[1].wait_recv()
    add(p_b.at[zz(1), h], b1.at[zz(1)])
    b_copies[3].wait_recv()
    add(p_b.at[zz(3), h], b1.at[zz(3)])

    a_up2.wait_recv()
    a_down2.wait_recv()
    p_a[z, 1 - h] = (
        p_a[z, 1 - h].astype(F32) + a2[0, 1 - h].astype(F32) + a2[1, 1 - h].astype(F32)
    ).astype(BF16)
    a_flip = remote(p_a.at[z, 1 - h], a3, flip)

    b_up.wait_recv()
    add(p_b.at[zz(1), h, 0:96], b2.at[0])
    b_up2 = remote(p_b.at[zz(1), h], b3.at[0], up)
    b_down.wait_recv()
    add(p_b.at[zz(3), h, 96:192], b2.at[1])
    b_down2 = remote(p_b.at[zz(3), h], b3.at[1], down)

    for copy in m_copies:
        copy.wait_recv()
    total = m_part[here].astype(F32)
    for index in range(7):
        total = total + m_recv[index].astype(F32)
    m_own[...] = total.astype(BF16)
    gm[slot(0, 0)] = m_own[...]
    pair = []

    def send(buf, dz, dh, device, rows=None):
        ref = buf.at[slot(dz, dh)] if rows is None else buf.at[slot(dz, dh), rows[0] : rows[1]]
        return remote(ref, ref, device)

    mf = send(gm, 0, 0, flip)
    mu = send(gm, 0, 0, up)
    md = send(gm, 0, 0, down)
    pair.append(send(gm, 0, 0, partner))
    x_proj = tn(proj_ref[...], xall[col])

    conv_copy.wait()
    head = head_ref[...]
    for k in range(9):
        taps[k] = jnp.broadcast_to(
            jnp.sum(conv[k].astype(F32) * head, axis=1, keepdims=True), (128, 128)
        )
    lane = lax.broadcasted_iota(jnp.int32, (128, CH), 1)
    sub = lax.broadcasted_iota(jnp.int32, (128, CH), 0)
    taps[9] = jnp.broadcast_to(
        jnp.sum(jnp.where(lane == sub + first_channel, head, 0.0), axis=1, keepdims=True), (128, 128)
    )

    b_copies[0].wait_recv()
    a_flip.wait_recv()
    pre[:, :TA] = (
        p_a[z, h].astype(F32) + a2[0, h].astype(F32) + a2[1, h].astype(F32) + a3[...].astype(F32)
    )
    b_up2.wait_recv()
    b_down2.wait_recv()
    pre[:, TA:] = (
        p_b[z, h].astype(F32) + b1[z].astype(F32) + b3[0].astype(F32) + b3[1].astype(F32)
    )

    @pl.loop(0, TOK // 128)
    def _(t):
        at = pl.ds(pl.multiple_of(t * 128, 128), 128)
        value = pre[:, at]
        hid[:, at] = (value * cdf(value)).astype(BF16)

    @pl.loop(0, TOK // 256)
    def _(t):
        at = pl.ds(pl.multiple_of(t * 256, 256), 256)
        zc[:, at] = tn(m_own[...], hid[:, at])

    strip = pl.ds(pl.multiple_of(col * STRIP, STRIP), STRIP)
    zc[:, strip] = zc[:, strip] + x_proj

    z1[...] = zc[pl.ds(pl.multiple_of(other * 128, 128), 128), :].astype(BF16)
    z1_copy = remote(z1, z1_recv, partner)

    bulk_from = len(sent)
    mine_a, mine_b = ga.at[slot(0, 0)], gb.at[slot(0, 0)]
    mf.wait_recv()
    mfu = send(gm, 0, 1, up)
    mfd = send(gm, 0, 1, down)
    pair.append(send(gm, 0, 1, partner))
    top, low = (0, 96), (96, 192)

    @pl.loop(0, TB // 128)
    def _(t):
        at = pl.ds(pl.multiple_of(t * 128, 128), 128)
        mine_b[:, at] = slope(pre[:, pl.ds(pl.multiple_of(TA + t * 128, 128), 128)]).astype(BF16)

    z1_copy.wait_recv()
    z2[...] = (
        zc[pl.ds(pl.multiple_of(c * 128, 128), 128), :] + z1_recv[...].astype(F32)
    ).astype(BF16)
    z2_copies = []
    for index, (dz, dh) in enumerate(chip_peers):
        at = pl.multiple_of((zz(dz) * 2 + hh(dh)) * 16, 16)
        z2_copies.append(remote(z2.at[pl.ds(at, 16)], z2_recv.at[index], at_row(dz, dh, 0)))
    bu = send(gb, 0, 0, up)
    bd = send(gb, 0, 0, down)
    mu.wait_recv()
    mu2 = send(gm, 3, 0, up)
    pair.append(send(gm, 3, 0, partner))
    md.wait_recv()
    pair.append(send(gm, 1, 0, partner))
    pair.append(send(gb, 0, 0, partner))

    @pl.loop(0, TA // 128)
    def _(t):
        at = pl.ds(pl.multiple_of(t * 128, 128), 128)
        mine_a[:, at] = slope(pre[:, at]).astype(BF16)

    fa = send(ga, 0, 0, flip)
    mfd.wait_recv()
    mfd2 = send(gm, 1, 1, down)
    pair.append(send(gm, 1, 1, partner))
    mfu.wait_recv()
    pair.append(send(gm, 3, 1, partner))
    pair.append(send(ga, 0, 0, partner))
    mine = pl.ds(pl.multiple_of(here * 16, 16), 16)
    part = z2[mine, :].astype(F32)
    for index, copy in enumerate(z2_copies):
        copy.wait_recv()
        part = part + z2_recv[index].astype(F32)
    z3[col] = part.astype(BF16)
    z3_copies = [remote(z3.at[col], z3.at[col], at_col(*peer)) for peer in col_peers]
    au = send(ga, 0, 0, up)
    ad = send(ga, 0, 0, down)
    fb = send(gb, 0, 0, flip)
    bu.wait_recv()
    bu2 = send(gb, 3, 0, up, top)
    pair.append(send(gb, 3, 0, partner))
    bd.wait_recv()
    bd2 = send(gb, 1, 0, down, low)
    pair.append(send(gb, 1, 0, partner))
    for copy in z3_copies:
        copy.wait_recv()
    total = z3[0].astype(F32)
    for index in range(1, 8):
        total = total + z3[index].astype(F32)
    field[mine, :] = total.astype(BF16)
    z4_copies = [
        remote(field.at[mine], field.at[mine], at_row(dz, dh, 0)) for dz, dh in chip_peers
    ]
    f_m = send(gb, 3, 0, flip)
    f_p = send(gb, 1, 0, flip)
    fa.wait_recv()
    fau = send(ga, 0, 1, up)
    fad = send(ga, 0, 1, down)
    pair.append(send(ga, 0, 1, partner))
    au.wait_recv()
    au2 = send(ga, 3, 0, up)
    pair.append(send(ga, 3, 0, partner))
    ad.wait_recv()
    pair.append(send(ga, 1, 0, partner))
    fb.wait_recv()
    pair.append(send(gb, 0, 1, partner))
    mu2.wait_recv()
    pair.append(send(gm, 2, 0, partner))
    mfd2.wait_recv()
    pair.append(send(gm, 2, 1, partner))
    for copy in z4_copies:
        copy.wait_recv()

    token = lax.broadcasted_iota(jnp.int32, (1, TOK), 1)
    line, place = token >> 6, token & (GW - 1)

    def moved(values, di, dj):
        shift = di * GW + dj
        if shift:
            values = pltpu.roll(values, (-shift) % TOK, 1)
        inside = (
            (line + di >= 0) & (line + di < GH) & (place + dj >= 0) & (place + dj < GW)
        )
        return jnp.where(inside, values, 0.0)

    @pl.loop(0, TOK // 128)
    def _(t):
        at = pl.ds(pl.multiple_of(t * 128, 128), 128)
        value = field[:, at].astype(F32)
        act = (value * cdf(value)).astype(BF16).astype(F32)
        for k in range(9):
            shifted[k : k + 1, at] = jnp.sum(act * taps[k], axis=0, keepdims=True)
        shifted[9:10, at] = jnp.sum(value * taps[9], axis=0, keepdims=True)

    pred = shifted[9:10, :]
    for k in range(9):
        pred = pred + moved(shifted[k : k + 1, :], k // 3 - 1, k % 3 - 1)
    for index in range(8):
        rows_buf[index : index + 1, :] = pred[:, index * STRIP : (index + 1) * STRIP]
    pred_all[c] = rows_buf[...]
    pred_copy = remote(pred_all.at[c], pred_all.at[c], partner)
    bu2.wait_recv()
    f_top = send(gb, 2, 0, flip, top)
    pair.append(send(gb, 2, 0, partner, top))
    bd2.wait_recv()
    f_low = send(gb, 2, 0, flip, low)
    pair.append(send(gb, 2, 0, partner, low))

    @pl.loop(0, TOK // 128)
    def _(t):
        at = pl.ds(pl.multiple_of(t * 128, 128), 128)
        field_slope[:, at] = slope(field[:, at].astype(F32))

    valid = jnp.concatenate([st_col[index][2:3] for index in range(8)], axis=0)
    target = jnp.concatenate([st_col[index][3:4] for index in range(8)], axis=0)
    pred_copy.wait_recv()
    err = valid * (pred_all[0] + pred_all[1] - target)

    def whole(values):
        return jnp.sum(jnp.sum(values, axis=1, keepdims=True), axis=0, keepdims=True)

    count = whole(valid)
    mean_err = whole(err) / count
    loss_ref[0, 0] = jnp.sum(whole(err * err) / count - FOCUS * mean_err * mean_err)
    grad_pred = valid * (2.0 * err - 2.0 * FOCUS * mean_err)
    grad_pred = jnp.concatenate([grad_pred[index : index + 1] for index in range(8)], axis=1)
    for k in range(9):
        shifted[k : k + 1, :] = moved(grad_pred, 1 - k // 3, 1 - k % 3)
    shifted[9:10, :] = grad_pred

    @pl.loop(0, TOK // 128)
    def _(t):
        at = pl.ds(pl.multiple_of(t * 128, 128), 128)
        back = taps[0] * shifted[0:1, at]
        for k in range(1, 9):
            back = back + taps[k] * shifted[k : k + 1, at]
        gz[pl.ds(first_channel, 128), at] = (
            taps[9] * shifted[9:10, at] + field_slope[:, at] * back
        ).astype(BF16)

    half_z = gz.at[pl.ds(first_channel, 128)]
    gz_copy = remote(half_z, half_z, partner)

    second_channel = pl.multiple_of(other * 128, 128)
    gh_own[:, pl.ds(first_channel, 128)] = nt(hid[...], half_z[...]).astype(BF16)
    gz_copy.wait_recv()
    gh_own[:, pl.ds(second_channel, 128)] = nt(
        hid[...], gz[pl.ds(second_channel, 128), :]
    ).astype(BF16)
    local(gh_own, gh_out.at[own_rows(0, 0)])
    bulk_to = len(sent)
    gh_copies = [
        remote(gh_own, gh_out.at[own_rows(0, 0)], at_row(dz, dh, 0)) for dz, dh in chip_peers
    ]
    gh_pair = [remote(gh_own, gh_out.at[own_rows(0, 0)], partner)]
    bulk_end = len(sent)
    f_m.wait_recv()
    pair.append(send(gb, 3, 1, partner))
    fad.wait_recv()
    fad2 = send(ga, 1, 1, down)
    pair.append(send(ga, 1, 1, partner))
    fau.wait_recv()
    pair.append(send(ga, 3, 1, partner))
    f_p.wait_recv()
    pair.append(send(gb, 1, 1, partner))
    f_top.wait_recv()
    pair.append(send(gb, 2, 1, partner, top))
    f_low.wait_recv()
    pair.append(send(gb, 2, 1, partner, low))
    au2.wait_recv()
    pair.append(send(ga, 2, 0, partner))
    fad2.wait_recv()
    pair.append(send(ga, 2, 1, partner))
    for copy in pair:
        copy.wait_recv()
    bulk = sent[bulk_from:bulk_to] + sent[bulk_end:]
    for copy in bulk:
        copy.wait_send()

    @pl.loop(0, 16)
    def _(k):
        weights = gm[k]
        ga[k] = (mm(weights, gz[:, :TA]) * ga[k].astype(F32)).astype(BF16)
        gb[k] = (mm(weights, gz[:, TA:]) * gb[k].astype(F32)).astype(BF16)
        pltpu.make_async_copy(ga.at[k], gp_out.at[pl.ds(pl.multiple_of(k * OWN, 64), OWN), :TA], out_sems.at[0, k]).start()
        pltpu.make_async_copy(gb.at[k], gp_out.at[pl.ds(pl.multiple_of(k * OWN, 64), OWN), TA:], out_sems.at[1, k]).start()

    for (dz, dh), copy in zip(chip_peers, gh_copies):
        copy.wait_recv()
        came = gh_out.at[own_rows(-dz, dh)]
        gh_pair.append(remote(came, came, partner))
    for copy in gh_pair:
        copy.wait_recv()

    @pl.loop(0, 16)
    def _(k):
        pltpu.make_async_copy(ga.at[k], gp_out.at[pl.ds(pl.multiple_of(k * OWN, 64), OWN), :TA], out_sems.at[0, k]).wait()
        pltpu.make_async_copy(gb.at[k], gp_out.at[pl.ds(pl.multiple_of(k * OWN, 64), OWN), TA:], out_sems.at[1, k]).wait()

    for copy in started[-2:]:
        copy.wait()
    for copy in sent:
        if not any(copy is other_copy for other_copy in bulk):
            copy.wait_send()


def weight_kernel(n_ref, gp_ref, gh_ref, proj_ref, up_ref, down_ref):
    up_ref[...] = nt(n_ref[...], gp_ref[...])
    down_ref[...] = nt(gh_ref[...], proj_ref[...])


def on_device(tokens, ln_gain, w_up, w_down, proj, conv_kernel, head_weight, depth_mm, lidar_mask):
    vmem = pl.BlockSpec(memory_space=pltpu.VMEM)
    anywhere = pl.BlockSpec(memory_space=pl.ANY)
    normed, grad_pre, grad_hidden, loss = pl.pallas_call(
        step_kernel,
        name="mlp_step",
        out_shape=[
            jax.ShapeDtypeStruct((FEAT, TOK), BF16),
            jax.ShapeDtypeStruct((HID, TOK), BF16),
            jax.ShapeDtypeStruct((HID, CH), BF16),
            jax.ShapeDtypeStruct((1, 1), F32),
        ],
        in_specs=[
            anywhere, vmem, anywhere, anywhere, anywhere, anywhere, vmem, anywhere, anywhere,
        ],
        out_specs=[anywhere, anywhere, anywhere, pl.BlockSpec(memory_space=pltpu.SMEM)],
        scratch_shapes=[
            pltpu.VMEM((STRIP, FEAT), BF16),
            pltpu.VMEM((FEAT, HID), BF16),
            pltpu.VMEM((HID, FEAT), BF16),
            pltpu.VMEM((FEAT, CH), BF16),
            pltpu.VMEM((9, 128, CH), BF16),
            pltpu.VMEM((2, GW), jnp.int32),
            pltpu.VMEM((2, GW), jnp.int32),
            pltpu.VMEM((8, FEAT, STRIP), BF16),
            pltpu.VMEM((16, 8, STRIP), F32),
            pltpu.VMEM((8, 8, STRIP), F32),
            pltpu.VMEM((HALF, 2 * FEAT), BF16),
            pltpu.VMEM((HALF, FEAT), BF16),
            pltpu.VMEM((HALF, FEAT), BF16),
            pltpu.VMEM((FEAT, CH), BF16),
            pltpu.VMEM((2 * FEAT, TOK), BF16),
            pltpu.VMEM((8, OWN, CH), F32),
            pltpu.VMEM((8, OWN, CH), BF16),
            pltpu.VMEM((7, OWN, CH), BF16),
            pltpu.VMEM((OWN, CH), BF16),
            pltpu.VMEM((4, 2, OWN, TA), BF16),
            pltpu.VMEM((4, 2, OWN, TB), BF16),
            pltpu.VMEM((2, OWN, TA), BF16),
            pltpu.VMEM((2, 2, OWN, TA), BF16),
            pltpu.VMEM((OWN, TA), BF16),
            pltpu.VMEM((4, OWN, TB), BF16),
            pltpu.VMEM((2, OWN // 2, TB), BF16),
            pltpu.VMEM((2, OWN, TB), BF16),
            pltpu.VMEM((OWN, TOK), F32),
            pltpu.VMEM((OWN, TOK), BF16),
            pltpu.VMEM((CH, TOK), F32),
            pltpu.VMEM((128, TOK), BF16),
            pltpu.VMEM((128, TOK), BF16),
            pltpu.VMEM((128, TOK), BF16),
            pltpu.VMEM((7, 16, TOK), BF16),
            pltpu.VMEM((8, 16, TOK), BF16),
            pltpu.VMEM((10, 128, 128), F32),
            pltpu.VMEM((128, TOK), BF16),
            pltpu.VMEM((128, TOK), F32),
            pltpu.VMEM((16, TOK), F32),
            pltpu.VMEM((2, 8, STRIP), F32),
            pltpu.VMEM((8, STRIP), F32),
            pltpu.VMEM((CH, TOK), BF16),
            pltpu.VMEM((16, OWN, CH), BF16),
            pltpu.VMEM((16, OWN, TA), BF16),
            pltpu.VMEM((16, OWN, TB), BF16),
            pltpu.VMEM((OWN, CH), BF16),
            pltpu.SemaphoreType.DMA((N_SEMS,)),
            pltpu.SemaphoreType.DMA((N_SEMS,)),
            pltpu.SemaphoreType.DMA((9,)),
            pltpu.SemaphoreType.DMA((2, 16)),
        ],
        compiler_params=pltpu.CompilerParams(
            collective_id=0, has_side_effects=True, vmem_limit_bytes=60 * 2**20
        ),
        cost_estimate=pl.CostEstimate(flops=6 * 10**9, bytes_accessed=16 * 2**20, transcendentals=10**6),
    )(
        tokens, ln_gain, w_up, w_down, proj, conv_kernel.reshape(9, CH, CH),
        head_weight.reshape(1, CH), depth_mm, lidar_mask,
    )
    grad_up, grad_down = pl.pallas_call(
        weight_kernel,
        name="weight_grads",
        grid=(HID // 512,),
        out_shape=[
            jax.ShapeDtypeStruct((FEAT, HID), F32),
            jax.ShapeDtypeStruct((HID, FEAT), F32),
        ],
        in_specs=[
            pl.BlockSpec((FEAT, TOK), lambda j: (0, 0)),
            pl.BlockSpec((512, TOK), lambda j: (j, 0)),
            pl.BlockSpec((512, CH), lambda j: (j, 0)),
            pl.BlockSpec((FEAT, CH), lambda j: (0, 0)),
        ],
        out_specs=[
            pl.BlockSpec((FEAT, 512), lambda j: (0, j)),
            pl.BlockSpec((512, FEAT), lambda j: (j, 0)),
        ],
        compiler_params=pltpu.CompilerParams(vmem_limit_bytes=60 * 2**20),
        cost_estimate=pl.CostEstimate(flops=3 * 10**9, bytes_accessed=18 * 2**20, transcendentals=0),
    )(normed, grad_pre, grad_hidden, proj)
    return (grad_up, grad_down, loss.reshape(()))


def solution(mesh):
    return jax.shard_map(
        on_device,
        mesh=mesh,
        in_specs=(
            P("col", "row"),
            P("row"),
            P("row", "col"),
            P("col", "row"),
            P("row", None),
            P(),
            P(),
            P("col", None),
            P("col", None),
        ),
        out_specs=(P("row", "col"), P("col", "row"), P()),
        check_vma=False,
    )
```

```python
import math

import jax
import jax.numpy as jnp
from jax import lax
from jax.experimental import pallas as pl
from jax.experimental.pallas import tpu as pltpu
from jax.sharding import PartitionSpec as P

MESH = pl.DeviceIdType.MESH
F32 = jnp.float32
BF16 = jnp.bfloat16

WIDTH = 6144
GW = 64
GH = 16
TOK = 1024
STRIP = 128
FEAT = 384
HID = 3072
HALF = 1536
OWN = 192
CH = 256
TA = 512
TB = TOK - TA
FOCUS = 0.85
EPS = 1e-06

ROOT_HALF = math.sqrt(0.5)
DENSITY = 1.0 / math.sqrt(2.0 * math.pi)

N_SEMS = 192


def cdf(v):
    return 0.5 * (1.0 + lax.erf(v * ROOT_HALF))


def slope(v):
    return cdf(v) + v * (DENSITY * jnp.exp(-0.5 * v * v))


def tn(a, b):
    return lax.dot_general(a, b, (((0,), (0,)), ((), ())), preferred_element_type=F32)


def nt(a, b):
    return lax.dot_general(a, b, (((1,), (1,)), ((), ())), preferred_element_type=F32)


def mm(a, b):
    return jnp.dot(a, b, preferred_element_type=F32)


def step_kernel(
    tok_hbm, gain_ref, wup_hbm, wdn_hbm, proj_hbm, conv_hbm, head_ref, depth_hbm, mask_hbm,
    up_out, gh_out, loss_ref,
    tok_ref, wup_ref, wdn, proj_ref, conv, depth_ref, mask_ref,
    xall, st_row, st_col, w_t, w_send, wd_peer, proj_peer, n_t, m_sum, m_part, m_recv, m_own,
    p_a, p_b, a1, a2, a3, b1, b2, b3, pre, hid, zc, z1, z1_recv, z2, z2_recv, z3,
    taps, field, field_slope, shifted, pred_all, rows_buf, gz, gm, ga, gb, gh_own, grad, up_own, send_sems, recv_sems, local_sems, out_sems,
):
    row, col = lax.axis_index("row"), lax.axis_index("col")
    z, h, c = row // 4, lax.rem(row // 2, 2), lax.rem(row, 2)
    used = [0]

    def zz(dz):
        return lax.rem(z + dz + 4, 4)

    def hh(dh):
        return lax.rem(h + dh, 2)

    def at_row(dz, dh, dc):
        return {"row": zz(dz) * 4 + hh(dh) * 2 + lax.rem(c + dc, 2)}

    def at_col(dl, dx):
        return {"col": lax.rem(col // 4 + dl, 2) * 4 + lax.rem(lax.rem(col, 4) + dx, 4)}

    def remote(src, dst, device):
        at = used[0]
        used[0] += 1
        copy = pltpu.make_async_remote_copy(
            src_ref=src, dst_ref=dst, send_sem=send_sems.at[at], recv_sem=recv_sems.at[at],
            device_id=device, device_id_type=MESH,
        )
        copy.start()
        sent.append(copy)
        return copy

    def slot(dz, dh):
        return c * 8 + zz(dz) * 2 + hh(dh)

    def own_rows(dz, dh):
        return pl.ds(pl.multiple_of(slot(dz, dh) * OWN, 64), OWN)

    sent = []
    row_peers = [
        (dz, dh, dc) for dz in (2, 1, 3, 0) for dh in (1, 0) for dc in (1, 0) if (dz, dh, dc) != (0, 0, 0)
    ]
    chip_peers = [(dz, dh) for dz in (2, 1, 3, 0) for dh in (1, 0) if (dz, dh) != (0, 0)]
    col_peers = [(dl, dx) for dl in (1, 0) for dx in (2, 1, 3, 0) if (dl, dx) != (0, 0)]
    partner = at_row(0, 0, 1)
    here = z * 2 + h
    other = 1 - c

    barrier = pltpu.get_barrier_semaphore()
    for peer in row_peers:
        pl.semaphore_signal(barrier, inc=1, device_id=at_row(*peer), device_id_type=MESH)
    for peer in col_peers:
        pl.semaphore_signal(barrier, inc=1, device_id=at_col(*peer), device_id_type=MESH)

    started = []

    def local(src, dst):
        copy = pltpu.make_async_copy(src, dst, local_sems.at[len(started)])
        copy.start()
        started.append(copy)
        return copy

    first_channel = pl.multiple_of(c * 128, 128)
    tok_copy = local(tok_hbm, tok_ref)
    proj_in = local(proj_hbm, proj_ref)
    wdn_copy = local(wdn_hbm, wdn)
    wup_copy = local(wup_hbm, wup_ref)
    depth_copy = local(depth_hbm, depth_ref)
    mask_copy = local(mask_hbm, mask_ref)
    conv_copy = local(conv_hbm.at[:, pl.ds(first_channel, 128), :], conv)

    tok_copy.wait()
    x_t = tok_ref[...].astype(F32).T
    xall[col] = x_t.astype(BF16)
    st_row[row] = jnp.concatenate(
        [
            jnp.sum(x_t, 0, keepdims=True),
            jnp.sum(x_t * x_t, 0, keepdims=True),
            jnp.zeros((6, STRIP), F32),
        ],
        axis=0,
    )
    own_half = pl.multiple_of(c * HALF, HALF)
    to_peer = pl.multiple_of(other * HALF, HALF)
    pl.semaphore_wait(barrier, len(row_peers) + len(col_peers))

    stat_copies = [remote(st_row.at[row], st_row.at[row], at_row(*peer)) for peer in row_peers]
    across = remote(xall.at[col], xall.at[col], at_col(1, 0))
    token_copies = [remote(xall.at[col], xall.at[col], at_col(0, dx)) for dx in (2, 1, 3)]
    proj_in.wait()
    wdn_copy.wait()
    wd_copy = remote(wdn.at[pl.ds(to_peer, HALF)], wd_peer, partner)
    proj_copy = remote(proj_ref, proj_peer, partner)

    @pl.loop(0, 8)
    def _(k):
        m_sum[k] = mm(wdn[pl.ds(pl.multiple_of(own_half + k * OWN, 64), OWN), :], proj_ref[...])

    across.wait_recv()
    came = xall.at[lax.rem(col + 4, 8)]
    token_copies += [remote(came, came, at_col(0, dx)) for dx in (2, 1, 3)]

    wd_copy.wait_recv()
    proj_copy.wait_recv()

    @pl.loop(0, 8)
    def _(k):
        more = mm(wd_peer[pl.ds(pl.multiple_of(k * OWN, 64), OWN), :], proj_peer[...])
        m_part[k] = (m_sum[k] + more).astype(BF16)

    m_copies = []
    for index, (dz, dh) in enumerate(chip_peers):
        m_copies.append(
            remote(m_part.at[zz(dz) * 2 + hh(dh)], m_recv.at[index], at_row(dz, dh, 0))
        )

    for copy in stat_copies:
        copy.wait_recv()
    total = st_row[0]
    for index in range(1, 16):
        total = total + st_row[index]
    mean = total[0:1] / WIDTH
    spread = total[1:2] / WIDTH - mean * mean
    depth_copy.wait()
    mask_copy.wait()
    depth = depth_ref[...].astype(F32)
    seen = mask_ref[...].astype(F32)
    st_col[col] = jnp.concatenate(
        [
            mean,
            lax.rsqrt(spread + EPS),
            jnp.concatenate([seen[0:1], seen[1:2]], axis=1),
            jnp.log(jnp.concatenate([depth[0:1], depth[1:2]], axis=1) * 0.001),
            jnp.zeros((4, STRIP), F32),
        ],
        axis=0,
    )
    norm_copies = [remote(st_col.at[col], st_col.at[col], at_col(*peer)) for peer in col_peers]

    feature_at = pl.multiple_of(c * FEAT, 128)
    wup_copy.wait()

    @pl.loop(0, HALF // 128)
    def _(i):
        at = pl.multiple_of(to_peer + i * 128, 128)
        w_send[pl.ds(pl.multiple_of(i * 128, 128), 128), :] = wup_ref[:, pl.ds(at, 128)].T

    w_copy = remote(w_send, w_t.at[:, pl.ds(feature_at, FEAT)], partner)

    @pl.loop(0, HALF // 128)
    def _(i):
        at = pl.multiple_of(own_half + i * 128, 128)
        w_t[pl.ds(pl.multiple_of(i * 128, 128), 128), pl.ds(feature_at, FEAT)] = wup_ref[:, pl.ds(at, 128)].T

    gain = jnp.broadcast_to(gain_ref[...].reshape(1, FEAT), (STRIP, FEAT)).T
    for copy in norm_copies:
        copy.wait_recv()
    for copy in token_copies:
        copy.wait_recv()

    n_copies = []
    for first in (0, 4):
        for index in range(first, first + 4):
            stats = st_col[index]
            n_t[pl.ds(feature_at, FEAT), index * STRIP : (index + 1) * STRIP] = (
                (xall[index].astype(F32) - stats[0:1]) * stats[1:2] * gain
            ).astype(BF16)
        half = n_t.at[pl.ds(feature_at, FEAT), first * STRIP : (first + 4) * STRIP]
        n_copies.append(remote(half, half, partner))
    w_copy.wait_recv()

    a_copies, b_copies = {}, {}

    def project(dz, into, first):
        base = pl.multiple_of(zz(dz) * 2 * OWN, 2 * OWN)

        @pl.loop(0, into.shape[3] // 256)
        def _(t):
            at = pl.multiple_of(t * 256, 256)
            both = mm(
                w_t[pl.ds(base, 2 * OWN), :], n_t[:, pl.ds(pl.multiple_of(first + at, 256), 256)]
            ).astype(BF16)
            into[zz(dz), 0, :, pl.ds(at, 256)] = both[:OWN]
            into[zz(dz), 1, :, pl.ds(at, 256)] = both[OWN:]

    up, down, flip = at_row(1, 0, 0), at_row(3, 0, 0), at_row(0, 1, 0)
    n_copies[0].wait_recv()
    project(2, p_a, 0)
    a_up = remote(p_a.at[zz(2), 0], a1.at[0], up)
    a_down = remote(p_a.at[zz(2), 1], a1.at[1], down)
    n_copies[1].wait_recv()
    for dz in (2, 1, 3, 0):
        project(dz, p_b, TA)
        b_copies[dz] = remote(p_b.at[zz(dz), 1 - h], b1.at[zz(dz)], flip)
    for dz in (1, 3, 0):
        project(dz, p_a, 0)

    def add(into, more):
        into[...] = (into[...].astype(F32) + more[...].astype(F32)).astype(BF16)

    a_up.wait_recv()
    add(p_a.at[zz(1), 0], a1.at[0])
    a_up2 = remote(p_a.at[zz(1)], a2.at[0], up)
    a_down.wait_recv()
    add(p_a.at[zz(3), 1], a1.at[1])
    a_down2 = remote(p_a.at[zz(3)], a2.at[1], down)

    b_copies[2].wait_recv()
    add(p_b.at[zz(2), h], b1.at[zz(2)])
    b_up = remote(p_b.at[zz(2), h, 0:96], b2.at[0], up)
    b_down = remote(p_b.at[zz(2), h, 96:192], b2.at[1], down)
    b_copies[1].wait_recv()
    add(p_b.at[zz(1), h], b1.at[zz(1)])
    b_copies[3].wait_recv()
    add(p_b.at[zz(3), h], b1.at[zz(3)])

    a_up2.wait_recv()
    a_down2.wait_recv()
    p_a[z, 1 - h] = (
        p_a[z, 1 - h].astype(F32) + a2[0, 1 - h].astype(F32) + a2[1, 1 - h].astype(F32)
    ).astype(BF16)
    a_flip = remote(p_a.at[z, 1 - h], a3, flip)

    b_up.wait_recv()
    add(p_b.at[zz(1), h, 0:96], b2.at[0])
    b_up2 = remote(p_b.at[zz(1), h], b3.at[0], up)
    b_down.wait_recv()
    add(p_b.at[zz(3), h, 96:192], b2.at[1])
    b_down2 = remote(p_b.at[zz(3), h], b3.at[1], down)

    for copy in m_copies:
        copy.wait_recv()
    total = m_part[here].astype(F32)
    for index in range(7):
        total = total + m_recv[index].astype(F32)
    m_own[...] = total.astype(BF16)
    gm[slot(0, 0)] = m_own[...]
    pair = {}

    def send(buf, dz, dh, device, rows=None):
        ref = buf.at[slot(dz, dh)] if rows is None else buf.at[slot(dz, dh), rows[0] : rows[1]]
        return remote(ref, ref, device)

    def share(name, buf, dz, dh, rows=None):
        pair[name] = send(buf, dz, dh, partner, rows)

    mf = send(gm, 0, 0, flip)
    mu = send(gm, 0, 0, up)
    md = send(gm, 0, 0, down)
    share("gm00", gm, 0, 0)
    x_proj = tn(proj_ref[...], xall[col])

    conv_copy.wait()
    head = head_ref[...]
    for k in range(9):
        taps[k] = jnp.broadcast_to(
            jnp.sum(conv[k].astype(F32) * head, axis=1, keepdims=True), (128, 128)
        )
    lane = lax.broadcasted_iota(jnp.int32, (128, CH), 1)
    sub = lax.broadcasted_iota(jnp.int32, (128, CH), 0)
    taps[9] = jnp.broadcast_to(
        jnp.sum(jnp.where(lane == sub + first_channel, head, 0.0), axis=1, keepdims=True), (128, 128)
    )

    b_copies[0].wait_recv()
    a_flip.wait_recv()
    pre[:, :TA] = (
        p_a[z, h].astype(F32) + a2[0, h].astype(F32) + a2[1, h].astype(F32) + a3[...].astype(F32)
    )
    b_up2.wait_recv()
    b_down2.wait_recv()
    pre[:, TA:] = (
        p_b[z, h].astype(F32) + b1[z].astype(F32) + b3[0].astype(F32) + b3[1].astype(F32)
    )

    @pl.loop(0, TOK // 128)
    def _(t):
        at = pl.ds(pl.multiple_of(t * 128, 128), 128)
        value = pre[:, at]
        hid[:, at] = (value * cdf(value)).astype(BF16)

    @pl.loop(0, TOK // 256)
    def _(t):
        at = pl.ds(pl.multiple_of(t * 256, 256), 256)
        zc[:, at] = tn(m_own[...], hid[:, at])

    strip = pl.ds(pl.multiple_of(col * STRIP, STRIP), STRIP)
    zc[:, strip] = zc[:, strip] + x_proj

    z1[...] = zc[pl.ds(pl.multiple_of(other * 128, 128), 128), :].astype(BF16)
    z1_copy = remote(z1, z1_recv, partner)

    mine_a, mine_b = ga.at[slot(0, 0)], gb.at[slot(0, 0)]
    mf.wait_recv()
    mfu = send(gm, 0, 1, up)
    mfd = send(gm, 0, 1, down)
    share("gm01", gm, 0, 1)
    top, low = (0, 96), (96, 192)

    @pl.loop(0, TB // 128)
    def _(t):
        at = pl.ds(pl.multiple_of(t * 128, 128), 128)
        mine_b[:, at] = slope(pre[:, pl.ds(pl.multiple_of(TA + t * 128, 128), 128)]).astype(BF16)

    z1_copy.wait_recv()
    z2[...] = (
        zc[pl.ds(pl.multiple_of(c * 128, 128), 128), :] + z1_recv[...].astype(F32)
    ).astype(BF16)
    z2_copies = []
    for index, (dz, dh) in enumerate(chip_peers):
        at = pl.multiple_of((zz(dz) * 2 + hh(dh)) * 16, 16)
        z2_copies.append(remote(z2.at[pl.ds(at, 16)], z2_recv.at[index], at_row(dz, dh, 0)))
    bu = send(gb, 0, 0, up)
    bd = send(gb, 0, 0, down)
    mu.wait_recv()
    mu2 = send(gm, 3, 0, up)
    share("gm30", gm, 3, 0)
    md.wait_recv()
    share("gm10", gm, 1, 0)
    share("gb00", gb, 0, 0)

    @pl.loop(0, TA // 128)
    def _(t):
        at = pl.ds(pl.multiple_of(t * 128, 128), 128)
        mine_a[:, at] = slope(pre[:, at]).astype(BF16)

    fa = send(ga, 0, 0, flip)
    mfd.wait_recv()
    mfd2 = send(gm, 1, 1, down)
    share("gm11", gm, 1, 1)
    mfu.wait_recv()
    share("gm31", gm, 3, 1)
    share("ga00", ga, 0, 0)
    mine = pl.ds(pl.multiple_of(here * 16, 16), 16)
    part = z2[mine, :].astype(F32)
    for index, copy in enumerate(z2_copies):
        copy.wait_recv()
        part = part + z2_recv[index].astype(F32)
    z3[col] = part.astype(BF16)
    z3_copies = [remote(z3.at[col], z3.at[col], at_col(*peer)) for peer in col_peers]
    au = send(ga, 0, 0, up)
    ad = send(ga, 0, 0, down)
    fb = send(gb, 0, 0, flip)
    bu.wait_recv()
    bu2 = send(gb, 3, 0, up, top)
    share("gb30", gb, 3, 0)
    bd.wait_recv()
    bd2 = send(gb, 1, 0, down, low)
    share("gb10", gb, 1, 0)
    for copy in z3_copies:
        copy.wait_recv()
    total = z3[0].astype(F32)
    for index in range(1, 8):
        total = total + z3[index].astype(F32)
    field[mine, :] = total.astype(BF16)
    z4_copies = [
        remote(field.at[mine], field.at[mine], at_row(dz, dh, 0)) for dz, dh in chip_peers
    ]
    f_m = send(gb, 3, 0, flip)
    f_p = send(gb, 1, 0, flip)
    fa.wait_recv()
    fau = send(ga, 0, 1, up)
    fad = send(ga, 0, 1, down)
    share("ga01", ga, 0, 1)
    au.wait_recv()
    au2 = send(ga, 3, 0, up)
    share("ga30", ga, 3, 0)
    ad.wait_recv()
    share("ga10", ga, 1, 0)
    fb.wait_recv()
    share("gb01", gb, 0, 1)
    bu2.wait_recv()
    f_top = send(gb, 2, 0, flip, top)
    share("gb20top", gb, 2, 0, top)
    bd2.wait_recv()
    f_low = send(gb, 2, 0, flip, low)
    share("gb20low", gb, 2, 0, low)
    mu2.wait_recv()
    share("gm20", gm, 2, 0)
    mfd2.wait_recv()
    share("gm21", gm, 2, 1)
    for copy in z4_copies:
        copy.wait_recv()

    token = lax.broadcasted_iota(jnp.int32, (1, TOK), 1)
    line, place = token >> 6, token & (GW - 1)

    def moved(values, di, dj):
        shift = di * GW + dj
        if shift:
            values = pltpu.roll(values, (-shift) % TOK, 1)
        inside = (
            (line + di >= 0) & (line + di < GH) & (place + dj >= 0) & (place + dj < GW)
        )
        return jnp.where(inside, values, 0.0)

    @pl.loop(0, TOK // 128)
    def _(t):
        at = pl.ds(pl.multiple_of(t * 128, 128), 128)
        value = field[:, at].astype(F32)
        act = (value * cdf(value)).astype(BF16).astype(F32)
        for k in range(9):
            shifted[k : k + 1, at] = jnp.sum(act * taps[k], axis=0, keepdims=True)
        shifted[9:10, at] = jnp.sum(value * taps[9], axis=0, keepdims=True)

    pred = shifted[9:10, :]
    for k in range(9):
        pred = pred + moved(shifted[k : k + 1, :], k // 3 - 1, k % 3 - 1)
    for index in range(8):
        rows_buf[index : index + 1, :] = pred[:, index * STRIP : (index + 1) * STRIP]
    pred_all[c] = rows_buf[...]
    pred_copy = remote(pred_all.at[c], pred_all.at[c], partner)

    @pl.loop(0, TOK // 128)
    def _(t):
        at = pl.ds(pl.multiple_of(t * 128, 128), 128)
        field_slope[:, at] = slope(field[:, at].astype(F32))

    valid = jnp.concatenate([st_col[index][2:3] for index in range(8)], axis=0)
    target = jnp.concatenate([st_col[index][3:4] for index in range(8)], axis=0)
    pred_copy.wait_recv()
    err = valid * (pred_all[0] + pred_all[1] - target)

    def whole(values):
        return jnp.sum(jnp.sum(values, axis=1, keepdims=True), axis=0, keepdims=True)

    count = whole(valid)
    mean_err = whole(err) / count
    loss_ref[0, 0] = jnp.sum(whole(err * err) / count - FOCUS * mean_err * mean_err)
    grad_pred = valid * (2.0 * err - 2.0 * FOCUS * mean_err)
    grad_pred = jnp.concatenate([grad_pred[index : index + 1] for index in range(8)], axis=1)
    for k in range(9):
        shifted[k : k + 1, :] = moved(grad_pred, 1 - k // 3, 1 - k % 3)
    shifted[9:10, :] = grad_pred

    @pl.loop(0, TOK // 128)
    def _(t):
        at = pl.ds(pl.multiple_of(t * 128, 128), 128)
        back = taps[0] * shifted[0:1, at]
        for k in range(1, 9):
            back = back + taps[k] * shifted[k : k + 1, at]
        gz[pl.ds(first_channel, 128), at] = (
            taps[9] * shifted[9:10, at] + field_slope[:, at] * back
        ).astype(BF16)

    half_z = gz.at[pl.ds(first_channel, 128)]
    gz_copy = remote(half_z, half_z, partner)

    second_channel = pl.multiple_of(other * 128, 128)
    gh_own[:, pl.ds(first_channel, 128)] = nt(hid[...], half_z[...]).astype(BF16)
    gz_copy.wait_recv()
    gh_own[:, pl.ds(second_channel, 128)] = nt(
        hid[...], gz[pl.ds(second_channel, 128), :]
    ).astype(BF16)
    local(gh_own, gh_out.at[own_rows(0, 0)])
    gh_copies = [
        remote(gh_own, gh_out.at[own_rows(0, 0)], at_row(dz, dh, 0)) for dz, dh in chip_peers
    ]
    gh_pair = [remote(gh_own, gh_out.at[own_rows(0, 0)], partner)]
    def ready(names):
        for name in names.split():
            pair[name].wait_recv()

    n_mine = n_t.at[pl.ds(feature_at, FEAT)]

    def column(dz):
        @pl.loop(0, 2)
        def _(core):
            base = core * 8 + zz(dz) * 2
            for half in (0, 1):
                rows = slice(half * OWN, (half + 1) * OWN)
                weights = gm[base + half]
                grad[rows, :TA] = (
                    mm(weights, gz[:, :TA]) * ga[base + half].astype(F32)
                ).astype(BF16)
                grad[rows, TA:] = (
                    mm(weights, gz[:, TA:]) * gb[base + half].astype(F32)
                ).astype(BF16)
            up_own[dz, core] = nt(n_mine[...], grad[...])
            at = pl.multiple_of(base * OWN, 2 * OWN)
            pltpu.make_async_copy(
                up_own.at[dz, core], up_out.at[:, pl.ds(at, 2 * OWN)], out_sems.at[dz, core]
            ).start()

    fad.wait_recv()
    fad2 = send(ga, 1, 1, down)
    share("ga11", ga, 1, 1)
    fau.wait_recv()
    share("ga31", ga, 3, 1)
    f_m.wait_recv()
    share("gb31", gb, 3, 1)
    f_p.wait_recv()
    share("gb11", gb, 1, 1)
    ready("gm00 gb00 ga00 gm01 ga01 gb01")
    column(0)
    f_top.wait_recv()
    share("gb21top", gb, 2, 1, top)
    f_low.wait_recv()
    share("gb21low", gb, 2, 1, low)
    ready("gm30 gb30 ga30 gm31 ga31 gb31")
    column(3)
    au2.wait_recv()
    share("ga20", ga, 2, 0)
    ready("gm10 gb10 ga10 gm11 ga11 gb11")
    column(1)
    fad2.wait_recv()
    share("ga21", ga, 2, 1)
    ready("gm20 gb20top gb20low ga20 gm21 ga21 gb21top gb21low")
    column(2)

    for (dz, dh), copy in zip(chip_peers, gh_copies):
        copy.wait_recv()
        came = gh_out.at[own_rows(-dz, dh)]
        gh_pair.append(remote(came, came, partner))
    for copy in gh_pair:
        copy.wait_recv()

    for dz in range(4):

        @pl.loop(0, 2)
        def _(core):
            at = pl.multiple_of((core * 8 + zz(dz) * 2) * OWN, 2 * OWN)
            pltpu.make_async_copy(
                up_own.at[dz, core], up_out.at[:, pl.ds(at, 2 * OWN)], out_sems.at[dz, core]
            ).wait()

    started[-1].wait()
    for copy in sent:
        copy.wait_send()


def weight_kernel(gh_ref, proj_ref, down_ref):
    down_ref[...] = nt(gh_ref[...], proj_ref[...])


def on_device(tokens, ln_gain, w_up, w_down, proj, conv_kernel, head_weight, depth_mm, lidar_mask):
    vmem = pl.BlockSpec(memory_space=pltpu.VMEM)
    anywhere = pl.BlockSpec(memory_space=pl.ANY)
    grad_up, grad_hidden, loss = pl.pallas_call(
        step_kernel,
        name="mlp_step",
        out_shape=[
            jax.ShapeDtypeStruct((FEAT, HID), F32),
            jax.ShapeDtypeStruct((HID, CH), BF16),
            jax.ShapeDtypeStruct((1, 1), F32),
        ],
        in_specs=[
            anywhere, vmem, anywhere, anywhere, anywhere, anywhere, vmem, anywhere, anywhere,
        ],
        out_specs=[anywhere, anywhere, pl.BlockSpec(memory_space=pltpu.SMEM)],
        scratch_shapes=[
            pltpu.VMEM((STRIP, FEAT), BF16),
            pltpu.VMEM((FEAT, HID), BF16),
            pltpu.VMEM((HID, FEAT), BF16),
            pltpu.VMEM((FEAT, CH), BF16),
            pltpu.VMEM((9, 128, CH), BF16),
            pltpu.VMEM((2, GW), jnp.int32),
            pltpu.VMEM((2, GW), jnp.int32),
            pltpu.VMEM((8, FEAT, STRIP), BF16),
            pltpu.VMEM((16, 8, STRIP), F32),
            pltpu.VMEM((8, 8, STRIP), F32),
            pltpu.VMEM((HALF, 2 * FEAT), BF16),
            pltpu.VMEM((HALF, FEAT), BF16),
            pltpu.VMEM((HALF, FEAT), BF16),
            pltpu.VMEM((FEAT, CH), BF16),
            pltpu.VMEM((2 * FEAT, TOK), BF16),
            pltpu.VMEM((8, OWN, CH), F32),
            pltpu.VMEM((8, OWN, CH), BF16),
            pltpu.VMEM((7, OWN, CH), BF16),
            pltpu.VMEM((OWN, CH), BF16),
            pltpu.VMEM((4, 2, OWN, TA), BF16),
            pltpu.VMEM((4, 2, OWN, TB), BF16),
            pltpu.VMEM((2, OWN, TA), BF16),
            pltpu.VMEM((2, 2, OWN, TA), BF16),
            pltpu.VMEM((OWN, TA), BF16),
            pltpu.VMEM((4, OWN, TB), BF16),
            pltpu.VMEM((2, OWN // 2, TB), BF16),
            pltpu.VMEM((2, OWN, TB), BF16),
            pltpu.VMEM((OWN, TOK), F32),
            pltpu.VMEM((OWN, TOK), BF16),
            pltpu.VMEM((CH, TOK), F32),
            pltpu.VMEM((128, TOK), BF16),
            pltpu.VMEM((128, TOK), BF16),
            pltpu.VMEM((128, TOK), BF16),
            pltpu.VMEM((7, 16, TOK), BF16),
            pltpu.VMEM((8, 16, TOK), BF16),
            pltpu.VMEM((10, 128, 128), F32),
            pltpu.VMEM((128, TOK), BF16),
            pltpu.VMEM((128, TOK), F32),
            pltpu.VMEM((16, TOK), F32),
            pltpu.VMEM((2, 8, STRIP), F32),
            pltpu.VMEM((8, STRIP), F32),
            pltpu.VMEM((CH, TOK), BF16),
            pltpu.VMEM((16, OWN, CH), BF16),
            pltpu.VMEM((16, OWN, TA), BF16),
            pltpu.VMEM((16, OWN, TB), BF16),
            pltpu.VMEM((OWN, CH), BF16),
            pltpu.VMEM((2 * OWN, TOK), BF16),
            pltpu.VMEM((4, 2, FEAT, 2 * OWN), F32),
            pltpu.SemaphoreType.DMA((N_SEMS,)),
            pltpu.SemaphoreType.DMA((N_SEMS,)),
            pltpu.SemaphoreType.DMA((9,)),
            pltpu.SemaphoreType.DMA((4, 2)),
        ],
        compiler_params=pltpu.CompilerParams(
            collective_id=0, has_side_effects=True, vmem_limit_bytes=60 * 2**20
        ),
        cost_estimate=pl.CostEstimate(flops=6 * 10**9, bytes_accessed=16 * 2**20, transcendentals=10**6),
    )(
        tokens, ln_gain, w_up, w_down, proj, conv_kernel.reshape(9, CH, CH),
        head_weight.reshape(1, CH), depth_mm, lidar_mask,
    )
    grad_down = pl.pallas_call(
        weight_kernel,
        name="weight_grads",
        grid=(HID // 512,),
        out_shape=jax.ShapeDtypeStruct((HID, FEAT), F32),
        in_specs=[
            pl.BlockSpec((512, CH), lambda j: (j, 0)),
            pl.BlockSpec((FEAT, CH), lambda j: (0, 0)),
        ],
        out_specs=pl.BlockSpec((512, FEAT), lambda j: (j, 0)),
        compiler_params=pltpu.CompilerParams(vmem_limit_bytes=60 * 2**20),
        cost_estimate=pl.CostEstimate(flops=6 * 10**8, bytes_accessed=6 * 2**20, transcendentals=0),
    )(grad_hidden, proj)
    return (grad_up, grad_down, loss.reshape(()))


def solution(mesh):
    return jax.shard_map(
        on_device,
        mesh=mesh,
        in_specs=(
            P("col", "row"),
            P("row"),
            P("row", "col"),
            P("col", "row"),
            P("row", None),
            P(),
            P(),
            P("col", None),
            P("col", None),
        ),
        out_specs=(P("row", "col"), P("col", "row"), P()),
        check_vma=False,
    )
```

```python
import math

import jax
import jax.numpy as jnp
from jax import lax
from jax.experimental import pallas as pl
from jax.experimental.pallas import tpu as pltpu
from jax.sharding import PartitionSpec as P

MESH = pl.DeviceIdType.MESH
F32 = jnp.float32
BF16 = jnp.bfloat16

WIDTH = 6144
GW = 64
GH = 16
TOK = 1024
STRIP = 128
FEAT = 384
HID = 3072
HALF = 1536
OWN = 192
CH = 256
TA = 512
TB = TOK - TA
FOCUS = 0.85
EPS = 1e-06

ROOT_HALF = math.sqrt(0.5)
DENSITY = 1.0 / math.sqrt(2.0 * math.pi)

N_SEMS = 192
N_DOWN = 6
N_UP = 8


def cdf(v):
    return 0.5 * (1.0 + lax.erf(v * ROOT_HALF))


def slope(v):
    return cdf(v) + v * (DENSITY * jnp.exp(-0.5 * v * v))


def tn(a, b):
    return lax.dot_general(a, b, (((0,), (0,)), ((), ())), preferred_element_type=F32)


def nt(a, b):
    return lax.dot_general(a, b, (((1,), (1,)), ((), ())), preferred_element_type=F32)


def mm(a, b):
    return jnp.dot(a, b, preferred_element_type=F32)


def step_kernel(
    tok_hbm, gain_ref, wup_hbm, wdn_hbm, proj_hbm, conv_hbm, head_ref, depth_hbm, mask_hbm,
    up_out, gh_out, loss_ref,
    tok_ref, wup_ref, wdn, proj_ref, conv, depth_ref, mask_ref,
    xall, st_row, st_col, w_t, w_send, wd_peer, proj_peer, n_t, m_sum, m_part, m_recv, m_own,
    p_a, p_b, a1, a2, a3, b1, b2, b3, pre, hid, zc, z1, z1_recv, z2, z2_recv, z3,
    taps, field, field_slope, shifted, pred_all, rows_buf, gz, gm, ga, gb, gh_own, grad, up_own, send_sems, recv_sems, local_sems, out_sems,
):
    row, col = lax.axis_index("row"), lax.axis_index("col")
    z, h, c = row // 4, lax.rem(row // 2, 2), lax.rem(row, 2)
    used = [0]

    def zz(dz):
        return lax.rem(z + dz + 4, 4)

    def hh(dh):
        return lax.rem(h + dh, 2)

    def at_row(dz, dh, dc):
        return {"row": zz(dz) * 4 + hh(dh) * 2 + lax.rem(c + dc, 2)}

    def at_col(dl, dx):
        return {"col": lax.rem(col // 4 + dl, 2) * 4 + lax.rem(lax.rem(col, 4) + dx, 4)}

    def remote(src, dst, device):
        at = used[0]
        used[0] += 1
        copy = pltpu.make_async_remote_copy(
            src_ref=src, dst_ref=dst, send_sem=send_sems.at[at], recv_sem=recv_sems.at[at],
            device_id=device, device_id_type=MESH,
        )
        copy.start()
        sent.append(copy)
        return copy

    def slot(dz, dh):
        return c * 8 + zz(dz) * 2 + hh(dh)

    def own_rows(dz, dh):
        return pl.ds(pl.multiple_of(slot(dz, dh) * OWN, 64), OWN)

    sent = []
    row_peers = [
        (dz, dh, dc) for dz in (2, 1, 3, 0) for dh in (1, 0) for dc in (1, 0) if (dz, dh, dc) != (0, 0, 0)
    ]
    chip_peers = [(dz, dh) for dz in (2, 1, 3, 0) for dh in (1, 0) if (dz, dh) != (0, 0)]
    col_peers = [(dl, dx) for dl in (1, 0) for dx in (2, 1, 3, 0) if (dl, dx) != (0, 0)]
    partner = at_row(0, 0, 1)
    here = z * 2 + h
    other = 1 - c

    barrier = pltpu.get_barrier_semaphore()
    for peer in row_peers:
        pl.semaphore_signal(barrier, inc=1, device_id=at_row(*peer), device_id_type=MESH)
    for peer in col_peers:
        pl.semaphore_signal(barrier, inc=1, device_id=at_col(*peer), device_id_type=MESH)

    started = []

    def local(src, dst):
        copy = pltpu.make_async_copy(src, dst, local_sems.at[len(started)])
        copy.start()
        started.append(copy)
        return copy

    first_channel = pl.multiple_of(c * 128, 128)
    tok_copy = local(tok_hbm, tok_ref)
    proj_in = local(proj_hbm, proj_ref)
    wdn_copy = local(wdn_hbm, wdn)
    wup_copy = local(wup_hbm, wup_ref)
    depth_copy = local(depth_hbm, depth_ref)
    mask_copy = local(mask_hbm, mask_ref)
    conv_copy = local(conv_hbm.at[:, pl.ds(first_channel, 128), :], conv)

    tok_copy.wait()
    x_t = tok_ref[...].astype(F32).T
    xall[col] = x_t.astype(BF16)
    st_row[row] = jnp.concatenate(
        [
            jnp.sum(x_t, 0, keepdims=True),
            jnp.sum(x_t * x_t, 0, keepdims=True),
            jnp.zeros((6, STRIP), F32),
        ],
        axis=0,
    )
    own_half = pl.multiple_of(c * HALF, HALF)
    to_peer = pl.multiple_of(other * HALF, HALF)
    pl.semaphore_wait(barrier, len(row_peers) + len(col_peers))

    stat_copies = [remote(st_row.at[row], st_row.at[row], at_row(*peer)) for peer in row_peers]
    across = remote(xall.at[col], xall.at[col], at_col(1, 0))
    token_copies = [remote(xall.at[col], xall.at[col], at_col(0, dx)) for dx in (2, 1, 3)]
    proj_in.wait()
    wdn_copy.wait()
    wd_copy = remote(wdn.at[pl.ds(to_peer, HALF)], wd_peer, partner)
    proj_copy = remote(proj_ref, proj_peer, partner)

    @pl.loop(0, 8)
    def _(k):
        m_sum[k] = mm(wdn[pl.ds(pl.multiple_of(own_half + k * OWN, 64), OWN), :], proj_ref[...])

    across.wait_recv()
    came = xall.at[lax.rem(col + 4, 8)]
    token_copies += [remote(came, came, at_col(0, dx)) for dx in (2, 1, 3)]

    wd_copy.wait_recv()
    proj_copy.wait_recv()

    @pl.loop(0, 8)
    def _(k):
        more = mm(wd_peer[pl.ds(pl.multiple_of(k * OWN, 64), OWN), :], proj_peer[...])
        m_part[k] = (m_sum[k] + more).astype(BF16)

    m_copies = []
    for index, (dz, dh) in enumerate(chip_peers):
        m_copies.append(
            remote(m_part.at[zz(dz) * 2 + hh(dh)], m_recv.at[index], at_row(dz, dh, 0))
        )

    for copy in stat_copies:
        copy.wait_recv()
    total = st_row[0]
    for index in range(1, 16):
        total = total + st_row[index]
    mean = total[0:1] / WIDTH
    spread = total[1:2] / WIDTH - mean * mean
    depth_copy.wait()
    mask_copy.wait()
    depth = depth_ref[...].astype(F32)
    seen = mask_ref[...].astype(F32)
    st_col[col] = jnp.concatenate(
        [
            mean,
            lax.rsqrt(spread + EPS),
            jnp.concatenate([seen[0:1], seen[1:2]], axis=1),
            jnp.log(jnp.concatenate([depth[0:1], depth[1:2]], axis=1) * 0.001),
            jnp.zeros((4, STRIP), F32),
        ],
        axis=0,
    )
    norm_copies = [remote(st_col.at[col], st_col.at[col], at_col(*peer)) for peer in col_peers]

    feature_at = pl.multiple_of(c * FEAT, 128)
    wup_copy.wait()

    @pl.loop(0, HALF // 128)
    def _(i):
        at = pl.multiple_of(to_peer + i * 128, 128)
        w_send[pl.ds(pl.multiple_of(i * 128, 128), 128), :] = wup_ref[:, pl.ds(at, 128)].T

    w_copy = remote(w_send, w_t.at[:, pl.ds(feature_at, FEAT)], partner)

    @pl.loop(0, HALF // 128)
    def _(i):
        at = pl.multiple_of(own_half + i * 128, 128)
        w_t[pl.ds(pl.multiple_of(i * 128, 128), 128), pl.ds(feature_at, FEAT)] = wup_ref[:, pl.ds(at, 128)].T

    gain = jnp.broadcast_to(gain_ref[...].reshape(1, FEAT), (STRIP, FEAT)).T
    for copy in norm_copies:
        copy.wait_recv()
    for copy in token_copies:
        copy.wait_recv()

    n_copies = []
    for first in (0, 4):
        for index in range(first, first + 4):
            stats = st_col[index]
            n_t[pl.ds(feature_at, FEAT), index * STRIP : (index + 1) * STRIP] = (
                (xall[index].astype(F32) - stats[0:1]) * stats[1:2] * gain
            ).astype(BF16)
        half = n_t.at[pl.ds(feature_at, FEAT), first * STRIP : (first + 4) * STRIP]
        n_copies.append(remote(half, half, partner))
    w_copy.wait_recv()

    a_copies, b_copies = {}, {}

    def project(dz, into, first):
        base = pl.multiple_of(zz(dz) * 2 * OWN, 2 * OWN)

        @pl.loop(0, into.shape[3] // 256)
        def _(t):
            at = pl.multiple_of(t * 256, 256)
            both = mm(
                w_t[pl.ds(base, 2 * OWN), :], n_t[:, pl.ds(pl.multiple_of(first + at, 256), 256)]
            ).astype(BF16)
            into[zz(dz), 0, :, pl.ds(at, 256)] = both[:OWN]
            into[zz(dz), 1, :, pl.ds(at, 256)] = both[OWN:]

    up, down, flip = at_row(1, 0, 0), at_row(3, 0, 0), at_row(0, 1, 0)
    n_copies[0].wait_recv()
    project(2, p_a, 0)
    a_up = remote(p_a.at[zz(2), 0], a1.at[0], up)
    a_down = remote(p_a.at[zz(2), 1], a1.at[1], down)
    n_copies[1].wait_recv()
    for dz in (2, 1, 3, 0):
        project(dz, p_b, TA)
        b_copies[dz] = remote(p_b.at[zz(dz), 1 - h], b1.at[zz(dz)], flip)
    for dz in (1, 3, 0):
        project(dz, p_a, 0)

    def add(into, more):
        into[...] = (into[...].astype(F32) + more[...].astype(F32)).astype(BF16)

    a_up.wait_recv()
    add(p_a.at[zz(1), 0], a1.at[0])
    a_up2 = remote(p_a.at[zz(1)], a2.at[0], up)
    a_down.wait_recv()
    add(p_a.at[zz(3), 1], a1.at[1])
    a_down2 = remote(p_a.at[zz(3)], a2.at[1], down)

    b_copies[2].wait_recv()
    add(p_b.at[zz(2), h], b1.at[zz(2)])
    b_up = remote(p_b.at[zz(2), h, 0:96], b2.at[0], up)
    b_down = remote(p_b.at[zz(2), h, 96:192], b2.at[1], down)
    b_copies[1].wait_recv()
    add(p_b.at[zz(1), h], b1.at[zz(1)])
    b_copies[3].wait_recv()
    add(p_b.at[zz(3), h], b1.at[zz(3)])

    a_up2.wait_recv()
    a_down2.wait_recv()
    p_a[z, 1 - h] = (
        p_a[z, 1 - h].astype(F32) + a2[0, 1 - h].astype(F32) + a2[1, 1 - h].astype(F32)
    ).astype(BF16)
    a_flip = remote(p_a.at[z, 1 - h], a3, flip)

    b_up.wait_recv()
    add(p_b.at[zz(1), h, 0:96], b2.at[0])
    b_up2 = remote(p_b.at[zz(1), h], b3.at[0], up)
    b_down.wait_recv()
    add(p_b.at[zz(3), h, 96:192], b2.at[1])
    b_down2 = remote(p_b.at[zz(3), h], b3.at[1], down)

    for copy in m_copies:
        copy.wait_recv()
    total = m_part[here].astype(F32)
    for index in range(7):
        total = total + m_recv[index].astype(F32)
    m_own[...] = total.astype(BF16)
    gm[slot(0, 0)] = m_own[...]
    pair = {}

    def send(buf, dz, dh, device, rows=None):
        ref = buf.at[slot(dz, dh)] if rows is None else buf.at[slot(dz, dh), rows[0] : rows[1]]
        return remote(ref, ref, device)

    def share(name, buf, dz, dh, rows=None):
        pair[name] = send(buf, dz, dh, partner, rows)

    mf = send(gm, 0, 0, flip)
    mu = send(gm, 0, 0, up)
    md = send(gm, 0, 0, down)
    share(("gm", 0, 0, ""), gm, 0, 0)
    x_proj = tn(proj_ref[...], xall[col])

    conv_copy.wait()
    head = head_ref[...]
    for k in range(9):
        taps[k] = jnp.broadcast_to(
            jnp.sum(conv[k].astype(F32) * head, axis=1, keepdims=True), (128, 128)
        )
    lane = lax.broadcasted_iota(jnp.int32, (128, CH), 1)
    sub = lax.broadcasted_iota(jnp.int32, (128, CH), 0)
    taps[9] = jnp.broadcast_to(
        jnp.sum(jnp.where(lane == sub + first_channel, head, 0.0), axis=1, keepdims=True), (128, 128)
    )

    b_copies[0].wait_recv()
    a_flip.wait_recv()
    pre[:, :TA] = (
        p_a[z, h].astype(F32) + a2[0, h].astype(F32) + a2[1, h].astype(F32) + a3[...].astype(F32)
    )
    b_up2.wait_recv()
    b_down2.wait_recv()
    pre[:, TA:] = (
        p_b[z, h].astype(F32) + b1[z].astype(F32) + b3[0].astype(F32) + b3[1].astype(F32)
    )

    @pl.loop(0, TOK // 128)
    def _(t):
        at = pl.ds(pl.multiple_of(t * 128, 128), 128)
        value = pre[:, at]
        hid[:, at] = (value * cdf(value)).astype(BF16)

    @pl.loop(0, TOK // 256)
    def _(t):
        at = pl.ds(pl.multiple_of(t * 256, 256), 256)
        zc[:, at] = tn(m_own[...], hid[:, at])

    strip = pl.ds(pl.multiple_of(col * STRIP, STRIP), STRIP)
    zc[:, strip] = zc[:, strip] + x_proj

    z1[...] = zc[pl.ds(pl.multiple_of(other * 128, 128), 128), :].astype(BF16)
    z1_copy = remote(z1, z1_recv, partner)

    mine_a, mine_b = ga.at[slot(0, 0)], gb.at[slot(0, 0)]
    mf.wait_recv()
    mfu = send(gm, 0, 1, up)
    mfd = send(gm, 0, 1, down)
    share(("gm", 0, 1, ""), gm, 0, 1)
    top, low = (0, 96), (96, 192)

    @pl.loop(0, TB // 128)
    def _(t):
        at = pl.ds(pl.multiple_of(t * 128, 128), 128)
        mine_b[:, at] = slope(pre[:, pl.ds(pl.multiple_of(TA + t * 128, 128), 128)]).astype(BF16)

    z1_copy.wait_recv()
    z2[...] = (
        zc[pl.ds(pl.multiple_of(c * 128, 128), 128), :] + z1_recv[...].astype(F32)
    ).astype(BF16)
    z2_copies = []
    for index, (dz, dh) in enumerate(chip_peers):
        at = pl.multiple_of((zz(dz) * 2 + hh(dh)) * 16, 16)
        z2_copies.append(remote(z2.at[pl.ds(at, 16)], z2_recv.at[index], at_row(dz, dh, 0)))
    bu = send(gb, 0, 0, up)
    bd = send(gb, 0, 0, down)
    mu.wait_recv()
    mu2 = send(gm, 3, 0, up)
    share(("gm", 3, 0, ""), gm, 3, 0)
    md.wait_recv()
    share(("gm", 1, 0, ""), gm, 1, 0)
    share(("gb", 0, 0, ""), gb, 0, 0)

    @pl.loop(0, TA // 128)
    def _(t):
        at = pl.ds(pl.multiple_of(t * 128, 128), 128)
        mine_a[:, at] = slope(pre[:, at]).astype(BF16)

    fa = send(ga, 0, 0, flip)
    mfd.wait_recv()
    mfd2 = send(gm, 1, 1, down)
    share(("gm", 1, 1, ""), gm, 1, 1)
    mfu.wait_recv()
    share(("gm", 3, 1, ""), gm, 3, 1)
    share(("ga", 0, 0, ""), ga, 0, 0)
    mine = pl.ds(pl.multiple_of(here * 16, 16), 16)
    part = z2[mine, :].astype(F32)
    for index, copy in enumerate(z2_copies):
        copy.wait_recv()
        part = part + z2_recv[index].astype(F32)
    z3[col] = part.astype(BF16)
    z3_copies = [remote(z3.at[col], z3.at[col], at_col(*peer)) for peer in col_peers]
    au = send(ga, 0, 0, up)
    ad = send(ga, 0, 0, down)
    fb = send(gb, 0, 0, flip)
    bu.wait_recv()
    bu2 = send(gb, 3, 0, up, top)
    share(("gb", 3, 0, ""), gb, 3, 0)
    bd.wait_recv()
    bd2 = send(gb, 1, 0, down, low)
    share(("gb", 1, 0, ""), gb, 1, 0)
    for copy in z3_copies:
        copy.wait_recv()
    total = z3[0].astype(F32)
    for index in range(1, 8):
        total = total + z3[index].astype(F32)
    field[mine, :] = total.astype(BF16)
    z4_copies = [
        remote(field.at[mine], field.at[mine], at_row(dz, dh, 0)) for dz, dh in chip_peers
    ]
    f_m = send(gb, 3, 0, flip)
    f_p = send(gb, 1, 0, flip)
    fa.wait_recv()
    fau = send(ga, 0, 1, up)
    fad = send(ga, 0, 1, down)
    share(("ga", 0, 1, ""), ga, 0, 1)
    au.wait_recv()
    au2 = send(ga, 3, 0, up)
    share(("ga", 3, 0, ""), ga, 3, 0)
    ad.wait_recv()
    share(("ga", 1, 0, ""), ga, 1, 0)
    fb.wait_recv()
    share(("gb", 0, 1, ""), gb, 0, 1)
    bu2.wait_recv()
    f_top = send(gb, 2, 0, flip, top)
    share(("gb", 2, 0, "top"), gb, 2, 0, top)
    bd2.wait_recv()
    f_low = send(gb, 2, 0, flip, low)
    share(("gb", 2, 0, "low"), gb, 2, 0, low)
    mu2.wait_recv()
    share(("gm", 2, 0, ""), gm, 2, 0)
    mfd2.wait_recv()
    share(("gm", 2, 1, ""), gm, 2, 1)
    for copy in z4_copies:
        copy.wait_recv()

    token = lax.broadcasted_iota(jnp.int32, (1, TOK), 1)
    line, place = token >> 6, token & (GW - 1)

    def moved(values, di, dj):
        shift = di * GW + dj
        if shift:
            values = pltpu.roll(values, (-shift) % TOK, 1)
        inside = (
            (line + di >= 0) & (line + di < GH) & (place + dj >= 0) & (place + dj < GW)
        )
        return jnp.where(inside, values, 0.0)

    @pl.loop(0, TOK // 128)
    def _(t):
        at = pl.ds(pl.multiple_of(t * 128, 128), 128)
        value = field[:, at].astype(F32)
        act = (value * cdf(value)).astype(BF16).astype(F32)
        for k in range(9):
            shifted[k : k + 1, at] = jnp.sum(act * taps[k], axis=0, keepdims=True)
        shifted[9:10, at] = jnp.sum(value * taps[9], axis=0, keepdims=True)

    pred = shifted[9:10, :]
    for k in range(9):
        pred = pred + moved(shifted[k : k + 1, :], k // 3 - 1, k % 3 - 1)
    for index in range(8):
        rows_buf[index : index + 1, :] = pred[:, index * STRIP : (index + 1) * STRIP]
    pred_all[c] = rows_buf[...]
    pred_copy = remote(pred_all.at[c], pred_all.at[c], partner)

    @pl.loop(0, TOK // 128)
    def _(t):
        at = pl.ds(pl.multiple_of(t * 128, 128), 128)
        field_slope[:, at] = slope(field[:, at].astype(F32))

    valid = jnp.concatenate([st_col[index][2:3] for index in range(8)], axis=0)
    target = jnp.concatenate([st_col[index][3:4] for index in range(8)], axis=0)
    pred_copy.wait_recv()
    err = valid * (pred_all[0] + pred_all[1] - target)

    def whole(values):
        return jnp.sum(jnp.sum(values, axis=1, keepdims=True), axis=0, keepdims=True)

    count = whole(valid)
    mean_err = whole(err) / count
    loss_ref[0, 0] = jnp.sum(whole(err * err) / count - FOCUS * mean_err * mean_err)
    grad_pred = valid * (2.0 * err - 2.0 * FOCUS * mean_err)
    grad_pred = jnp.concatenate([grad_pred[index : index + 1] for index in range(8)], axis=1)
    for k in range(9):
        shifted[k : k + 1, :] = moved(grad_pred, 1 - k // 3, 1 - k % 3)
    shifted[9:10, :] = grad_pred

    @pl.loop(0, TOK // 128)
    def _(t):
        at = pl.ds(pl.multiple_of(t * 128, 128), 128)
        back = taps[0] * shifted[0:1, at]
        for k in range(1, 9):
            back = back + taps[k] * shifted[k : k + 1, at]
        gz[pl.ds(first_channel, 128), at] = (
            taps[9] * shifted[9:10, at] + field_slope[:, at] * back
        ).astype(BF16)

    half_z = gz.at[pl.ds(first_channel, 128)]
    gz_copy = remote(half_z, half_z, partner)

    second_channel = pl.multiple_of(other * 128, 128)
    gh_own[:, pl.ds(first_channel, 128)] = nt(hid[...], half_z[...]).astype(BF16)
    gz_copy.wait_recv()
    gh_own[:, pl.ds(second_channel, 128)] = nt(
        hid[...], gz[pl.ds(second_channel, 128), :]
    ).astype(BF16)
    local(gh_own, gh_out.at[own_rows(0, 0)])
    gh_copies = [
        remote(gh_own, gh_out.at[own_rows(0, 0)], at_row(dz, dh, 0)) for dz, dh in chip_peers
    ]
    gh_pair = [remote(gh_own, gh_out.at[own_rows(0, 0)], partner)]
    def ready(dz):
        for key, copy in pair.items():
            if key[1] == dz:
                copy.wait_recv()

    n_mine = n_t.at[pl.ds(feature_at, FEAT)]

    def column(dz):
        @pl.loop(0, 2)
        def _(core):
            base = core * 8 + zz(dz) * 2
            for half in (0, 1):
                rows = slice(half * OWN, (half + 1) * OWN)
                weights = gm[base + half]
                grad[rows, :TA] = (
                    mm(weights, gz[:, :TA]) * ga[base + half].astype(F32)
                ).astype(BF16)
                grad[rows, TA:] = (
                    mm(weights, gz[:, TA:]) * gb[base + half].astype(F32)
                ).astype(BF16)
            up_own[dz, core] = nt(n_mine[...], grad[...])
            at = pl.multiple_of(base * OWN, 2 * OWN)
            pltpu.make_async_copy(
                up_own.at[dz, core], up_out.at[:, pl.ds(at, 2 * OWN)], out_sems.at[dz, core]
            ).start()

    fad.wait_recv()
    fad2 = send(ga, 1, 1, down)
    share(("ga", 1, 1, ""), ga, 1, 1)
    fau.wait_recv()
    share(("ga", 3, 1, ""), ga, 3, 1)
    f_m.wait_recv()
    share(("gb", 3, 1, ""), gb, 3, 1)
    f_p.wait_recv()
    share(("gb", 1, 1, ""), gb, 1, 1)
    ready(0)
    column(0)
    f_top.wait_recv()
    share(("gb", 2, 1, "top"), gb, 2, 1, top)
    f_low.wait_recv()
    share(("gb", 2, 1, "low"), gb, 2, 1, low)
    ready(3)
    column(3)
    au2.wait_recv()
    share(("ga", 2, 0, ""), ga, 2, 0)
    ready(1)
    column(1)
    fad2.wait_recv()
    share(("ga", 2, 1, ""), ga, 2, 1)
    ready(2)
    column(2)

    for (dz, dh), copy in zip(chip_peers, gh_copies):
        copy.wait_recv()
        came = gh_out.at[own_rows(-dz, dh)]
        gh_pair.append(remote(came, came, partner))
    for copy in gh_pair:
        copy.wait_recv()

    for dz in range(4):

        @pl.loop(0, 2)
        def _(core):
            at = pl.multiple_of((core * 8 + zz(dz) * 2) * OWN, 2 * OWN)
            pltpu.make_async_copy(
                up_own.at[dz, core], up_out.at[:, pl.ds(at, 2 * OWN)], out_sems.at[dz, core]
            ).wait()

    started[-1].wait()
    for copy in sent:
        copy.wait_send()


def weight_kernel(gh_hbm, proj_hbm, up_hbm, up_out, down_out, gh, proj, up, down, in_sems, out_sems):
    rows, lines = HID // N_DOWN, FEAT // N_UP

    def down_at(index):
        return pl.ds(index * rows, rows)

    def up_at(index):
        return pl.ds(index * lines, lines)

    proj_in = pltpu.make_async_copy(proj_hbm, proj, in_sems.at[0])
    gh_in = [
        pltpu.make_async_copy(gh_hbm.at[down_at(k)], gh.at[down_at(k)], in_sems.at[1 + k])
        for k in range(N_DOWN)
    ]
    up_in = [
        pltpu.make_async_copy(up_hbm.at[up_at(k)], up.at[up_at(k)], in_sems.at[1 + N_DOWN + k])
        for k in range(N_UP)
    ]
    for copy in [proj_in] + gh_in + up_in:
        copy.start()
    leaving = []
    proj_in.wait()
    for k in range(N_DOWN):
        gh_in[k].wait()
        down[down_at(k), :] = nt(gh[down_at(k), :], proj[...])
        leaving.append(
            pltpu.make_async_copy(down.at[down_at(k)], down_out.at[down_at(k)], out_sems.at[k])
        )
        leaving[-1].start()
    for k in range(N_UP):
        up_in[k].wait()
        leaving.append(
            pltpu.make_async_copy(up.at[up_at(k)], up_out.at[up_at(k)], out_sems.at[N_DOWN + k])
        )
        leaving[-1].start()
    for copy in leaving:
        copy.wait()


def on_device(tokens, ln_gain, w_up, w_down, proj, conv_kernel, head_weight, depth_mm, lidar_mask):
    vmem = pl.BlockSpec(memory_space=pltpu.VMEM)
    anywhere = pl.BlockSpec(memory_space=pl.ANY)
    up_held, grad_hidden, loss = pl.pallas_call(
        step_kernel,
        name="mlp_step",
        out_shape=[
            jax.ShapeDtypeStruct((FEAT, HID), F32),
            jax.ShapeDtypeStruct((HID, CH), BF16),
            jax.ShapeDtypeStruct((1, 1), F32),
        ],
        in_specs=[
            anywhere, vmem, anywhere, anywhere, anywhere, anywhere, vmem, anywhere, anywhere,
        ],
        out_specs=[anywhere, anywhere, pl.BlockSpec(memory_space=pltpu.SMEM)],
        scratch_shapes=[
            pltpu.VMEM((STRIP, FEAT), BF16),
            pltpu.VMEM((FEAT, HID), BF16),
            pltpu.VMEM((HID, FEAT), BF16),
            pltpu.VMEM((FEAT, CH), BF16),
            pltpu.VMEM((9, 128, CH), BF16),
            pltpu.VMEM((2, GW), jnp.int32),
            pltpu.VMEM((2, GW), jnp.int32),
            pltpu.VMEM((8, FEAT, STRIP), BF16),
            pltpu.VMEM((16, 8, STRIP), F32),
            pltpu.VMEM((8, 8, STRIP), F32),
            pltpu.VMEM((HALF, 2 * FEAT), BF16),
            pltpu.VMEM((HALF, FEAT), BF16),
            pltpu.VMEM((HALF, FEAT), BF16),
            pltpu.VMEM((FEAT, CH), BF16),
            pltpu.VMEM((2 * FEAT, TOK), BF16),
            pltpu.VMEM((8, OWN, CH), F32),
            pltpu.VMEM((8, OWN, CH), BF16),
            pltpu.VMEM((7, OWN, CH), BF16),
            pltpu.VMEM((OWN, CH), BF16),
            pltpu.VMEM((4, 2, OWN, TA), BF16),
            pltpu.VMEM((4, 2, OWN, TB), BF16),
            pltpu.VMEM((2, OWN, TA), BF16),
            pltpu.VMEM((2, 2, OWN, TA), BF16),
            pltpu.VMEM((OWN, TA), BF16),
            pltpu.VMEM((4, OWN, TB), BF16),
            pltpu.VMEM((2, OWN // 2, TB), BF16),
            pltpu.VMEM((2, OWN, TB), BF16),
            pltpu.VMEM((OWN, TOK), F32),
            pltpu.VMEM((OWN, TOK), BF16),
            pltpu.VMEM((CH, TOK), F32),
            pltpu.VMEM((128, TOK), BF16),
            pltpu.VMEM((128, TOK), BF16),
            pltpu.VMEM((128, TOK), BF16),
            pltpu.VMEM((7, 16, TOK), BF16),
            pltpu.VMEM((8, 16, TOK), BF16),
            pltpu.VMEM((10, 128, 128), F32),
            pltpu.VMEM((128, TOK), BF16),
            pltpu.VMEM((128, TOK), F32),
            pltpu.VMEM((16, TOK), F32),
            pltpu.VMEM((2, 8, STRIP), F32),
            pltpu.VMEM((8, STRIP), F32),
            pltpu.VMEM((CH, TOK), BF16),
            pltpu.VMEM((16, OWN, CH), BF16),
            pltpu.VMEM((16, OWN, TA), BF16),
            pltpu.VMEM((16, OWN, TB), BF16),
            pltpu.VMEM((OWN, CH), BF16),
            pltpu.VMEM((2 * OWN, TOK), BF16),
            pltpu.VMEM((4, 2, FEAT, 2 * OWN), F32),
            pltpu.SemaphoreType.DMA((N_SEMS,)),
            pltpu.SemaphoreType.DMA((N_SEMS,)),
            pltpu.SemaphoreType.DMA((9,)),
            pltpu.SemaphoreType.DMA((4, 2)),
        ],
        compiler_params=pltpu.CompilerParams(
            collective_id=0, has_side_effects=True, vmem_limit_bytes=60 * 2**20
        ),
        cost_estimate=pl.CostEstimate(flops=6 * 10**9, bytes_accessed=16 * 2**20, transcendentals=10**6),
    )(
        tokens, ln_gain, w_up, w_down, proj, conv_kernel.reshape(9, CH, CH),
        head_weight.reshape(1, CH), depth_mm, lidar_mask,
    )
    grad_up, grad_down = pl.pallas_call(
        weight_kernel,
        name="weight_grads",
        out_shape=[
            jax.ShapeDtypeStruct((FEAT, HID), F32),
            jax.ShapeDtypeStruct((HID, FEAT), F32),
        ],
        in_specs=[anywhere, anywhere, anywhere],
        out_specs=[anywhere, anywhere],
        scratch_shapes=[
            pltpu.VMEM((HID, CH), BF16),
            pltpu.VMEM((FEAT, CH), BF16),
            pltpu.VMEM((FEAT, HID), F32),
            pltpu.VMEM((HID, FEAT), F32),
            pltpu.SemaphoreType.DMA((1 + N_DOWN + N_UP,)),
            pltpu.SemaphoreType.DMA((N_DOWN + N_UP,)),
        ],
        compiler_params=pltpu.CompilerParams(vmem_limit_bytes=60 * 2**20),
        cost_estimate=pl.CostEstimate(flops=6 * 10**8, bytes_accessed=16 * 2**20, transcendentals=0),
    )(grad_hidden, proj, up_held)
    return (grad_up, grad_down, loss.reshape(()))


def solution(mesh):
    return jax.shard_map(
        on_device,
        mesh=mesh,
        in_specs=(
            P("col", "row"),
            P("row"),
            P("row", "col"),
            P("col", "row"),
            P("row", None),
            P(),
            P(),
            P("col", None),
            P("col", None),
        ),
        out_specs=(P("row", "col"), P("col", "row"), P()),
        check_vma=False,
    )
```

```python
import math

import jax
import jax.numpy as jnp
from jax import lax
from jax.experimental import pallas as pl
from jax.experimental.pallas import tpu as pltpu
from jax.sharding import PartitionSpec as P

MESH = pl.DeviceIdType.MESH
F32 = jnp.float32
BF16 = jnp.bfloat16

WIDTH = 6144
GW = 64
GH = 16
TOK = 1024
STRIP = 128
FEAT = 384
HID = 3072
HALF = 1536
OWN = 192
CH = 256
TA = 512
TB = TOK - TA
FOCUS = 0.85
EPS = 1e-06

ROOT_HALF = math.sqrt(0.5)
DENSITY = 1.0 / math.sqrt(2.0 * math.pi)

N_SEMS = 192
N_DOWN = 6
N_UP = 8


def cdf(v):
    return 0.5 * (1.0 + lax.erf(v * ROOT_HALF))


def slope(v):
    return cdf(v) + v * (DENSITY * jnp.exp(-0.5 * v * v))


def tn(a, b):
    return lax.dot_general(a, b, (((0,), (0,)), ((), ())), preferred_element_type=F32)


def nt(a, b):
    return lax.dot_general(a, b, (((1,), (1,)), ((), ())), preferred_element_type=F32)


def mm(a, b):
    return jnp.dot(a, b, preferred_element_type=F32)


def step_kernel(
    tok_hbm, gain_ref, wup_hbm, wdn_hbm, proj_hbm, conv_hbm, head_ref, depth_hbm, mask_hbm,
    up_out, gh_out, loss_ref,
    tok_ref, wup_ref, wdn, proj_ref, conv, depth_ref, mask_ref,
    xall, st_row, st_col, w_t, w_send, wd_peer, proj_peer, n_t, m_sum, m_part, m_recv, m_own,
    p_a, p_b, a1, a2, a3, b1, b2, b3, pre, hid, zc, z1, z1_recv, z2, z2_recv, z3,
    taps, field, field_slope, shifted, pred_all, rows_buf, gz, gm, ga, gb, gh_own, grad, up_own, send_sems, recv_sems, local_sems, out_sems,
):
    row, col = lax.axis_index("row"), lax.axis_index("col")
    z, h, c = row // 4, lax.rem(row // 2, 2), lax.rem(row, 2)
    used = [0]

    def zz(dz):
        return lax.rem(z + dz + 4, 4)

    def hh(dh):
        return lax.rem(h + dh, 2)

    def at_row(dz, dh, dc):
        return {"row": zz(dz) * 4 + hh(dh) * 2 + lax.rem(c + dc, 2)}

    def at_col(dl, dx):
        return {"col": lax.rem(col // 4 + dl, 2) * 4 + lax.rem(lax.rem(col, 4) + dx, 4)}

    def remote(src, dst, device):
        at = used[0]
        used[0] += 1
        copy = pltpu.make_async_remote_copy(
            src_ref=src, dst_ref=dst, send_sem=send_sems.at[at], recv_sem=recv_sems.at[at],
            device_id=device, device_id_type=MESH,
        )
        copy.start()
        sent.append(copy)
        return copy

    def slot(dz, dh):
        return c * 8 + zz(dz) * 2 + hh(dh)

    def own_rows(dz, dh):
        return pl.ds(pl.multiple_of(slot(dz, dh) * OWN, 64), OWN)

    sent = []
    row_peers = [
        (dz, dh, dc) for dz in (2, 1, 3, 0) for dh in (1, 0) for dc in (1, 0) if (dz, dh, dc) != (0, 0, 0)
    ]
    chip_peers = [(dz, dh) for dz in (2, 1, 3, 0) for dh in (1, 0) if (dz, dh) != (0, 0)]
    col_peers = [(dl, dx) for dl in (1, 0) for dx in (2, 1, 3, 0) if (dl, dx) != (0, 0)]
    partner = at_row(0, 0, 1)
    here = z * 2 + h
    other = 1 - c

    barrier = pltpu.get_barrier_semaphore()
    for peer in row_peers:
        pl.semaphore_signal(barrier, inc=1, device_id=at_row(*peer), device_id_type=MESH)
    for peer in col_peers:
        pl.semaphore_signal(barrier, inc=1, device_id=at_col(*peer), device_id_type=MESH)

    started = []

    def local(src, dst):
        copy = pltpu.make_async_copy(src, dst, local_sems.at[len(started)])
        copy.start()
        started.append(copy)
        return copy

    first_channel = pl.multiple_of(c * 128, 128)
    tok_copy = local(tok_hbm, tok_ref)
    proj_in = local(proj_hbm, proj_ref)
    wdn_copy = local(wdn_hbm, wdn)
    wup_copy = local(wup_hbm, wup_ref)
    depth_copy = local(depth_hbm, depth_ref)
    mask_copy = local(mask_hbm, mask_ref)
    conv_copy = local(conv_hbm.at[:, pl.ds(first_channel, 128), :], conv)

    tok_copy.wait()
    x_t = tok_ref[...].astype(F32).T
    xall[col] = x_t.astype(BF16)
    st_row[row] = jnp.concatenate(
        [
            jnp.sum(x_t, 0, keepdims=True),
            jnp.sum(x_t * x_t, 0, keepdims=True),
            jnp.zeros((6, STRIP), F32),
        ],
        axis=0,
    )
    own_half = pl.multiple_of(c * HALF, HALF)
    to_peer = pl.multiple_of(other * HALF, HALF)
    pl.semaphore_wait(barrier, len(row_peers) + len(col_peers))

    stat_copies = [remote(st_row.at[row], st_row.at[row], at_row(*peer)) for peer in row_peers]
    across = remote(xall.at[col], xall.at[col], at_col(1, 0))
    token_copies = [remote(xall.at[col], xall.at[col], at_col(0, dx)) for dx in (2, 1, 3)]
    proj_in.wait()
    wdn_copy.wait()
    wd_copy = remote(wdn.at[pl.ds(to_peer, HALF)], wd_peer, partner)
    proj_copy = remote(proj_ref, proj_peer, partner)

    @pl.loop(0, 8)
    def _(k):
        m_sum[k] = mm(wdn[pl.ds(pl.multiple_of(own_half + k * OWN, 64), OWN), :], proj_ref[...])

    across.wait_recv()
    came = xall.at[lax.rem(col + 4, 8)]
    token_copies += [remote(came, came, at_col(0, dx)) for dx in (2, 1, 3)]

    wd_copy.wait_recv()
    proj_copy.wait_recv()

    @pl.loop(0, 8)
    def _(k):
        more = mm(wd_peer[pl.ds(pl.multiple_of(k * OWN, 64), OWN), :], proj_peer[...])
        m_part[k] = (m_sum[k] + more).astype(BF16)

    m_copies = []
    for index, (dz, dh) in enumerate(chip_peers):
        m_copies.append(
            remote(m_part.at[zz(dz) * 2 + hh(dh)], m_recv.at[index], at_row(dz, dh, 0))
        )

    for copy in stat_copies:
        copy.wait_recv()
    total = st_row[0]
    for index in range(1, 16):
        total = total + st_row[index]
    mean = total[0:1] / WIDTH
    spread = total[1:2] / WIDTH - mean * mean
    depth_copy.wait()
    mask_copy.wait()
    depth = depth_ref[...].astype(F32)
    seen = mask_ref[...].astype(F32)
    st_col[col] = jnp.concatenate(
        [
            mean,
            lax.rsqrt(spread + EPS),
            jnp.concatenate([seen[0:1], seen[1:2]], axis=1),
            jnp.log(jnp.concatenate([depth[0:1], depth[1:2]], axis=1) * 0.001),
            jnp.zeros((4, STRIP), F32),
        ],
        axis=0,
    )
    norm_copies = [remote(st_col.at[col], st_col.at[col], at_col(*peer)) for peer in col_peers]

    feature_at = pl.multiple_of(c * FEAT, 128)
    wup_copy.wait()

    @pl.loop(0, HALF // 128)
    def _(i):
        at = pl.multiple_of(to_peer + i * 128, 128)
        w_send[pl.ds(pl.multiple_of(i * 128, 128), 128), :] = wup_ref[:, pl.ds(at, 128)].T

    w_copy = remote(w_send, w_t.at[:, pl.ds(feature_at, FEAT)], partner)

    @pl.loop(0, HALF // 128)
    def _(i):
        at = pl.multiple_of(own_half + i * 128, 128)
        w_t[pl.ds(pl.multiple_of(i * 128, 128), 128), pl.ds(feature_at, FEAT)] = wup_ref[:, pl.ds(at, 128)].T

    gain = jnp.broadcast_to(gain_ref[...].reshape(1, FEAT), (STRIP, FEAT)).T
    for copy in norm_copies:
        copy.wait_recv()
    for copy in token_copies:
        copy.wait_recv()

    n_copies = []
    for first in (0, 4):
        for index in range(first, first + 4):
            stats = st_col[index]
            n_t[pl.ds(feature_at, FEAT), index * STRIP : (index + 1) * STRIP] = (
                (xall[index].astype(F32) - stats[0:1]) * stats[1:2] * gain
            ).astype(BF16)
        half = n_t.at[pl.ds(feature_at, FEAT), first * STRIP : (first + 4) * STRIP]
        n_copies.append(remote(half, half, partner))
    w_copy.wait_recv()

    a_copies, b_copies = {}, {}

    def project(dz, into, first):
        base = pl.multiple_of(zz(dz) * 2 * OWN, 2 * OWN)

        @pl.loop(0, into.shape[3] // 256)
        def _(t):
            at = pl.multiple_of(t * 256, 256)
            both = mm(
                w_t[pl.ds(base, 2 * OWN), :], n_t[:, pl.ds(pl.multiple_of(first + at, 256), 256)]
            ).astype(BF16)
            into[zz(dz), 0, :, pl.ds(at, 256)] = both[:OWN]
            into[zz(dz), 1, :, pl.ds(at, 256)] = both[OWN:]

    up, down, flip = at_row(1, 0, 0), at_row(3, 0, 0), at_row(0, 1, 0)
    n_copies[0].wait_recv()
    project(2, p_a, 0)
    a_up = remote(p_a.at[zz(2), 0], a1.at[0], up)
    a_down = remote(p_a.at[zz(2), 1], a1.at[1], down)
    n_copies[1].wait_recv()

    def project_b(dz):
        project(dz, p_b, TA)
        b_copies[dz] = remote(p_b.at[zz(dz), 1 - h], b1.at[zz(dz)], flip)

    project_b(2)
    project(1, p_a, 0)
    a_up1 = remote(p_a.at[zz(1), 1], a2.at[0, 1], up)
    project(3, p_a, 0)
    a_down1 = remote(p_a.at[zz(3), 0], a2.at[1, 0], down)
    for dz in (1, 3, 0):
        project_b(dz)
    project(0, p_a, 0)

    def add(into, more):
        into[...] = (into[...].astype(F32) + more[...].astype(F32)).astype(BF16)

    a_up.wait_recv()
    add(p_a.at[zz(1), 0], a1.at[0])
    a_up2 = remote(p_a.at[zz(1), 0], a2.at[0, 0], up)
    a_down.wait_recv()
    add(p_a.at[zz(3), 1], a1.at[1])
    a_down2 = remote(p_a.at[zz(3), 1], a2.at[1, 1], down)

    b_copies[2].wait_recv()
    add(p_b.at[zz(2), h], b1.at[zz(2)])
    b_up = remote(p_b.at[zz(2), h, 0:96], b2.at[0], up)
    b_down = remote(p_b.at[zz(2), h, 96:192], b2.at[1], down)
    b_copies[1].wait_recv()
    add(p_b.at[zz(1), h], b1.at[zz(1)])
    b_copies[3].wait_recv()
    add(p_b.at[zz(3), h], b1.at[zz(3)])

    for copy in (a_up1, a_down1, a_up2, a_down2):
        copy.wait_recv()
    p_a[z, 1 - h] = (
        p_a[z, 1 - h].astype(F32) + a2[0, 1 - h].astype(F32) + a2[1, 1 - h].astype(F32)
    ).astype(BF16)
    a_flip = remote(p_a.at[z, 1 - h], a3, flip)

    b_up.wait_recv()
    add(p_b.at[zz(1), h, 0:96], b2.at[0])
    b_up2 = remote(p_b.at[zz(1), h], b3.at[0], up)
    b_down.wait_recv()
    add(p_b.at[zz(3), h, 96:192], b2.at[1])
    b_down2 = remote(p_b.at[zz(3), h], b3.at[1], down)

    for copy in m_copies:
        copy.wait_recv()
    total = m_part[here].astype(F32)
    for index in range(7):
        total = total + m_recv[index].astype(F32)
    m_own[...] = total.astype(BF16)
    gm[slot(0, 0)] = m_own[...]
    pair = {}

    def send(buf, dz, dh, device, rows=None):
        ref = buf.at[slot(dz, dh)] if rows is None else buf.at[slot(dz, dh), rows[0] : rows[1]]
        return remote(ref, ref, device)

    def share(name, buf, dz, dh, rows=None):
        pair[name] = send(buf, dz, dh, partner, rows)

    mf = send(gm, 0, 0, flip)
    mu = send(gm, 0, 0, up)
    md = send(gm, 0, 0, down)
    share(("gm", 0, 0, ""), gm, 0, 0)
    x_proj = tn(proj_ref[...], xall[col])

    conv_copy.wait()
    head = head_ref[...]
    for k in range(9):
        taps[k] = jnp.broadcast_to(
            jnp.sum(conv[k].astype(F32) * head, axis=1, keepdims=True), (128, 128)
        )
    lane = lax.broadcasted_iota(jnp.int32, (128, CH), 1)
    sub = lax.broadcasted_iota(jnp.int32, (128, CH), 0)
    taps[9] = jnp.broadcast_to(
        jnp.sum(jnp.where(lane == sub + first_channel, head, 0.0), axis=1, keepdims=True), (128, 128)
    )

    b_copies[0].wait_recv()
    a_flip.wait_recv()
    pre[:, :TA] = (
        p_a[z, h].astype(F32) + a2[0, h].astype(F32) + a2[1, h].astype(F32) + a3[...].astype(F32)
    )
    b_up2.wait_recv()
    b_down2.wait_recv()
    pre[:, TA:] = (
        p_b[z, h].astype(F32) + b1[z].astype(F32) + b3[0].astype(F32) + b3[1].astype(F32)
    )

    @pl.loop(0, TOK // 128)
    def _(t):
        at = pl.ds(pl.multiple_of(t * 128, 128), 128)
        value = pre[:, at]
        hid[:, at] = (value * cdf(value)).astype(BF16)

    @pl.loop(0, TOK // 256)
    def _(t):
        at = pl.ds(pl.multiple_of(t * 256, 256), 256)
        zc[:, at] = tn(m_own[...], hid[:, at])

    strip = pl.ds(pl.multiple_of(col * STRIP, STRIP), STRIP)
    zc[:, strip] = zc[:, strip] + x_proj

    z1[...] = zc[pl.ds(pl.multiple_of(other * 128, 128), 128), :].astype(BF16)
    z1_copy = remote(z1, z1_recv, partner)

    mine_a, mine_b = ga.at[slot(0, 0)], gb.at[slot(0, 0)]
    mf.wait_recv()
    mfu = send(gm, 0, 1, up)
    mfd = send(gm, 0, 1, down)
    share(("gm", 0, 1, ""), gm, 0, 1)
    top, low = (0, 96), (96, 192)

    @pl.loop(0, TB // 128)
    def _(t):
        at = pl.ds(pl.multiple_of(t * 128, 128), 128)
        mine_b[:, at] = slope(pre[:, pl.ds(pl.multiple_of(TA + t * 128, 128), 128)]).astype(BF16)

    z1_copy.wait_recv()
    z2[...] = (
        zc[pl.ds(pl.multiple_of(c * 128, 128), 128), :] + z1_recv[...].astype(F32)
    ).astype(BF16)
    z2_copies = []
    for index, (dz, dh) in enumerate(chip_peers):
        at = pl.multiple_of((zz(dz) * 2 + hh(dh)) * 16, 16)
        z2_copies.append(remote(z2.at[pl.ds(at, 16)], z2_recv.at[index], at_row(dz, dh, 0)))
    bu = send(gb, 0, 0, up)
    bd = send(gb, 0, 0, down)
    mu.wait_recv()
    mu2 = send(gm, 3, 0, up)
    share(("gm", 3, 0, ""), gm, 3, 0)
    md.wait_recv()
    share(("gm", 1, 0, ""), gm, 1, 0)
    share(("gb", 0, 0, ""), gb, 0, 0)

    @pl.loop(0, TA // 128)
    def _(t):
        at = pl.ds(pl.multiple_of(t * 128, 128), 128)
        mine_a[:, at] = slope(pre[:, at]).astype(BF16)

    fa = send(ga, 0, 0, flip)
    mfd.wait_recv()
    mfd2 = send(gm, 1, 1, down)
    share(("gm", 1, 1, ""), gm, 1, 1)
    mfu.wait_recv()
    share(("gm", 3, 1, ""), gm, 3, 1)
    share(("ga", 0, 0, ""), ga, 0, 0)
    mine = pl.ds(pl.multiple_of(here * 16, 16), 16)
    part = z2[mine, :].astype(F32)
    for index, copy in enumerate(z2_copies):
        copy.wait_recv()
        part = part + z2_recv[index].astype(F32)
    z3[col] = part.astype(BF16)
    z3_copies = [remote(z3.at[col], z3.at[col], at_col(*peer)) for peer in col_peers]
    au = send(ga, 0, 0, up)
    ad = send(ga, 0, 0, down)
    fb = send(gb, 0, 0, flip)
    bu.wait_recv()
    bu2 = send(gb, 3, 0, up, top)
    share(("gb", 3, 0, ""), gb, 3, 0)
    bd.wait_recv()
    bd2 = send(gb, 1, 0, down, low)
    share(("gb", 1, 0, ""), gb, 1, 0)
    for copy in z3_copies:
        copy.wait_recv()
    total = z3[0].astype(F32)
    for index in range(1, 8):
        total = total + z3[index].astype(F32)
    field[mine, :] = total.astype(BF16)
    z4_copies = [
        remote(field.at[mine], field.at[mine], at_row(dz, dh, 0)) for dz, dh in chip_peers
    ]
    f_m = send(gb, 3, 0, flip)
    f_p = send(gb, 1, 0, flip)
    fa.wait_recv()
    fau = send(ga, 0, 1, up)
    fad = send(ga, 0, 1, down)
    share(("ga", 0, 1, ""), ga, 0, 1)
    au.wait_recv()
    au2 = send(ga, 3, 0, up)
    share(("ga", 3, 0, ""), ga, 3, 0)
    ad.wait_recv()
    share(("ga", 1, 0, ""), ga, 1, 0)
    fb.wait_recv()
    share(("gb", 0, 1, ""), gb, 0, 1)
    bu2.wait_recv()
    f_top = send(gb, 2, 0, flip, top)
    share(("gb", 2, 0, "top"), gb, 2, 0, top)
    bd2.wait_recv()
    f_low = send(gb, 2, 0, flip, low)
    share(("gb", 2, 0, "low"), gb, 2, 0, low)
    mu2.wait_recv()
    share(("gm", 2, 0, ""), gm, 2, 0)
    mfd2.wait_recv()
    share(("gm", 2, 1, ""), gm, 2, 1)
    for copy in z4_copies:
        copy.wait_recv()

    token = lax.broadcasted_iota(jnp.int32, (1, TOK), 1)
    line, place = token >> 6, token & (GW - 1)

    def moved(values, di, dj):
        shift = di * GW + dj
        if shift:
            values = pltpu.roll(values, (-shift) % TOK, 1)
        inside = (
            (line + di >= 0) & (line + di < GH) & (place + dj >= 0) & (place + dj < GW)
        )
        return jnp.where(inside, values, 0.0)

    @pl.loop(0, TOK // 128)
    def _(t):
        at = pl.ds(pl.multiple_of(t * 128, 128), 128)
        value = field[:, at].astype(F32)
        act = (value * cdf(value)).astype(BF16).astype(F32)
        for k in range(9):
            shifted[k : k + 1, at] = jnp.sum(act * taps[k], axis=0, keepdims=True)
        shifted[9:10, at] = jnp.sum(value * taps[9], axis=0, keepdims=True)

    pred = shifted[9:10, :]
    for k in range(9):
        pred = pred + moved(shifted[k : k + 1, :], k // 3 - 1, k % 3 - 1)
    for index in range(8):
        rows_buf[index : index + 1, :] = pred[:, index * STRIP : (index + 1) * STRIP]
    pred_all[c] = rows_buf[...]
    pred_copy = remote(pred_all.at[c], pred_all.at[c], partner)
    fad.wait_recv()
    fad2 = send(ga, 1, 1, down)
    share(("ga", 1, 1, ""), ga, 1, 1)
    fau.wait_recv()
    share(("ga", 3, 1, ""), ga, 3, 1)

    @pl.loop(0, TOK // 128)
    def _(t):
        at = pl.ds(pl.multiple_of(t * 128, 128), 128)
        field_slope[:, at] = slope(field[:, at].astype(F32))

    valid = jnp.concatenate([st_col[index][2:3] for index in range(8)], axis=0)
    target = jnp.concatenate([st_col[index][3:4] for index in range(8)], axis=0)
    pred_copy.wait_recv()
    err = valid * (pred_all[0] + pred_all[1] - target)

    def whole(values):
        return jnp.sum(jnp.sum(values, axis=1, keepdims=True), axis=0, keepdims=True)

    count = whole(valid)
    mean_err = whole(err) / count
    loss_ref[0, 0] = jnp.sum(whole(err * err) / count - FOCUS * mean_err * mean_err)
    grad_pred = valid * (2.0 * err - 2.0 * FOCUS * mean_err)
    grad_pred = jnp.concatenate([grad_pred[index : index + 1] for index in range(8)], axis=1)
    for k in range(9):
        shifted[k : k + 1, :] = moved(grad_pred, 1 - k // 3, 1 - k % 3)
    shifted[9:10, :] = grad_pred

    @pl.loop(0, TOK // 128)
    def _(t):
        at = pl.ds(pl.multiple_of(t * 128, 128), 128)
        back = taps[0] * shifted[0:1, at]
        for k in range(1, 9):
            back = back + taps[k] * shifted[k : k + 1, at]
        gz[pl.ds(first_channel, 128), at] = (
            taps[9] * shifted[9:10, at] + field_slope[:, at] * back
        ).astype(BF16)

    half_z = gz.at[pl.ds(first_channel, 128)]
    gz_copy = remote(half_z, half_z, partner)

    second_channel = pl.multiple_of(other * 128, 128)
    gh_own[:, pl.ds(first_channel, 128)] = nt(hid[...], half_z[...]).astype(BF16)
    gz_copy.wait_recv()
    gh_own[:, pl.ds(second_channel, 128)] = nt(
        hid[...], gz[pl.ds(second_channel, 128), :]
    ).astype(BF16)
    local(gh_own, gh_out.at[own_rows(0, 0)])
    gh_copies = [
        remote(gh_own, gh_out.at[own_rows(0, 0)], at_row(dz, dh, 0)) for dz, dh in chip_peers
    ]
    gh_pair = [remote(gh_own, gh_out.at[own_rows(0, 0)], partner)]
    def ready(dz):
        for key, copy in pair.items():
            if key[1] == dz:
                copy.wait_recv()

    n_mine = n_t.at[pl.ds(feature_at, FEAT)]

    def column(dz):
        @pl.loop(0, 2)
        def _(core):
            base = core * 8 + zz(dz) * 2
            for half in (0, 1):
                rows = slice(half * OWN, (half + 1) * OWN)
                weights = gm[base + half]
                grad[rows, :TA] = (
                    mm(weights, gz[:, :TA]) * ga[base + half].astype(F32)
                ).astype(BF16)
                grad[rows, TA:] = (
                    mm(weights, gz[:, TA:]) * gb[base + half].astype(F32)
                ).astype(BF16)
            up_own[dz, core] = nt(n_mine[...], grad[...])
            at = pl.multiple_of(base * OWN, 2 * OWN)
            pltpu.make_async_copy(
                up_own.at[dz, core], up_out.at[:, pl.ds(at, 2 * OWN)], out_sems.at[dz, core]
            ).start()

    f_m.wait_recv()
    share(("gb", 3, 1, ""), gb, 3, 1)
    f_p.wait_recv()
    share(("gb", 1, 1, ""), gb, 1, 1)
    ready(0)
    column(0)
    f_top.wait_recv()
    share(("gb", 2, 1, "top"), gb, 2, 1, top)
    f_low.wait_recv()
    share(("gb", 2, 1, "low"), gb, 2, 1, low)
    ready(3)
    column(3)
    au2.wait_recv()
    share(("ga", 2, 0, ""), ga, 2, 0)
    ready(1)
    column(1)
    fad2.wait_recv()
    share(("ga", 2, 1, ""), ga, 2, 1)
    ready(2)
    column(2)

    for (dz, dh), copy in zip(chip_peers, gh_copies):
        copy.wait_recv()
        came = gh_out.at[own_rows(-dz, dh)]
        gh_pair.append(remote(came, came, partner))
    for copy in gh_pair:
        copy.wait_recv()

    for dz in range(4):

        @pl.loop(0, 2)
        def _(core):
            at = pl.multiple_of((core * 8 + zz(dz) * 2) * OWN, 2 * OWN)
            pltpu.make_async_copy(
                up_own.at[dz, core], up_out.at[:, pl.ds(at, 2 * OWN)], out_sems.at[dz, core]
            ).wait()

    started[-1].wait()
    for copy in sent:
        copy.wait_send()


def weight_kernel(gh_hbm, proj_hbm, up_hbm, up_out, down_out, gh, proj, up, down, in_sems, out_sems):
    rows, lines = HID // N_DOWN, FEAT // N_UP

    def down_at(index):
        return pl.ds(index * rows, rows)

    def up_at(index):
        return pl.ds(index * lines, lines)

    proj_in = pltpu.make_async_copy(proj_hbm, proj, in_sems.at[0])
    gh_in = [
        pltpu.make_async_copy(gh_hbm.at[down_at(k)], gh.at[down_at(k)], in_sems.at[1 + k])
        for k in range(N_DOWN)
    ]
    up_in = [
        pltpu.make_async_copy(up_hbm.at[up_at(k)], up.at[up_at(k)], in_sems.at[1 + N_DOWN + k])
        for k in range(N_UP)
    ]
    for copy in [proj_in] + gh_in + up_in:
        copy.start()
    leaving = []
    proj_in.wait()
    for k in range(N_DOWN):
        gh_in[k].wait()
        down[down_at(k), :] = nt(gh[down_at(k), :], proj[...])
        leaving.append(
            pltpu.make_async_copy(down.at[down_at(k)], down_out.at[down_at(k)], out_sems.at[k])
        )
        leaving[-1].start()
    for k in range(N_UP):
        up_in[k].wait()
        leaving.append(
            pltpu.make_async_copy(up.at[up_at(k)], up_out.at[up_at(k)], out_sems.at[N_DOWN + k])
        )
        leaving[-1].start()
    for copy in leaving:
        copy.wait()


def on_device(tokens, ln_gain, w_up, w_down, proj, conv_kernel, head_weight, depth_mm, lidar_mask):
    vmem = pl.BlockSpec(memory_space=pltpu.VMEM)
    anywhere = pl.BlockSpec(memory_space=pl.ANY)
    up_held, grad_hidden, loss = pl.pallas_call(
        step_kernel,
        name="mlp_step",
        out_shape=[
            jax.ShapeDtypeStruct((FEAT, HID), F32),
            jax.ShapeDtypeStruct((HID, CH), BF16),
            jax.ShapeDtypeStruct((1, 1), F32),
        ],
        in_specs=[
            anywhere, vmem, anywhere, anywhere, anywhere, anywhere, vmem, anywhere, anywhere,
        ],
        out_specs=[anywhere, anywhere, pl.BlockSpec(memory_space=pltpu.SMEM)],
        scratch_shapes=[
            pltpu.VMEM((STRIP, FEAT), BF16),
            pltpu.VMEM((FEAT, HID), BF16),
            pltpu.VMEM((HID, FEAT), BF16),
            pltpu.VMEM((FEAT, CH), BF16),
            pltpu.VMEM((9, 128, CH), BF16),
            pltpu.VMEM((2, GW), jnp.int32),
            pltpu.VMEM((2, GW), jnp.int32),
            pltpu.VMEM((8, FEAT, STRIP), BF16),
            pltpu.VMEM((16, 8, STRIP), F32),
            pltpu.VMEM((8, 8, STRIP), F32),
            pltpu.VMEM((HALF, 2 * FEAT), BF16),
            pltpu.VMEM((HALF, FEAT), BF16),
            pltpu.VMEM((HALF, FEAT), BF16),
            pltpu.VMEM((FEAT, CH), BF16),
            pltpu.VMEM((2 * FEAT, TOK), BF16),
            pltpu.VMEM((8, OWN, CH), F32),
            pltpu.VMEM((8, OWN, CH), BF16),
            pltpu.VMEM((7, OWN, CH), BF16),
            pltpu.VMEM((OWN, CH), BF16),
            pltpu.VMEM((4, 2, OWN, TA), BF16),
            pltpu.VMEM((4, 2, OWN, TB), BF16),
            pltpu.VMEM((2, OWN, TA), BF16),
            pltpu.VMEM((2, 2, OWN, TA), BF16),
            pltpu.VMEM((OWN, TA), BF16),
            pltpu.VMEM((4, OWN, TB), BF16),
            pltpu.VMEM((2, OWN // 2, TB), BF16),
            pltpu.VMEM((2, OWN, TB), BF16),
            pltpu.VMEM((OWN, TOK), F32),
            pltpu.VMEM((OWN, TOK), BF16),
            pltpu.VMEM((CH, TOK), F32),
            pltpu.VMEM((128, TOK), BF16),
            pltpu.VMEM((128, TOK), BF16),
            pltpu.VMEM((128, TOK), BF16),
            pltpu.VMEM((7, 16, TOK), BF16),
            pltpu.VMEM((8, 16, TOK), BF16),
            pltpu.VMEM((10, 128, 128), F32),
            pltpu.VMEM((128, TOK), BF16),
            pltpu.VMEM((128, TOK), F32),
            pltpu.VMEM((16, TOK), F32),
            pltpu.VMEM((2, 8, STRIP), F32),
            pltpu.VMEM((8, STRIP), F32),
            pltpu.VMEM((CH, TOK), BF16),
            pltpu.VMEM((16, OWN, CH), BF16),
            pltpu.VMEM((16, OWN, TA), BF16),
            pltpu.VMEM((16, OWN, TB), BF16),
            pltpu.VMEM((OWN, CH), BF16),
            pltpu.VMEM((2 * OWN, TOK), BF16),
            pltpu.VMEM((4, 2, FEAT, 2 * OWN), F32),
            pltpu.SemaphoreType.DMA((N_SEMS,)),
            pltpu.SemaphoreType.DMA((N_SEMS,)),
            pltpu.SemaphoreType.DMA((9,)),
            pltpu.SemaphoreType.DMA((4, 2)),
        ],
        compiler_params=pltpu.CompilerParams(
            collective_id=0, has_side_effects=True, vmem_limit_bytes=60 * 2**20
        ),
        cost_estimate=pl.CostEstimate(flops=6 * 10**9, bytes_accessed=16 * 2**20, transcendentals=10**6),
    )(
        tokens, ln_gain, w_up, w_down, proj, conv_kernel.reshape(9, CH, CH),
        head_weight.reshape(1, CH), depth_mm, lidar_mask,
    )
    grad_up, grad_down = pl.pallas_call(
        weight_kernel,
        name="weight_grads",
        out_shape=[
            jax.ShapeDtypeStruct((FEAT, HID), F32),
            jax.ShapeDtypeStruct((HID, FEAT), F32),
        ],
        in_specs=[anywhere, anywhere, anywhere],
        out_specs=[anywhere, anywhere],
        scratch_shapes=[
            pltpu.VMEM((HID, CH), BF16),
            pltpu.VMEM((FEAT, CH), BF16),
            pltpu.VMEM((FEAT, HID), F32),
            pltpu.VMEM((HID, FEAT), F32),
            pltpu.SemaphoreType.DMA((1 + N_DOWN + N_UP,)),
            pltpu.SemaphoreType.DMA((N_DOWN + N_UP,)),
        ],
        compiler_params=pltpu.CompilerParams(vmem_limit_bytes=60 * 2**20),
        cost_estimate=pl.CostEstimate(flops=6 * 10**8, bytes_accessed=16 * 2**20, transcendentals=0),
    )(grad_hidden, proj, up_held)
    return (grad_up, grad_down, loss.reshape(()))


def solution(mesh):
    return jax.shard_map(
        on_device,
        mesh=mesh,
        in_specs=(
            P("col", "row"),
            P("row"),
            P("row", "col"),
            P("col", "row"),
            P("row", None),
            P(),
            P(),
            P("col", None),
            P("col", None),
        ),
        out_specs=(P("row", "col"), P("col", "row"), P()),
        check_vma=False,
    )
```

```python
import math

import jax
import jax.numpy as jnp
from jax import lax
from jax.experimental import pallas as pl
from jax.experimental.pallas import tpu as pltpu
from jax.sharding import PartitionSpec as P

MESH = pl.DeviceIdType.MESH
F32 = jnp.float32
BF16 = jnp.bfloat16

WIDTH = 6144
GW = 64
GH = 16
TOK = 1024
STRIP = 128
FEAT = 384
HID = 3072
HALF = 1536
OWN = 192
CH = 256
TA = 512
TB = TOK - TA
FOCUS = 0.85
EPS = 1e-06

ROOT_HALF = math.sqrt(0.5)
DENSITY = 1.0 / math.sqrt(2.0 * math.pi)

N_SEMS = 192
N_DOWN = 6
N_UP = 8


def cdf(v):
    return 0.5 * (1.0 + lax.erf(v * ROOT_HALF))


def slope(v):
    return cdf(v) + v * (DENSITY * jnp.exp(-0.5 * v * v))


def tn(a, b):
    return lax.dot_general(a, b, (((0,), (0,)), ((), ())), preferred_element_type=F32)


def nt(a, b):
    return lax.dot_general(a, b, (((1,), (1,)), ((), ())), preferred_element_type=F32)


def mm(a, b):
    return jnp.dot(a, b, preferred_element_type=F32)


def step_kernel(
    tok_hbm, gain_ref, wup_hbm, wdn_hbm, proj_hbm, conv_hbm, head_ref, depth_hbm, mask_hbm,
    up_out, gh_out, loss_ref,
    tok_ref, wup_ref, wdn, proj_ref, conv, depth_ref, mask_ref,
    xall, st_row, st_col, w_t, w_send, wd_peer, proj_peer, n_t, m_sum, m_part, m_recv, m_own,
    p_a, p_b, a1, a2, a3, b1, b2, b3, pre, hid, zc, z1, z1_recv, z2, z2_recv, z3,
    taps, field, field_slope, shifted, pred_all, rows_buf, gz, gm, ga, gb, gh_own, grad, up_own, send_sems, recv_sems, local_sems, out_sems,
):
    row, col = lax.axis_index("row"), lax.axis_index("col")
    z, h, c = row // 4, lax.rem(row // 2, 2), lax.rem(row, 2)
    used = [0]

    def zz(dz):
        return lax.rem(z + dz + 4, 4)

    def hh(dh):
        return lax.rem(h + dh, 2)

    def at_row(dz, dh, dc):
        return {"row": zz(dz) * 4 + hh(dh) * 2 + lax.rem(c + dc, 2)}

    def at_col(dl, dx):
        return {"col": lax.rem(col // 4 + dl, 2) * 4 + lax.rem(lax.rem(col, 4) + dx, 4)}

    def remote(src, dst, device):
        at = used[0]
        used[0] += 1
        copy = pltpu.make_async_remote_copy(
            src_ref=src, dst_ref=dst, send_sem=send_sems.at[at], recv_sem=recv_sems.at[at],
            device_id=device, device_id_type=MESH,
        )
        copy.start()
        sent.append(copy)
        return copy

    def slot(dz, dh):
        return c * 8 + zz(dz) * 2 + hh(dh)

    def own_rows(dz, dh):
        return pl.ds(pl.multiple_of(slot(dz, dh) * OWN, 64), OWN)

    sent = []
    row_peers = [
        (dz, dh, dc) for dz in (2, 1, 3, 0) for dh in (1, 0) for dc in (1, 0) if (dz, dh, dc) != (0, 0, 0)
    ]
    chip_peers = [(dz, dh) for dz in (2, 1, 3, 0) for dh in (1, 0) if (dz, dh) != (0, 0)]
    col_peers = [(dl, dx) for dl in (1, 0) for dx in (2, 1, 3, 0) if (dl, dx) != (0, 0)]
    partner = at_row(0, 0, 1)
    here = z * 2 + h
    other = 1 - c

    barrier = pltpu.get_barrier_semaphore()
    for peer in row_peers:
        pl.semaphore_signal(barrier, inc=1, device_id=at_row(*peer), device_id_type=MESH)
    for peer in col_peers:
        pl.semaphore_signal(barrier, inc=1, device_id=at_col(*peer), device_id_type=MESH)

    started = []

    def local(src, dst):
        copy = pltpu.make_async_copy(src, dst, local_sems.at[len(started)])
        copy.start()
        started.append(copy)
        return copy

    first_channel = pl.multiple_of(c * 128, 128)
    tok_copy = local(tok_hbm, tok_ref)
    proj_in = local(proj_hbm, proj_ref)
    wdn_copy = local(wdn_hbm, wdn)
    wup_copy = local(wup_hbm, wup_ref)
    depth_copy = local(depth_hbm, depth_ref)
    mask_copy = local(mask_hbm, mask_ref)
    conv_copy = local(conv_hbm.at[:, pl.ds(first_channel, 128), :], conv)

    tok_copy.wait()
    x_t = tok_ref[...].astype(F32).T
    xall[col] = x_t.astype(BF16)
    st_row[row] = jnp.concatenate(
        [
            jnp.sum(x_t, 0, keepdims=True),
            jnp.sum(x_t * x_t, 0, keepdims=True),
            jnp.zeros((6, STRIP), F32),
        ],
        axis=0,
    )
    own_half = pl.multiple_of(c * HALF, HALF)
    to_peer = pl.multiple_of(other * HALF, HALF)
    pl.semaphore_wait(barrier, len(row_peers) + len(col_peers))

    stat_copies = [remote(st_row.at[row], st_row.at[row], at_row(*peer)) for peer in row_peers]
    across = remote(xall.at[col], xall.at[col], at_col(1, 0))
    token_copies = [remote(xall.at[col], xall.at[col], at_col(0, dx)) for dx in (2, 1, 3)]
    proj_in.wait()
    wdn_copy.wait()
    wd_copy = remote(wdn.at[pl.ds(to_peer, HALF)], wd_peer, partner)
    proj_copy = remote(proj_ref, proj_peer, partner)

    @pl.loop(0, 8)
    def _(k):
        m_sum[k] = mm(wdn[pl.ds(pl.multiple_of(own_half + k * OWN, 64), OWN), :], proj_ref[...])

    across.wait_recv()
    came = xall.at[lax.rem(col + 4, 8)]
    token_copies += [remote(came, came, at_col(0, dx)) for dx in (2, 1, 3)]

    wd_copy.wait_recv()
    proj_copy.wait_recv()

    @pl.loop(0, 8)
    def _(k):
        more = mm(wd_peer[pl.ds(pl.multiple_of(k * OWN, 64), OWN), :], proj_peer[...])
        m_part[k] = (m_sum[k] + more).astype(BF16)

    m_copies = []
    for index, (dz, dh) in enumerate(chip_peers):
        m_copies.append(
            remote(m_part.at[zz(dz) * 2 + hh(dh)], m_recv.at[index], at_row(dz, dh, 0))
        )

    for copy in stat_copies:
        copy.wait_recv()
    total = st_row[0]
    for index in range(1, 16):
        total = total + st_row[index]
    mean = total[0:1] / WIDTH
    spread = total[1:2] / WIDTH - mean * mean
    depth_copy.wait()
    mask_copy.wait()
    depth = depth_ref[...].astype(F32)
    seen = mask_ref[...].astype(F32)
    st_col[col] = jnp.concatenate(
        [
            mean,
            lax.rsqrt(spread + EPS),
            jnp.concatenate([seen[0:1], seen[1:2]], axis=1),
            jnp.log(jnp.concatenate([depth[0:1], depth[1:2]], axis=1) * 0.001),
            jnp.zeros((4, STRIP), F32),
        ],
        axis=0,
    )
    norm_copies = [remote(st_col.at[col], st_col.at[col], at_col(*peer)) for peer in col_peers]

    feature_at = pl.multiple_of(c * FEAT, 128)
    wup_copy.wait()

    @pl.loop(0, HALF // 128)
    def _(i):
        at = pl.multiple_of(to_peer + i * 128, 128)
        w_send[pl.ds(pl.multiple_of(i * 128, 128), 128), :] = wup_ref[:, pl.ds(at, 128)].T

    w_copy = remote(w_send, w_t.at[:, pl.ds(feature_at, FEAT)], partner)

    @pl.loop(0, HALF // 128)
    def _(i):
        at = pl.multiple_of(own_half + i * 128, 128)
        w_t[pl.ds(pl.multiple_of(i * 128, 128), 128), pl.ds(feature_at, FEAT)] = wup_ref[:, pl.ds(at, 128)].T

    gain = jnp.broadcast_to(gain_ref[...].reshape(1, FEAT), (STRIP, FEAT)).T
    for copy in norm_copies:
        copy.wait_recv()
    for copy in token_copies:
        copy.wait_recv()

    n_copies = []
    for first in (0, 4):
        for index in range(first, first + 4):
            stats = st_col[index]
            n_t[pl.ds(feature_at, FEAT), index * STRIP : (index + 1) * STRIP] = (
                (xall[index].astype(F32) - stats[0:1]) * stats[1:2] * gain
            ).astype(BF16)
        half = n_t.at[pl.ds(feature_at, FEAT), first * STRIP : (first + 4) * STRIP]
        n_copies.append(remote(half, half, partner))
    w_copy.wait_recv()

    a_copies, b_copies = {}, {}

    def project(dz, into, first):
        base = pl.multiple_of(zz(dz) * 2 * OWN, 2 * OWN)

        @pl.loop(0, into.shape[3] // 256)
        def _(t):
            at = pl.multiple_of(t * 256, 256)
            both = mm(
                w_t[pl.ds(base, 2 * OWN), :], n_t[:, pl.ds(pl.multiple_of(first + at, 256), 256)]
            ).astype(BF16)
            into[zz(dz), 0, :, pl.ds(at, 256)] = both[:OWN]
            into[zz(dz), 1, :, pl.ds(at, 256)] = both[OWN:]

    up, down, flip = at_row(1, 0, 0), at_row(3, 0, 0), at_row(0, 1, 0)
    n_copies[0].wait_recv()
    project(2, p_a, 0)
    a_up = remote(p_a.at[zz(2), 0], a1.at[0], up)
    a_down = remote(p_a.at[zz(2), 1], a1.at[1], down)
    n_copies[1].wait_recv()

    def project_b(dz):
        project(dz, p_b, TA)
        b_copies[dz] = remote(p_b.at[zz(dz), 1 - h], b1.at[zz(dz)], flip)

    project_b(2)
    project(1, p_a, 0)
    a_up1 = remote(p_a.at[zz(1), 1], a2.at[0, 1], up)
    project(3, p_a, 0)
    a_down1 = remote(p_a.at[zz(3), 0], a2.at[1, 0], down)
    for dz in (1, 3, 0):
        project_b(dz)
    project(0, p_a, 0)

    def add(into, more):
        into[...] = (into[...].astype(F32) + more[...].astype(F32)).astype(BF16)

    a_up.wait_recv()
    add(p_a.at[zz(1), 0], a1.at[0])
    a_up2 = remote(p_a.at[zz(1), 0], a2.at[0, 0], up)
    a_down.wait_recv()
    add(p_a.at[zz(3), 1], a1.at[1])
    a_down2 = remote(p_a.at[zz(3), 1], a2.at[1, 1], down)

    b_copies[2].wait_recv()
    add(p_b.at[zz(2), h], b1.at[zz(2)])
    b_up = remote(p_b.at[zz(2), h, 0:96], b2.at[0], up)
    b_down = remote(p_b.at[zz(2), h, 96:192], b2.at[1], down)
    b_copies[1].wait_recv()
    add(p_b.at[zz(1), h], b1.at[zz(1)])
    b_copies[3].wait_recv()
    add(p_b.at[zz(3), h], b1.at[zz(3)])

    for copy in (a_up1, a_down1, a_up2, a_down2):
        copy.wait_recv()
    p_a[z, 1 - h] = (
        p_a[z, 1 - h].astype(F32) + a2[0, 1 - h].astype(F32) + a2[1, 1 - h].astype(F32)
    ).astype(BF16)
    a_flip = remote(p_a.at[z, 1 - h], a3, flip)

    b_up.wait_recv()
    add(p_b.at[zz(1), h, 0:96], b2.at[0])
    b_up2 = remote(p_b.at[zz(1), h], b3.at[0], up)
    b_down.wait_recv()
    add(p_b.at[zz(3), h, 96:192], b2.at[1])
    b_down2 = remote(p_b.at[zz(3), h], b3.at[1], down)

    for copy in m_copies:
        copy.wait_recv()
    total = m_part[here].astype(F32)
    for index in range(7):
        total = total + m_recv[index].astype(F32)
    m_own[...] = total.astype(BF16)
    gm[slot(0, 0)] = m_own[...]
    pair = {}

    def send(buf, dz, dh, device, rows=None):
        ref = buf.at[slot(dz, dh)] if rows is None else buf.at[slot(dz, dh), rows[0] : rows[1]]
        return remote(ref, ref, device)

    def share(name, buf, dz, dh, rows=None):
        pair[name] = send(buf, dz, dh, partner, rows)

    mf = send(gm, 0, 0, flip)
    mu = send(gm, 0, 0, up)
    md = send(gm, 0, 0, down)
    share(("gm", 0, 0, ""), gm, 0, 0)
    zc[...] = jnp.zeros_like(zc)
    zc[:, pl.ds(pl.multiple_of(col * STRIP, STRIP), STRIP)] = tn(proj_ref[...], xall[col])

    conv_copy.wait()
    head = head_ref[...]
    for k in range(9):
        taps[k] = jnp.broadcast_to(
            jnp.sum(conv[k].astype(F32) * head, axis=1, keepdims=True), (128, 128)
        )
    lane = lax.broadcasted_iota(jnp.int32, (128, CH), 1)
    sub = lax.broadcasted_iota(jnp.int32, (128, CH), 0)
    taps[9] = jnp.broadcast_to(
        jnp.sum(jnp.where(lane == sub + first_channel, head, 0.0), axis=1, keepdims=True), (128, 128)
    )

    lanes = (slice(0, TA), slice(TA, TOK))
    mine = pl.ds(pl.multiple_of(here * 16, 16), 16)
    mine_a, mine_b = ga.at[slot(0, 0)], gb.at[slot(0, 0)]
    top, low = (0, 96), (96, 192)

    def hidden(part):
        @pl.loop(0, TA // 256)
        def _(t):
            at = pl.ds(pl.multiple_of(part * TA + t * 256, 256), 256)
            value = pre[:, at]
            value = (value * cdf(value)).astype(BF16)
            hid[:, at] = value
            zc[:, at] = zc[:, at] + tn(m_own[...], value)

        at = lanes[part]
        z1[:, at] = zc[pl.ds(pl.multiple_of(other * 128, 128), 128), at].astype(BF16)
        return remote(z1.at[:, at], z1_recv.at[:, at], partner)

    def steep(part, into):
        @pl.loop(0, TA // 128)
        def _(t):
            at = pl.ds(pl.multiple_of(t * 128, 128), 128)
            into[:, at] = slope(
                pre[:, pl.ds(pl.multiple_of(part * TA + t * 128, 128), 128)]
            ).astype(BF16)

    def over_row(part, copy):
        at = lanes[part]
        copy.wait_recv()
        z2[:, at] = (
            zc[pl.ds(pl.multiple_of(c * 128, 128), 128), at] + z1_recv[:, at].astype(F32)
        ).astype(BF16)
        copies = []
        for index, (dz, dh) in enumerate(chip_peers):
            rows = pl.ds(pl.multiple_of((zz(dz) * 2 + hh(dh)) * 16, 16), 16)
            copies.append(remote(z2.at[rows, at], z2_recv.at[index, :, at], at_row(dz, dh, 0)))
        return copies

    def over_col(part, copies):
        at = lanes[part]
        total = z2[mine, at].astype(F32)
        for index, copy in enumerate(copies):
            copy.wait_recv()
            total = total + z2_recv[index, :, at].astype(F32)
        z3[col, :, at] = total.astype(BF16)
        return [remote(z3.at[col, :, at], z3.at[col, :, at], at_col(*peer)) for peer in col_peers]

    def to_row(part, copies):
        at = lanes[part]
        for copy in copies:
            copy.wait_recv()
        total = z3[0, :, at].astype(F32)
        for index in range(1, 8):
            total = total + z3[index, :, at].astype(F32)
        field[mine, at] = total.astype(BF16)
        return [
            remote(field.at[mine, at], field.at[mine, at], at_row(dz, dh, 0)) for dz, dh in chip_peers
        ]

    a_flip.wait_recv()
    pre[:, :TA] = (
        p_a[z, h].astype(F32) + a2[0, h].astype(F32) + a2[1, h].astype(F32) + a3[...].astype(F32)
    )
    z1_a = hidden(0)
    steep(0, mine_a)
    z2_a = over_row(0, z1_a)
    fa = send(ga, 0, 0, flip)
    au = send(ga, 0, 0, up)
    ad = send(ga, 0, 0, down)
    share(("ga", 0, 0, ""), ga, 0, 0)

    b_copies[0].wait_recv()
    b_up2.wait_recv()
    b_down2.wait_recv()
    pre[:, TA:] = (
        p_b[z, h].astype(F32) + b1[z].astype(F32) + b3[0].astype(F32) + b3[1].astype(F32)
    )
    z1_b = hidden(1)
    z3_a = over_col(0, z2_a)
    steep(1, mine_b)
    z2_b = over_row(1, z1_b)
    bu = send(gb, 0, 0, up)
    bd = send(gb, 0, 0, down)
    share(("gb", 0, 0, ""), gb, 0, 0)
    mf.wait_recv()
    mfu = send(gm, 0, 1, up)
    mfd = send(gm, 0, 1, down)
    share(("gm", 0, 1, ""), gm, 0, 1)
    mu.wait_recv()
    mu2 = send(gm, 3, 0, up)
    share(("gm", 3, 0, ""), gm, 3, 0)
    md.wait_recv()
    share(("gm", 1, 0, ""), gm, 1, 0)
    z4_a = to_row(0, z3_a)
    z3_b = over_col(1, z2_b)
    fb = send(gb, 0, 0, flip)
    fa.wait_recv()
    fau = send(ga, 0, 1, up)
    fad = send(ga, 0, 1, down)
    share(("ga", 0, 1, ""), ga, 0, 1)
    mfd.wait_recv()
    mfd2 = send(gm, 1, 1, down)
    share(("gm", 1, 1, ""), gm, 1, 1)
    mfu.wait_recv()
    share(("gm", 3, 1, ""), gm, 3, 1)
    bu.wait_recv()
    f_m = send(gb, 3, 0, flip)
    share(("gb", 3, 0, ""), gb, 3, 0)
    bd.wait_recv()
    f_p = send(gb, 1, 0, flip)
    share(("gb", 1, 0, ""), gb, 1, 0)
    z4_b = to_row(1, z3_b)
    bu2 = send(gb, 3, 0, up, top)
    bd2 = send(gb, 1, 0, down, low)
    au.wait_recv()
    au2 = send(ga, 3, 0, up)
    share(("ga", 3, 0, ""), ga, 3, 0)
    ad.wait_recv()
    share(("ga", 1, 0, ""), ga, 1, 0)
    fb.wait_recv()
    share(("gb", 0, 1, ""), gb, 0, 1)
    mu2.wait_recv()
    share(("gm", 2, 0, ""), gm, 2, 0)
    for copy in z4_a + z4_b:
        copy.wait_recv()

    token = lax.broadcasted_iota(jnp.int32, (1, TOK), 1)
    line, place = token >> 6, token & (GW - 1)

    def moved(values, di, dj):
        shift = di * GW + dj
        if shift:
            values = pltpu.roll(values, (-shift) % TOK, 1)
        inside = (
            (line + di >= 0) & (line + di < GH) & (place + dj >= 0) & (place + dj < GW)
        )
        return jnp.where(inside, values, 0.0)

    @pl.loop(0, TOK // 128)
    def _(t):
        at = pl.ds(pl.multiple_of(t * 128, 128), 128)
        value = field[:, at].astype(F32)
        act = (value * cdf(value)).astype(BF16).astype(F32)
        for k in range(9):
            shifted[k : k + 1, at] = jnp.sum(act * taps[k], axis=0, keepdims=True)
        shifted[9:10, at] = jnp.sum(value * taps[9], axis=0, keepdims=True)

    pred = shifted[9:10, :]
    for k in range(9):
        pred = pred + moved(shifted[k : k + 1, :], k // 3 - 1, k % 3 - 1)
    for index in range(8):
        rows_buf[index : index + 1, :] = pred[:, index * STRIP : (index + 1) * STRIP]
    pred_all[c] = rows_buf[...]
    pred_copy = remote(pred_all.at[c], pred_all.at[c], partner)
    mfd2.wait_recv()
    share(("gm", 2, 1, ""), gm, 2, 1)
    bu2.wait_recv()
    f_top = send(gb, 2, 0, flip, top)
    share(("gb", 2, 0, "top"), gb, 2, 0, top)
    bd2.wait_recv()
    f_low = send(gb, 2, 0, flip, low)
    share(("gb", 2, 0, "low"), gb, 2, 0, low)
    fad.wait_recv()
    fad2 = send(ga, 1, 1, down)
    share(("ga", 1, 1, ""), ga, 1, 1)
    fau.wait_recv()
    share(("ga", 3, 1, ""), ga, 3, 1)

    @pl.loop(0, TOK // 128)
    def _(t):
        at = pl.ds(pl.multiple_of(t * 128, 128), 128)
        field_slope[:, at] = slope(field[:, at].astype(F32))

    valid = jnp.concatenate([st_col[index][2:3] for index in range(8)], axis=0)
    target = jnp.concatenate([st_col[index][3:4] for index in range(8)], axis=0)
    pred_copy.wait_recv()
    err = valid * (pred_all[0] + pred_all[1] - target)

    def whole(values):
        return jnp.sum(jnp.sum(values, axis=1, keepdims=True), axis=0, keepdims=True)

    count = whole(valid)
    mean_err = whole(err) / count
    loss_ref[0, 0] = jnp.sum(whole(err * err) / count - FOCUS * mean_err * mean_err)
    grad_pred = valid * (2.0 * err - 2.0 * FOCUS * mean_err)
    grad_pred = jnp.concatenate([grad_pred[index : index + 1] for index in range(8)], axis=1)
    for k in range(9):
        shifted[k : k + 1, :] = moved(grad_pred, 1 - k // 3, 1 - k % 3)
    shifted[9:10, :] = grad_pred

    @pl.loop(0, TOK // 128)
    def _(t):
        at = pl.ds(pl.multiple_of(t * 128, 128), 128)
        back = taps[0] * shifted[0:1, at]
        for k in range(1, 9):
            back = back + taps[k] * shifted[k : k + 1, at]
        gz[pl.ds(first_channel, 128), at] = (
            taps[9] * shifted[9:10, at] + field_slope[:, at] * back
        ).astype(BF16)

    half_z = gz.at[pl.ds(first_channel, 128)]
    gz_copy = remote(half_z, half_z, partner)

    second_channel = pl.multiple_of(other * 128, 128)
    gh_own[:, pl.ds(first_channel, 128)] = nt(hid[...], half_z[...]).astype(BF16)
    gz_copy.wait_recv()
    gh_own[:, pl.ds(second_channel, 128)] = nt(
        hid[...], gz[pl.ds(second_channel, 128), :]
    ).astype(BF16)
    local(gh_own, gh_out.at[own_rows(0, 0)])
    gh_copies = [
        remote(gh_own, gh_out.at[own_rows(0, 0)], at_row(dz, dh, 0)) for dz, dh in chip_peers
    ]
    gh_pair = [remote(gh_own, gh_out.at[own_rows(0, 0)], partner)]
    def ready(dz):
        for key, copy in pair.items():
            if key[1] == dz:
                copy.wait_recv()

    n_mine = n_t.at[pl.ds(feature_at, FEAT)]

    def column(dz):
        @pl.loop(0, 2)
        def _(core):
            base = core * 8 + zz(dz) * 2
            for half in (0, 1):
                rows = slice(half * OWN, (half + 1) * OWN)
                weights = gm[base + half]
                grad[rows, :TA] = (
                    mm(weights, gz[:, :TA]) * ga[base + half].astype(F32)
                ).astype(BF16)
                grad[rows, TA:] = (
                    mm(weights, gz[:, TA:]) * gb[base + half].astype(F32)
                ).astype(BF16)
            up_own[dz, core] = nt(n_mine[...], grad[...])
            at = pl.multiple_of(base * OWN, 2 * OWN)
            pltpu.make_async_copy(
                up_own.at[dz, core], up_out.at[:, pl.ds(at, 2 * OWN)], out_sems.at[dz, core]
            ).start()

    f_m.wait_recv()
    share(("gb", 3, 1, ""), gb, 3, 1)
    f_p.wait_recv()
    share(("gb", 1, 1, ""), gb, 1, 1)
    ready(0)
    column(0)
    f_top.wait_recv()
    share(("gb", 2, 1, "top"), gb, 2, 1, top)
    f_low.wait_recv()
    share(("gb", 2, 1, "low"), gb, 2, 1, low)
    ready(3)
    column(3)
    au2.wait_recv()
    share(("ga", 2, 0, ""), ga, 2, 0)
    ready(1)
    column(1)
    fad2.wait_recv()
    share(("ga", 2, 1, ""), ga, 2, 1)
    ready(2)
    column(2)

    for (dz, dh), copy in zip(chip_peers, gh_copies):
        copy.wait_recv()
        came = gh_out.at[own_rows(-dz, dh)]
        gh_pair.append(remote(came, came, partner))
    for copy in gh_pair:
        copy.wait_recv()

    for dz in range(4):

        @pl.loop(0, 2)
        def _(core):
            at = pl.multiple_of((core * 8 + zz(dz) * 2) * OWN, 2 * OWN)
            pltpu.make_async_copy(
                up_own.at[dz, core], up_out.at[:, pl.ds(at, 2 * OWN)], out_sems.at[dz, core]
            ).wait()

    started[-1].wait()
    for copy in sent:
        copy.wait_send()


def weight_kernel(gh_hbm, proj_hbm, up_hbm, up_out, down_out, gh, proj, up, down, in_sems, out_sems):
    rows, lines = HID // N_DOWN, FEAT // N_UP

    def down_at(index):
        return pl.ds(index * rows, rows)

    def up_at(index):
        return pl.ds(index * lines, lines)

    proj_in = pltpu.make_async_copy(proj_hbm, proj, in_sems.at[0])
    gh_in = [
        pltpu.make_async_copy(gh_hbm.at[down_at(k)], gh.at[down_at(k)], in_sems.at[1 + k])
        for k in range(N_DOWN)
    ]
    up_in = [
        pltpu.make_async_copy(up_hbm.at[up_at(k)], up.at[up_at(k)], in_sems.at[1 + N_DOWN + k])
        for k in range(N_UP)
    ]
    for copy in [proj_in] + gh_in + up_in:
        copy.start()
    leaving = []
    proj_in.wait()
    for k in range(N_DOWN):
        gh_in[k].wait()
        down[down_at(k), :] = nt(gh[down_at(k), :], proj[...])
        leaving.append(
            pltpu.make_async_copy(down.at[down_at(k)], down_out.at[down_at(k)], out_sems.at[k])
        )
        leaving[-1].start()
    for k in range(N_UP):
        up_in[k].wait()
        leaving.append(
            pltpu.make_async_copy(up.at[up_at(k)], up_out.at[up_at(k)], out_sems.at[N_DOWN + k])
        )
        leaving[-1].start()
    for copy in leaving:
        copy.wait()


def on_device(tokens, ln_gain, w_up, w_down, proj, conv_kernel, head_weight, depth_mm, lidar_mask):
    vmem = pl.BlockSpec(memory_space=pltpu.VMEM)
    anywhere = pl.BlockSpec(memory_space=pl.ANY)
    up_held, grad_hidden, loss = pl.pallas_call(
        step_kernel,
        name="mlp_step",
        out_shape=[
            jax.ShapeDtypeStruct((FEAT, HID), F32),
            jax.ShapeDtypeStruct((HID, CH), BF16),
            jax.ShapeDtypeStruct((1, 1), F32),
        ],
        in_specs=[
            anywhere, vmem, anywhere, anywhere, anywhere, anywhere, vmem, anywhere, anywhere,
        ],
        out_specs=[anywhere, anywhere, pl.BlockSpec(memory_space=pltpu.SMEM)],
        scratch_shapes=[
            pltpu.VMEM((STRIP, FEAT), BF16),
            pltpu.VMEM((FEAT, HID), BF16),
            pltpu.VMEM((HID, FEAT), BF16),
            pltpu.VMEM((FEAT, CH), BF16),
            pltpu.VMEM((9, 128, CH), BF16),
            pltpu.VMEM((2, GW), jnp.int32),
            pltpu.VMEM((2, GW), jnp.int32),
            pltpu.VMEM((8, FEAT, STRIP), BF16),
            pltpu.VMEM((16, 8, STRIP), F32),
            pltpu.VMEM((8, 8, STRIP), F32),
            pltpu.VMEM((HALF, 2 * FEAT), BF16),
            pltpu.VMEM((HALF, FEAT), BF16),
            pltpu.VMEM((HALF, FEAT), BF16),
            pltpu.VMEM((FEAT, CH), BF16),
            pltpu.VMEM((2 * FEAT, TOK), BF16),
            pltpu.VMEM((8, OWN, CH), F32),
            pltpu.VMEM((8, OWN, CH), BF16),
            pltpu.VMEM((7, OWN, CH), BF16),
            pltpu.VMEM((OWN, CH), BF16),
            pltpu.VMEM((4, 2, OWN, TA), BF16),
            pltpu.VMEM((4, 2, OWN, TB), BF16),
            pltpu.VMEM((2, OWN, TA), BF16),
            pltpu.VMEM((2, 2, OWN, TA), BF16),
            pltpu.VMEM((OWN, TA), BF16),
            pltpu.VMEM((4, OWN, TB), BF16),
            pltpu.VMEM((2, OWN // 2, TB), BF16),
            pltpu.VMEM((2, OWN, TB), BF16),
            pltpu.VMEM((OWN, TOK), F32),
            pltpu.VMEM((OWN, TOK), BF16),
            pltpu.VMEM((CH, TOK), F32),
            pltpu.VMEM((128, TOK), BF16),
            pltpu.VMEM((128, TOK), BF16),
            pltpu.VMEM((128, TOK), BF16),
            pltpu.VMEM((7, 16, TOK), BF16),
            pltpu.VMEM((8, 16, TOK), BF16),
            pltpu.VMEM((10, 128, 128), F32),
            pltpu.VMEM((128, TOK), BF16),
            pltpu.VMEM((128, TOK), F32),
            pltpu.VMEM((16, TOK), F32),
            pltpu.VMEM((2, 8, STRIP), F32),
            pltpu.VMEM((8, STRIP), F32),
            pltpu.VMEM((CH, TOK), BF16),
            pltpu.VMEM((16, OWN, CH), BF16),
            pltpu.VMEM((16, OWN, TA), BF16),
            pltpu.VMEM((16, OWN, TB), BF16),
            pltpu.VMEM((OWN, CH), BF16),
            pltpu.VMEM((2 * OWN, TOK), BF16),
            pltpu.VMEM((4, 2, FEAT, 2 * OWN), F32),
            pltpu.SemaphoreType.DMA((N_SEMS,)),
            pltpu.SemaphoreType.DMA((N_SEMS,)),
            pltpu.SemaphoreType.DMA((9,)),
            pltpu.SemaphoreType.DMA((4, 2)),
        ],
        compiler_params=pltpu.CompilerParams(
            collective_id=0, has_side_effects=True, vmem_limit_bytes=60 * 2**20
        ),
        cost_estimate=pl.CostEstimate(flops=6 * 10**9, bytes_accessed=16 * 2**20, transcendentals=10**6),
    )(
        tokens, ln_gain, w_up, w_down, proj, conv_kernel.reshape(9, CH, CH),
        head_weight.reshape(1, CH), depth_mm, lidar_mask,
    )
    grad_up, grad_down = pl.pallas_call(
        weight_kernel,
        name="weight_grads",
        out_shape=[
            jax.ShapeDtypeStruct((FEAT, HID), F32),
            jax.ShapeDtypeStruct((HID, FEAT), F32),
        ],
        in_specs=[anywhere, anywhere, anywhere],
        out_specs=[anywhere, anywhere],
        scratch_shapes=[
            pltpu.VMEM((HID, CH), BF16),
            pltpu.VMEM((FEAT, CH), BF16),
            pltpu.VMEM((FEAT, HID), F32),
            pltpu.VMEM((HID, FEAT), F32),
            pltpu.SemaphoreType.DMA((1 + N_DOWN + N_UP,)),
            pltpu.SemaphoreType.DMA((N_DOWN + N_UP,)),
        ],
        compiler_params=pltpu.CompilerParams(vmem_limit_bytes=60 * 2**20),
        cost_estimate=pl.CostEstimate(flops=6 * 10**8, bytes_accessed=16 * 2**20, transcendentals=0),
    )(grad_hidden, proj, up_held)
    return (grad_up, grad_down, loss.reshape(()))


def solution(mesh):
    return jax.shard_map(
        on_device,
        mesh=mesh,
        in_specs=(
            P("col", "row"),
            P("row"),
            P("row", "col"),
            P("col", "row"),
            P("row", None),
            P(),
            P(),
            P("col", None),
            P("col", None),
        ),
        out_specs=(P("row", "col"), P("col", "row"), P()),
        check_vma=False,
    )
```

```python
import math

import jax
import jax.numpy as jnp
from jax import lax
from jax.experimental import pallas as pl
from jax.experimental.pallas import tpu as pltpu
from jax.sharding import PartitionSpec as P

MESH = pl.DeviceIdType.MESH
F32 = jnp.float32
BF16 = jnp.bfloat16

WIDTH = 6144
GW = 64
GH = 16
TOK = 1024
STRIP = 128
FEAT = 384
HID = 3072
HALF = 1536
OWN = 192
CH = 256
TA = 512
TB = TOK - TA
FOCUS = 0.85
EPS = 1e-06

ROOT_HALF = math.sqrt(0.5)
DENSITY = 1.0 / math.sqrt(2.0 * math.pi)

N_SEMS = 192
N_DOWN = 6
N_UP = 8


def cdf(v):
    return 0.5 * (1.0 + lax.erf(v * ROOT_HALF))


def slope(v):
    return cdf(v) + v * (DENSITY * jnp.exp(-0.5 * v * v))


def tn(a, b):
    return lax.dot_general(a, b, (((0,), (0,)), ((), ())), preferred_element_type=F32)


def nt(a, b):
    return lax.dot_general(a, b, (((1,), (1,)), ((), ())), preferred_element_type=F32)


def mm(a, b):
    return jnp.dot(a, b, preferred_element_type=F32)


def step_kernel(
    tok_hbm, gain_ref, wup_hbm, wdn_hbm, proj_hbm, conv_hbm, head_ref, depth_hbm, mask_hbm,
    up_out, gh_out, loss_ref,
    tok_ref, wup_ref, wdn, proj_ref, conv, depth_ref, mask_ref,
    xall, st_row, st_col, w_t, w_send, wd_peer, proj_peer, n_t, m_sum, m_part, m_recv, m_own,
    p_a, p_b, a1, a2, a3, b1, b2, b3, pre, hid, zc, z1, z1_recv, z2, z2_recv, z3,
    taps, field, field_slope, shifted, pred_all, rows_buf, gz, gm, ga, gb, gh_own, grad, up_own, send_sems, recv_sems, local_sems, out_sems,
):
    row, col = lax.axis_index("row"), lax.axis_index("col")
    z, h, c = row // 4, lax.rem(row // 2, 2), lax.rem(row, 2)
    used = [0]

    def zz(dz):
        return lax.rem(z + dz + 4, 4)

    def hh(dh):
        return lax.rem(h + dh, 2)

    def at_row(dz, dh, dc):
        return {"row": zz(dz) * 4 + hh(dh) * 2 + lax.rem(c + dc, 2)}

    def at_col(dl, dx):
        return {"col": lax.rem(col // 4 + dl, 2) * 4 + lax.rem(lax.rem(col, 4) + dx, 4)}

    def remote(src, dst, device):
        at = used[0]
        used[0] += 1
        copy = pltpu.make_async_remote_copy(
            src_ref=src, dst_ref=dst, send_sem=send_sems.at[at], recv_sem=recv_sems.at[at],
            device_id=device, device_id_type=MESH,
        )
        copy.start()
        sent.append(copy)
        return copy

    def slot(dz, dh):
        return c * 8 + zz(dz) * 2 + hh(dh)

    def own_rows(dz, dh):
        return pl.ds(pl.multiple_of(slot(dz, dh) * OWN, 64), OWN)

    sent = []
    row_peers = [
        (dz, dh, dc) for dz in (2, 1, 3, 0) for dh in (1, 0) for dc in (1, 0) if (dz, dh, dc) != (0, 0, 0)
    ]
    chip_peers = [(dz, dh) for dz in (2, 1, 3, 0) for dh in (1, 0) if (dz, dh) != (0, 0)]
    col_peers = [(dl, dx) for dl in (1, 0) for dx in (2, 1, 3, 0) if (dl, dx) != (0, 0)]
    partner = at_row(0, 0, 1)
    here = z * 2 + h
    other = 1 - c

    barrier = pltpu.get_barrier_semaphore()
    for peer in row_peers:
        pl.semaphore_signal(barrier, inc=1, device_id=at_row(*peer), device_id_type=MESH)
    for peer in col_peers:
        pl.semaphore_signal(barrier, inc=1, device_id=at_col(*peer), device_id_type=MESH)

    started = []

    def local(src, dst):
        copy = pltpu.make_async_copy(src, dst, local_sems.at[len(started)])
        copy.start()
        started.append(copy)
        return copy

    first_channel = pl.multiple_of(c * 128, 128)
    tok_copy = local(tok_hbm, tok_ref)
    proj_in = local(proj_hbm, proj_ref)
    wdn_copy = local(wdn_hbm, wdn)
    wup_copy = local(wup_hbm, wup_ref)
    depth_copy = local(depth_hbm, depth_ref)
    mask_copy = local(mask_hbm, mask_ref)
    conv_copy = local(conv_hbm.at[:, pl.ds(first_channel, 128), :], conv)

    tok_copy.wait()
    x_t = tok_ref[...].astype(F32).T
    xall[col] = x_t.astype(BF16)
    st_row[row] = jnp.concatenate(
        [
            jnp.sum(x_t, 0, keepdims=True),
            jnp.sum(x_t * x_t, 0, keepdims=True),
            jnp.zeros((6, STRIP), F32),
        ],
        axis=0,
    )
    own_half = pl.multiple_of(c * HALF, HALF)
    to_peer = pl.multiple_of(other * HALF, HALF)
    pl.semaphore_wait(barrier, len(row_peers) + len(col_peers))

    stat_copies = [remote(st_row.at[row], st_row.at[row], at_row(*peer)) for peer in row_peers]
    across = remote(xall.at[col], xall.at[col], at_col(1, 0))
    token_copies = [remote(xall.at[col], xall.at[col], at_col(0, dx)) for dx in (2, 1, 3)]
    proj_in.wait()
    wdn_copy.wait()
    wd_copy = remote(wdn.at[pl.ds(to_peer, HALF)], wd_peer, partner)
    proj_copy = remote(proj_ref, proj_peer, partner)

    @pl.loop(0, 8)
    def _(k):
        m_sum[k] = mm(wdn[pl.ds(pl.multiple_of(own_half + k * OWN, 64), OWN), :], proj_ref[...])

    across.wait_recv()
    came = xall.at[lax.rem(col + 4, 8)]
    token_copies += [remote(came, came, at_col(0, dx)) for dx in (2, 1, 3)]

    wd_copy.wait_recv()
    proj_copy.wait_recv()

    @pl.loop(0, 8)
    def _(k):
        more = mm(wd_peer[pl.ds(pl.multiple_of(k * OWN, 64), OWN), :], proj_peer[...])
        m_part[k] = (m_sum[k] + more).astype(BF16)

    m_copies = []
    for index, (dz, dh) in enumerate(chip_peers):
        m_copies.append(
            remote(m_part.at[zz(dz) * 2 + hh(dh)], m_recv.at[index], at_row(dz, dh, 0))
        )

    for copy in stat_copies:
        copy.wait_recv()
    total = st_row[0]
    for index in range(1, 16):
        total = total + st_row[index]
    mean = total[0:1] / WIDTH
    spread = total[1:2] / WIDTH - mean * mean
    depth_copy.wait()
    mask_copy.wait()
    depth = depth_ref[...].astype(F32)
    seen = mask_ref[...].astype(F32)
    st_col[col] = jnp.concatenate(
        [
            mean,
            lax.rsqrt(spread + EPS),
            jnp.concatenate([seen[0:1], seen[1:2]], axis=1),
            jnp.log(jnp.concatenate([depth[0:1], depth[1:2]], axis=1) * 0.001),
            jnp.zeros((4, STRIP), F32),
        ],
        axis=0,
    )
    norm_copies = [remote(st_col.at[col], st_col.at[col], at_col(*peer)) for peer in col_peers]

    feature_at = pl.multiple_of(c * FEAT, 128)
    wup_copy.wait()

    @pl.loop(0, HALF // 128)
    def _(i):
        at = pl.multiple_of(to_peer + i * 128, 128)
        w_send[pl.ds(pl.multiple_of(i * 128, 128), 128), :] = wup_ref[:, pl.ds(at, 128)].T

    w_copy = remote(w_send, w_t.at[:, pl.ds(feature_at, FEAT)], partner)

    @pl.loop(0, HALF // 128)
    def _(i):
        at = pl.multiple_of(own_half + i * 128, 128)
        w_t[pl.ds(pl.multiple_of(i * 128, 128), 128), pl.ds(feature_at, FEAT)] = wup_ref[:, pl.ds(at, 128)].T

    gain = jnp.broadcast_to(gain_ref[...].reshape(1, FEAT), (STRIP, FEAT)).T
    for copy in norm_copies:
        copy.wait_recv()
    for copy in token_copies:
        copy.wait_recv()

    n_copies = []
    for first in (0, 4):
        for index in range(first, first + 4):
            stats = st_col[index]
            n_t[pl.ds(feature_at, FEAT), index * STRIP : (index + 1) * STRIP] = (
                (xall[index].astype(F32) - stats[0:1]) * stats[1:2] * gain
            ).astype(BF16)
        half = n_t.at[pl.ds(feature_at, FEAT), first * STRIP : (first + 4) * STRIP]
        n_copies.append(remote(half, half, partner))
    w_copy.wait_recv()

    a_copies, b_copies = {}, {}

    def project(dz, into, first):
        base = pl.multiple_of(zz(dz) * 2 * OWN, 2 * OWN)

        @pl.loop(0, into.shape[3] // 256)
        def _(t):
            at = pl.multiple_of(t * 256, 256)
            both = mm(
                w_t[pl.ds(base, 2 * OWN), :], n_t[:, pl.ds(pl.multiple_of(first + at, 256), 256)]
            ).astype(BF16)
            into[zz(dz), 0, :, pl.ds(at, 256)] = both[:OWN]
            into[zz(dz), 1, :, pl.ds(at, 256)] = both[OWN:]

    up, down, flip = at_row(1, 0, 0), at_row(3, 0, 0), at_row(0, 1, 0)
    n_copies[0].wait_recv()
    project(2, p_a, 0)
    a_up = remote(p_a.at[zz(2), 0], a1.at[0], up)
    a_down = remote(p_a.at[zz(2), 1], a1.at[1], down)
    n_copies[1].wait_recv()

    def project_b(dz):
        project(dz, p_b, TA)
        b_copies[dz] = remote(p_b.at[zz(dz), 1 - h], b1.at[zz(dz)], flip)

    project_b(2)
    project(1, p_a, 0)
    a_up1 = remote(p_a.at[zz(1), 1], a2.at[0, 1], up)
    project(3, p_a, 0)
    a_down1 = remote(p_a.at[zz(3), 0], a2.at[1, 0], down)
    for dz in (1, 3, 0):
        project_b(dz)
    project(0, p_a, 0)

    def add(into, more):
        into[...] = (into[...].astype(F32) + more[...].astype(F32)).astype(BF16)

    a_up.wait_recv()
    add(p_a.at[zz(1), 0], a1.at[0])
    a_up2 = remote(p_a.at[zz(1), 0], a2.at[0, 0], up)
    a_down.wait_recv()
    add(p_a.at[zz(3), 1], a1.at[1])
    a_down2 = remote(p_a.at[zz(3), 1], a2.at[1, 1], down)

    b_copies[2].wait_recv()
    add(p_b.at[zz(2), h], b1.at[zz(2)])
    b_up = remote(p_b.at[zz(2), h, 0:96], b2.at[0], up)
    b_down = remote(p_b.at[zz(2), h, 96:192], b2.at[1], down)
    b_copies[1].wait_recv()
    add(p_b.at[zz(1), h], b1.at[zz(1)])
    b_copies[3].wait_recv()
    add(p_b.at[zz(3), h], b1.at[zz(3)])

    for copy in (a_up1, a_down1, a_up2, a_down2):
        copy.wait_recv()
    p_a[z, 1 - h] = (
        p_a[z, 1 - h].astype(F32) + a2[0, 1 - h].astype(F32) + a2[1, 1 - h].astype(F32)
    ).astype(BF16)
    a_flip = remote(p_a.at[z, 1 - h], a3, flip)

    b_up.wait_recv()
    add(p_b.at[zz(1), h, 0:96], b2.at[0])
    b_up2 = remote(p_b.at[zz(1), h], b3.at[0], up)
    b_down.wait_recv()
    add(p_b.at[zz(3), h, 96:192], b2.at[1])
    b_down2 = remote(p_b.at[zz(3), h], b3.at[1], down)

    for copy in m_copies:
        copy.wait_recv()
    total = m_part[here].astype(F32)
    for index in range(7):
        total = total + m_recv[index].astype(F32)
    m_own[...] = total.astype(BF16)
    gm[slot(0, 0)] = m_own[...]
    pair = {}

    def send(buf, dz, dh, device, rows=None):
        ref = buf.at[slot(dz, dh)] if rows is None else buf.at[slot(dz, dh), rows[0] : rows[1]]
        return remote(ref, ref, device)

    def share(name, buf, dz, dh, rows=None):
        pair[name] = send(buf, dz, dh, partner, rows)

    mf = send(gm, 0, 0, flip)
    mu = send(gm, 0, 0, up)
    md = send(gm, 0, 0, down)
    share(("gm", 0, 0, ""), gm, 0, 0)
    zc[...] = jnp.zeros_like(zc)
    zc[:, pl.ds(pl.multiple_of(col * STRIP, STRIP), STRIP)] = tn(proj_ref[...], xall[col])

    conv_copy.wait()
    head = head_ref[...]
    for k in range(9):
        taps[k] = jnp.broadcast_to(
            jnp.sum(conv[k].astype(F32) * head, axis=1, keepdims=True), (128, 128)
        )
    lane = lax.broadcasted_iota(jnp.int32, (128, CH), 1)
    sub = lax.broadcasted_iota(jnp.int32, (128, CH), 0)
    taps[9] = jnp.broadcast_to(
        jnp.sum(jnp.where(lane == sub + first_channel, head, 0.0), axis=1, keepdims=True), (128, 128)
    )

    mine_a, mine_b = ga.at[slot(0, 0)], gb.at[slot(0, 0)]

    def hidden(part):
        @pl.loop(0, TA // 256)
        def _(t):
            at = pl.ds(pl.multiple_of(part * TA + t * 256, 256), 256)
            value = pre[:, at]
            value = (value * cdf(value)).astype(BF16)
            hid[:, at] = value
            zc[:, at] = zc[:, at] + tn(m_own[...], value)

    a_flip.wait_recv()
    pre[:, :TA] = (
        p_a[z, h].astype(F32) + a2[0, h].astype(F32) + a2[1, h].astype(F32) + a3[...].astype(F32)
    )
    hidden(0)

    @pl.loop(0, TA // 128)
    def _(t):
        at = pl.ds(pl.multiple_of(t * 128, 128), 128)
        mine_a[:, at] = slope(pre[:, at]).astype(BF16)

    b_copies[0].wait_recv()
    b_up2.wait_recv()
    b_down2.wait_recv()
    pre[:, TA:] = (
        p_b[z, h].astype(F32) + b1[z].astype(F32) + b3[0].astype(F32) + b3[1].astype(F32)
    )
    hidden(1)

    z1[...] = zc[pl.ds(pl.multiple_of(other * 128, 128), 128), :].astype(BF16)
    z1_copy = remote(z1, z1_recv, partner)

    mf.wait_recv()
    mfu = send(gm, 0, 1, up)
    mfd = send(gm, 0, 1, down)
    share(("gm", 0, 1, ""), gm, 0, 1)
    top, low = (0, 96), (96, 192)

    @pl.loop(0, TB // 128)
    def _(t):
        at = pl.ds(pl.multiple_of(t * 128, 128), 128)
        mine_b[:, at] = slope(pre[:, pl.ds(pl.multiple_of(TA + t * 128, 128), 128)]).astype(BF16)

    z1_copy.wait_recv()
    z2[...] = (
        zc[pl.ds(pl.multiple_of(c * 128, 128), 128), :] + z1_recv[...].astype(F32)
    ).astype(BF16)
    z2_copies = []
    for index, (dz, dh) in enumerate(chip_peers):
        at = pl.multiple_of((zz(dz) * 2 + hh(dh)) * 16, 16)
        z2_copies.append(remote(z2.at[pl.ds(at, 16)], z2_recv.at[index], at_row(dz, dh, 0)))
    bu = send(gb, 0, 0, up)
    bd = send(gb, 0, 0, down)
    mu.wait_recv()
    mu2 = send(gm, 3, 0, up)
    share(("gm", 3, 0, ""), gm, 3, 0)
    md.wait_recv()
    share(("gm", 1, 0, ""), gm, 1, 0)
    share(("gb", 0, 0, ""), gb, 0, 0)

    fa = send(ga, 0, 0, flip)
    mfd.wait_recv()
    mfd2 = send(gm, 1, 1, down)
    share(("gm", 1, 1, ""), gm, 1, 1)
    mfu.wait_recv()
    share(("gm", 3, 1, ""), gm, 3, 1)
    share(("ga", 0, 0, ""), ga, 0, 0)
    mine = pl.ds(pl.multiple_of(here * 16, 16), 16)
    part = z2[mine, :].astype(F32)
    for index, copy in enumerate(z2_copies):
        copy.wait_recv()
        part = part + z2_recv[index].astype(F32)
    z3[col] = part.astype(BF16)
    z3_copies = [remote(z3.at[col], z3.at[col], at_col(*peer)) for peer in col_peers]
    au = send(ga, 0, 0, up)
    ad = send(ga, 0, 0, down)
    fb = send(gb, 0, 0, flip)
    bu.wait_recv()
    bu2 = send(gb, 3, 0, up, top)
    share(("gb", 3, 0, ""), gb, 3, 0)
    bd.wait_recv()
    bd2 = send(gb, 1, 0, down, low)
    share(("gb", 1, 0, ""), gb, 1, 0)
    for copy in z3_copies:
        copy.wait_recv()
    total = z3[0].astype(F32)
    for index in range(1, 8):
        total = total + z3[index].astype(F32)
    field[mine, :] = total.astype(BF16)
    z4_copies = [
        remote(field.at[mine], field.at[mine], at_row(dz, dh, 0)) for dz, dh in chip_peers
    ]
    f_m = send(gb, 3, 0, flip)
    f_p = send(gb, 1, 0, flip)
    fa.wait_recv()
    fau = send(ga, 0, 1, up)
    fad = send(ga, 0, 1, down)
    share(("ga", 0, 1, ""), ga, 0, 1)
    au.wait_recv()
    au2 = send(ga, 3, 0, up)
    share(("ga", 3, 0, ""), ga, 3, 0)
    ad.wait_recv()
    share(("ga", 1, 0, ""), ga, 1, 0)
    fb.wait_recv()
    share(("gb", 0, 1, ""), gb, 0, 1)
    bu2.wait_recv()
    f_top = send(gb, 2, 0, flip, top)
    share(("gb", 2, 0, "top"), gb, 2, 0, top)
    bd2.wait_recv()
    f_low = send(gb, 2, 0, flip, low)
    share(("gb", 2, 0, "low"), gb, 2, 0, low)
    mu2.wait_recv()
    share(("gm", 2, 0, ""), gm, 2, 0)
    mfd2.wait_recv()
    share(("gm", 2, 1, ""), gm, 2, 1)
    for copy in z4_copies:
        copy.wait_recv()

    token = lax.broadcasted_iota(jnp.int32, (1, TOK), 1)
    line, place = token >> 6, token & (GW - 1)

    def moved(values, di, dj):
        shift = di * GW + dj
        if shift:
            values = pltpu.roll(values, (-shift) % TOK, 1)
        inside = (
            (line + di >= 0) & (line + di < GH) & (place + dj >= 0) & (place + dj < GW)
        )
        return jnp.where(inside, values, 0.0)

    @pl.loop(0, TOK // 128)
    def _(t):
        at = pl.ds(pl.multiple_of(t * 128, 128), 128)
        value = field[:, at].astype(F32)
        act = (value * cdf(value)).astype(BF16).astype(F32)
        for k in range(9):
            shifted[k : k + 1, at] = jnp.sum(act * taps[k], axis=0, keepdims=True)
        shifted[9:10, at] = jnp.sum(value * taps[9], axis=0, keepdims=True)

    pred = shifted[9:10, :]
    for k in range(9):
        pred = pred + moved(shifted[k : k + 1, :], k // 3 - 1, k % 3 - 1)
    for index in range(8):
        rows_buf[index : index + 1, :] = pred[:, index * STRIP : (index + 1) * STRIP]
    pred_all[c] = rows_buf[...]
    pred_copy = remote(pred_all.at[c], pred_all.at[c], partner)
    fad.wait_recv()
    fad2 = send(ga, 1, 1, down)
    share(("ga", 1, 1, ""), ga, 1, 1)
    fau.wait_recv()
    share(("ga", 3, 1, ""), ga, 3, 1)

    @pl.loop(0, TOK // 128)
    def _(t):
        at = pl.ds(pl.multiple_of(t * 128, 128), 128)
        field_slope[:, at] = slope(field[:, at].astype(F32))

    valid = jnp.concatenate([st_col[index][2:3] for index in range(8)], axis=0)
    target = jnp.concatenate([st_col[index][3:4] for index in range(8)], axis=0)
    pred_copy.wait_recv()
    err = valid * (pred_all[0] + pred_all[1] - target)

    def whole(values):
        return jnp.sum(jnp.sum(values, axis=1, keepdims=True), axis=0, keepdims=True)

    count = whole(valid)
    mean_err = whole(err) / count
    loss_ref[0, 0] = jnp.sum(whole(err * err) / count - FOCUS * mean_err * mean_err)
    grad_pred = valid * (2.0 * err - 2.0 * FOCUS * mean_err)
    grad_pred = jnp.concatenate([grad_pred[index : index + 1] for index in range(8)], axis=1)
    for k in range(9):
        shifted[k : k + 1, :] = moved(grad_pred, 1 - k // 3, 1 - k % 3)
    shifted[9:10, :] = grad_pred

    @pl.loop(0, TOK // 128)
    def _(t):
        at = pl.ds(pl.multiple_of(t * 128, 128), 128)
        back = taps[0] * shifted[0:1, at]
        for k in range(1, 9):
            back = back + taps[k] * shifted[k : k + 1, at]
        gz[pl.ds(first_channel, 128), at] = (
            taps[9] * shifted[9:10, at] + field_slope[:, at] * back
        ).astype(BF16)

    half_z = gz.at[pl.ds(first_channel, 128)]
    gz_copy = remote(half_z, half_z, partner)

    second_channel = pl.multiple_of(other * 128, 128)
    gh_own[:, pl.ds(first_channel, 128)] = nt(hid[...], half_z[...]).astype(BF16)
    gz_copy.wait_recv()
    gh_own[:, pl.ds(second_channel, 128)] = nt(
        hid[...], gz[pl.ds(second_channel, 128), :]
    ).astype(BF16)
    local(gh_own, gh_out.at[own_rows(0, 0)])
    gh_copies = [
        remote(gh_own, gh_out.at[own_rows(0, 0)], at_row(dz, dh, 0)) for dz, dh in chip_peers
    ]
    gh_pair = [remote(gh_own, gh_out.at[own_rows(0, 0)], partner)]
    def ready(dz):
        for key, copy in pair.items():
            if key[1] == dz:
                copy.wait_recv()

    n_mine = n_t.at[pl.ds(feature_at, FEAT)]

    def column(dz):
        @pl.loop(0, 2)
        def _(core):
            base = core * 8 + zz(dz) * 2
            for half in (0, 1):
                rows = slice(half * OWN, (half + 1) * OWN)
                weights = gm[base + half]
                grad[rows, :TA] = (
                    mm(weights, gz[:, :TA]) * ga[base + half].astype(F32)
                ).astype(BF16)
                grad[rows, TA:] = (
                    mm(weights, gz[:, TA:]) * gb[base + half].astype(F32)
                ).astype(BF16)
            up_own[dz, core] = nt(n_mine[...], grad[...])
            at = pl.multiple_of(base * OWN, 2 * OWN)
            pltpu.make_async_copy(
                up_own.at[dz, core], up_out.at[:, pl.ds(at, 2 * OWN)], out_sems.at[dz, core]
            ).start()

    f_m.wait_recv()
    share(("gb", 3, 1, ""), gb, 3, 1)
    f_p.wait_recv()
    share(("gb", 1, 1, ""), gb, 1, 1)
    ready(0)
    column(0)
    f_top.wait_recv()
    share(("gb", 2, 1, "top"), gb, 2, 1, top)
    f_low.wait_recv()
    share(("gb", 2, 1, "low"), gb, 2, 1, low)
    ready(3)
    column(3)
    au2.wait_recv()
    share(("ga", 2, 0, ""), ga, 2, 0)
    ready(1)
    column(1)
    fad2.wait_recv()
    share(("ga", 2, 1, ""), ga, 2, 1)
    ready(2)
    column(2)

    for (dz, dh), copy in zip(chip_peers, gh_copies):
        copy.wait_recv()
        came = gh_out.at[own_rows(-dz, dh)]
        gh_pair.append(remote(came, came, partner))
    for copy in gh_pair:
        copy.wait_recv()

    for dz in range(4):

        @pl.loop(0, 2)
        def _(core):
            at = pl.multiple_of((core * 8 + zz(dz) * 2) * OWN, 2 * OWN)
            pltpu.make_async_copy(
                up_own.at[dz, core], up_out.at[:, pl.ds(at, 2 * OWN)], out_sems.at[dz, core]
            ).wait()

    started[-1].wait()
    for copy in sent:
        copy.wait_send()


def weight_kernel(gh_hbm, proj_hbm, up_hbm, up_out, down_out, gh, proj, up, down, in_sems, out_sems):
    rows, lines = HID // N_DOWN, FEAT // N_UP

    def down_at(index):
        return pl.ds(index * rows, rows)

    def up_at(index):
        return pl.ds(index * lines, lines)

    proj_in = pltpu.make_async_copy(proj_hbm, proj, in_sems.at[0])
    gh_in = [
        pltpu.make_async_copy(gh_hbm.at[down_at(k)], gh.at[down_at(k)], in_sems.at[1 + k])
        for k in range(N_DOWN)
    ]
    up_in = [
        pltpu.make_async_copy(up_hbm.at[up_at(k)], up.at[up_at(k)], in_sems.at[1 + N_DOWN + k])
        for k in range(N_UP)
    ]
    for copy in [proj_in] + gh_in + up_in:
        copy.start()
    leaving = []
    proj_in.wait()
    for k in range(N_DOWN):
        gh_in[k].wait()
        down[down_at(k), :] = nt(gh[down_at(k), :], proj[...])
        leaving.append(
            pltpu.make_async_copy(down.at[down_at(k)], down_out.at[down_at(k)], out_sems.at[k])
        )
        leaving[-1].start()
    for k in range(N_UP):
        up_in[k].wait()
        leaving.append(
            pltpu.make_async_copy(up.at[up_at(k)], up_out.at[up_at(k)], out_sems.at[N_DOWN + k])
        )
        leaving[-1].start()
    for copy in leaving:
        copy.wait()


def on_device(tokens, ln_gain, w_up, w_down, proj, conv_kernel, head_weight, depth_mm, lidar_mask):
    vmem = pl.BlockSpec(memory_space=pltpu.VMEM)
    anywhere = pl.BlockSpec(memory_space=pl.ANY)
    up_held, grad_hidden, loss = pl.pallas_call(
        step_kernel,
        name="mlp_step",
        out_shape=[
            jax.ShapeDtypeStruct((FEAT, HID), F32),
            jax.ShapeDtypeStruct((HID, CH), BF16),
            jax.ShapeDtypeStruct((1, 1), F32),
        ],
        in_specs=[
            anywhere, vmem, anywhere, anywhere, anywhere, anywhere, vmem, anywhere, anywhere,
        ],
        out_specs=[anywhere, anywhere, pl.BlockSpec(memory_space=pltpu.SMEM)],
        scratch_shapes=[
            pltpu.VMEM((STRIP, FEAT), BF16),
            pltpu.VMEM((FEAT, HID), BF16),
            pltpu.VMEM((HID, FEAT), BF16),
            pltpu.VMEM((FEAT, CH), BF16),
            pltpu.VMEM((9, 128, CH), BF16),
            pltpu.VMEM((2, GW), jnp.int32),
            pltpu.VMEM((2, GW), jnp.int32),
            pltpu.VMEM((8, FEAT, STRIP), BF16),
            pltpu.VMEM((16, 8, STRIP), F32),
            pltpu.VMEM((8, 8, STRIP), F32),
            pltpu.VMEM((HALF, 2 * FEAT), BF16),
            pltpu.VMEM((HALF, FEAT), BF16),
            pltpu.VMEM((HALF, FEAT), BF16),
            pltpu.VMEM((FEAT, CH), BF16),
            pltpu.VMEM((2 * FEAT, TOK), BF16),
            pltpu.VMEM((8, OWN, CH), F32),
            pltpu.VMEM((8, OWN, CH), BF16),
            pltpu.VMEM((7, OWN, CH), BF16),
            pltpu.VMEM((OWN, CH), BF16),
            pltpu.VMEM((4, 2, OWN, TA), BF16),
            pltpu.VMEM((4, 2, OWN, TB), BF16),
            pltpu.VMEM((2, OWN, TA), BF16),
            pltpu.VMEM((2, 2, OWN, TA), BF16),
            pltpu.VMEM((OWN, TA), BF16),
            pltpu.VMEM((4, OWN, TB), BF16),
            pltpu.VMEM((2, OWN // 2, TB), BF16),
            pltpu.VMEM((2, OWN, TB), BF16),
            pltpu.VMEM((OWN, TOK), F32),
            pltpu.VMEM((OWN, TOK), BF16),
            pltpu.VMEM((CH, TOK), F32),
            pltpu.VMEM((128, TOK), BF16),
            pltpu.VMEM((128, TOK), BF16),
            pltpu.VMEM((128, TOK), BF16),
            pltpu.VMEM((7, 16, TOK), BF16),
            pltpu.VMEM((8, 16, TOK), BF16),
            pltpu.VMEM((10, 128, 128), F32),
            pltpu.VMEM((128, TOK), BF16),
            pltpu.VMEM((128, TOK), F32),
            pltpu.VMEM((16, TOK), F32),
            pltpu.VMEM((2, 8, STRIP), F32),
            pltpu.VMEM((8, STRIP), F32),
            pltpu.VMEM((CH, TOK), BF16),
            pltpu.VMEM((16, OWN, CH), BF16),
            pltpu.VMEM((16, OWN, TA), BF16),
            pltpu.VMEM((16, OWN, TB), BF16),
            pltpu.VMEM((OWN, CH), BF16),
            pltpu.VMEM((2 * OWN, TOK), BF16),
            pltpu.VMEM((4, 2, FEAT, 2 * OWN), F32),
            pltpu.SemaphoreType.DMA((N_SEMS,)),
            pltpu.SemaphoreType.DMA((N_SEMS,)),
            pltpu.SemaphoreType.DMA((9,)),
            pltpu.SemaphoreType.DMA((4, 2)),
        ],
        compiler_params=pltpu.CompilerParams(
            collective_id=0, has_side_effects=True, vmem_limit_bytes=60 * 2**20
        ),
        cost_estimate=pl.CostEstimate(flops=6 * 10**9, bytes_accessed=16 * 2**20, transcendentals=10**6),
    )(
        tokens, ln_gain, w_up, w_down, proj, conv_kernel.reshape(9, CH, CH),
        head_weight.reshape(1, CH), depth_mm, lidar_mask,
    )
    grad_up, grad_down = pl.pallas_call(
        weight_kernel,
        name="weight_grads",
        out_shape=[
            jax.ShapeDtypeStruct((FEAT, HID), F32),
            jax.ShapeDtypeStruct((HID, FEAT), F32),
        ],
        in_specs=[anywhere, anywhere, anywhere],
        out_specs=[anywhere, anywhere],
        scratch_shapes=[
            pltpu.VMEM((HID, CH), BF16),
            pltpu.VMEM((FEAT, CH), BF16),
            pltpu.VMEM((FEAT, HID), F32),
            pltpu.VMEM((HID, FEAT), F32),
            pltpu.SemaphoreType.DMA((1 + N_DOWN + N_UP,)),
            pltpu.SemaphoreType.DMA((N_DOWN + N_UP,)),
        ],
        compiler_params=pltpu.CompilerParams(vmem_limit_bytes=60 * 2**20),
        cost_estimate=pl.CostEstimate(flops=6 * 10**8, bytes_accessed=16 * 2**20, transcendentals=0),
    )(grad_hidden, proj, up_held)
    return (grad_up, grad_down, loss.reshape(()))


def solution(mesh):
    return jax.shard_map(
        on_device,
        mesh=mesh,
        in_specs=(
            P("col", "row"),
            P("row"),
            P("row", "col"),
            P("col", "row"),
            P("row", None),
            P(),
            P(),
            P("col", None),
            P("col", None),
        ),
        out_specs=(P("row", "col"), P("col", "row"), P()),
        check_vma=False,
    )
```

```python
import math

import jax
import jax.numpy as jnp
from jax import lax
from jax.experimental import pallas as pl
from jax.experimental.pallas import tpu as pltpu
from jax.sharding import PartitionSpec as P

MESH = pl.DeviceIdType.MESH
F32 = jnp.float32
BF16 = jnp.bfloat16

WIDTH = 6144
GW = 64
GH = 16
TOK = 1024
STRIP = 128
FEAT = 384
HID = 3072
HALF = 1536
OWN = 192
CH = 256
TA = 512
TB = TOK - TA
FOCUS = 0.85
EPS = 1e-06

ROOT_HALF = math.sqrt(0.5)
DENSITY = 1.0 / math.sqrt(2.0 * math.pi)

N_SEMS = 192
N_DOWN = 6
N_UP = 8


def cdf(v):
    return 0.5 * (1.0 + lax.erf(v * ROOT_HALF))


def slope(v):
    return cdf(v) + v * (DENSITY * jnp.exp(-0.5 * v * v))


def tn(a, b):
    return lax.dot_general(a, b, (((0,), (0,)), ((), ())), preferred_element_type=F32)


def nt(a, b):
    return lax.dot_general(a, b, (((1,), (1,)), ((), ())), preferred_element_type=F32)


def mm(a, b):
    return jnp.dot(a, b, preferred_element_type=F32)


def step_kernel(
    tok_hbm, gain_ref, wup_hbm, wdn_hbm, proj_hbm, conv_hbm, head_ref, depth_hbm, mask_hbm,
    up_out, gh_out, loss_ref,
    tok_ref, wup_ref, wdn, proj_ref, conv, depth_ref, mask_ref,
    xall, st_row, st_col, w_t, w_send, wd_peer, proj_peer, n_t, m_sum, m_part, m_recv, m_own,
    p_a, p_b, a1, a2, a3, b1, b2, b3, pre, hid, zc, z1, z1_recv, z2, z2_recv, z3,
    taps, field, field_slope, shifted, pred_all, rows_buf, gz, gm, ga, gb, gh_own, grad, up_own, send_sems, recv_sems, local_sems, out_sems,
):
    row, col = lax.axis_index("row"), lax.axis_index("col")
    z, h, c = row // 4, lax.rem(row // 2, 2), lax.rem(row, 2)
    used = [0]

    def zz(dz):
        return lax.rem(z + dz + 4, 4)

    def hh(dh):
        return lax.rem(h + dh, 2)

    def at_row(dz, dh, dc):
        return {"row": zz(dz) * 4 + hh(dh) * 2 + lax.rem(c + dc, 2)}

    def at_col(dl, dx):
        return {"col": lax.rem(col // 4 + dl, 2) * 4 + lax.rem(lax.rem(col, 4) + dx, 4)}

    def remote(src, dst, device):
        at = used[0]
        used[0] += 1
        copy = pltpu.make_async_remote_copy(
            src_ref=src, dst_ref=dst, send_sem=send_sems.at[at], recv_sem=recv_sems.at[at],
            device_id=device, device_id_type=MESH,
        )
        copy.start()
        sent.append(copy)
        return copy

    def slot(dz, dh):
        return c * 8 + zz(dz) * 2 + hh(dh)

    def own_rows(dz, dh):
        return pl.ds(pl.multiple_of(slot(dz, dh) * OWN, 64), OWN)

    sent = []
    row_peers = [
        (dz, dh, dc) for dz in (2, 1, 3, 0) for dh in (1, 0) for dc in (1, 0) if (dz, dh, dc) != (0, 0, 0)
    ]
    chip_peers = [(dz, dh) for dz in (2, 1, 3, 0) for dh in (1, 0) if (dz, dh) != (0, 0)]
    col_peers = [(dl, dx) for dl in (1, 0) for dx in (2, 1, 3, 0) if (dl, dx) != (0, 0)]
    partner = at_row(0, 0, 1)
    here = z * 2 + h
    other = 1 - c

    barrier = pltpu.get_barrier_semaphore()
    for peer in row_peers:
        pl.semaphore_signal(barrier, inc=1, device_id=at_row(*peer), device_id_type=MESH)
    for peer in col_peers:
        pl.semaphore_signal(barrier, inc=1, device_id=at_col(*peer), device_id_type=MESH)

    started = []

    def local(src, dst):
        copy = pltpu.make_async_copy(src, dst, local_sems.at[len(started)])
        copy.start()
        started.append(copy)
        return copy

    first_channel = pl.multiple_of(c * 128, 128)
    tok_copy = local(tok_hbm, tok_ref)
    proj_in = local(proj_hbm, proj_ref)
    wdn_copy = local(wdn_hbm, wdn)
    wup_copy = local(wup_hbm, wup_ref)
    depth_copy = local(depth_hbm, depth_ref)
    mask_copy = local(mask_hbm, mask_ref)
    conv_copy = local(conv_hbm.at[:, pl.ds(first_channel, 128), :], conv)

    tok_copy.wait()
    x_t = tok_ref[...].astype(F32).T
    xall[col] = x_t.astype(BF16)
    st_row[row] = jnp.concatenate(
        [
            jnp.sum(x_t, 0, keepdims=True),
            jnp.sum(x_t * x_t, 0, keepdims=True),
            jnp.zeros((6, STRIP), F32),
        ],
        axis=0,
    )
    own_half = pl.multiple_of(c * HALF, HALF)
    to_peer = pl.multiple_of(other * HALF, HALF)
    pl.semaphore_wait(barrier, len(row_peers) + len(col_peers))

    stat_copies = [remote(st_row.at[row], st_row.at[row], at_row(*peer)) for peer in row_peers]
    across = remote(xall.at[col], xall.at[col], at_col(1, 0))
    token_copies = [remote(xall.at[col], xall.at[col], at_col(0, dx)) for dx in (2, 1, 3)]
    proj_in.wait()
    wdn_copy.wait()
    wd_copy = remote(wdn.at[pl.ds(to_peer, HALF)], wd_peer, partner)
    proj_copy = remote(proj_ref, proj_peer, partner)

    @pl.loop(0, 8)
    def _(k):
        m_sum[k] = mm(wdn[pl.ds(pl.multiple_of(own_half + k * OWN, 64), OWN), :], proj_ref[...])

    across.wait_recv()
    came = xall.at[lax.rem(col + 4, 8)]
    token_copies += [remote(came, came, at_col(0, dx)) for dx in (2, 1, 3)]

    wd_copy.wait_recv()
    proj_copy.wait_recv()

    @pl.loop(0, 8)
    def _(k):
        more = mm(wd_peer[pl.ds(pl.multiple_of(k * OWN, 64), OWN), :], proj_peer[...])
        m_part[k] = (m_sum[k] + more).astype(BF16)

    m_copies = []
    for index, (dz, dh) in enumerate(chip_peers):
        m_copies.append(
            remote(m_part.at[zz(dz) * 2 + hh(dh)], m_recv.at[index], at_row(dz, dh, 0))
        )

    for copy in stat_copies:
        copy.wait_recv()
    total = st_row[0]
    for index in range(1, 16):
        total = total + st_row[index]
    mean = total[0:1] / WIDTH
    spread = total[1:2] / WIDTH - mean * mean
    depth_copy.wait()
    mask_copy.wait()
    depth = depth_ref[...].astype(F32)
    seen = mask_ref[...].astype(F32)
    st_col[col] = jnp.concatenate(
        [
            mean,
            lax.rsqrt(spread + EPS),
            jnp.concatenate([seen[0:1], seen[1:2]], axis=1),
            jnp.log(jnp.concatenate([depth[0:1], depth[1:2]], axis=1) * 0.001),
            jnp.zeros((4, STRIP), F32),
        ],
        axis=0,
    )
    norm_copies = [remote(st_col.at[col], st_col.at[col], at_col(*peer)) for peer in col_peers]

    feature_at = pl.multiple_of(c * FEAT, 128)
    wup_copy.wait()

    @pl.loop(0, HALF // 128)
    def _(i):
        at = pl.multiple_of(to_peer + i * 128, 128)
        w_send[pl.ds(pl.multiple_of(i * 128, 128), 128), :] = wup_ref[:, pl.ds(at, 128)].T

    w_copy = remote(w_send, w_t.at[:, pl.ds(feature_at, FEAT)], partner)

    @pl.loop(0, HALF // 128)
    def _(i):
        at = pl.multiple_of(own_half + i * 128, 128)
        w_t[pl.ds(pl.multiple_of(i * 128, 128), 128), pl.ds(feature_at, FEAT)] = wup_ref[:, pl.ds(at, 128)].T

    gain = jnp.broadcast_to(gain_ref[...].reshape(1, FEAT), (STRIP, FEAT)).T
    for copy in norm_copies:
        copy.wait_recv()
    for copy in token_copies:
        copy.wait_recv()

    n_copies = []
    for first in (0, 4):
        for index in range(first, first + 4):
            stats = st_col[index]
            n_t[pl.ds(feature_at, FEAT), index * STRIP : (index + 1) * STRIP] = (
                (xall[index].astype(F32) - stats[0:1]) * stats[1:2] * gain
            ).astype(BF16)
        half = n_t.at[pl.ds(feature_at, FEAT), first * STRIP : (first + 4) * STRIP]
        n_copies.append(remote(half, half, partner))
    w_copy.wait_recv()

    a_copies, b_copies = {}, {}

    def project(dz, into, first):
        base = pl.multiple_of(zz(dz) * 2 * OWN, 2 * OWN)

        @pl.loop(0, into.shape[3] // 256)
        def _(t):
            at = pl.multiple_of(t * 256, 256)
            both = mm(
                w_t[pl.ds(base, 2 * OWN), :], n_t[:, pl.ds(pl.multiple_of(first + at, 256), 256)]
            ).astype(BF16)
            into[zz(dz), 0, :, pl.ds(at, 256)] = both[:OWN]
            into[zz(dz), 1, :, pl.ds(at, 256)] = both[OWN:]

    up, down, flip = at_row(1, 0, 0), at_row(3, 0, 0), at_row(0, 1, 0)
    n_copies[0].wait_recv()
    project(2, p_a, 0)
    a_up = remote(p_a.at[zz(2), 0], a1.at[0], up)
    a_down = remote(p_a.at[zz(2), 1], a1.at[1], down)
    n_copies[1].wait_recv()

    def project_b(dz):
        project(dz, p_b, TA)
        b_copies[dz] = remote(p_b.at[zz(dz), 1 - h], b1.at[zz(dz)], flip)

    project_b(2)
    project(1, p_a, 0)
    a_up1 = remote(p_a.at[zz(1), 1], a2.at[0, 1], up)
    project(3, p_a, 0)
    a_down1 = remote(p_a.at[zz(3), 0], a2.at[1, 0], down)
    for dz in (1, 3, 0):
        project_b(dz)
    project(0, p_a, 0)

    def add(into, more):
        into[...] = (into[...].astype(F32) + more[...].astype(F32)).astype(BF16)

    a_up.wait_recv()
    add(p_a.at[zz(1), 0], a1.at[0])
    a_up2 = remote(p_a.at[zz(1), 0], a2.at[0, 0], up)
    a_down.wait_recv()
    add(p_a.at[zz(3), 1], a1.at[1])
    a_down2 = remote(p_a.at[zz(3), 1], a2.at[1, 1], down)

    b_copies[2].wait_recv()
    add(p_b.at[zz(2), h], b1.at[zz(2)])
    b_up = remote(p_b.at[zz(2), h, 0:96], b2.at[0], up)
    b_down = remote(p_b.at[zz(2), h, 96:192], b2.at[1], down)
    b_copies[1].wait_recv()
    add(p_b.at[zz(1), h], b1.at[zz(1)])
    b_copies[3].wait_recv()
    add(p_b.at[zz(3), h], b1.at[zz(3)])

    for copy in (a_up1, a_down1, a_up2, a_down2):
        copy.wait_recv()
    p_a[z, 1 - h] = (
        p_a[z, 1 - h].astype(F32) + a2[0, 1 - h].astype(F32) + a2[1, 1 - h].astype(F32)
    ).astype(BF16)
    a_flip = remote(p_a.at[z, 1 - h], a3, flip)

    b_up.wait_recv()
    add(p_b.at[zz(1), h, 0:96], b2.at[0])
    b_up2 = remote(p_b.at[zz(1), h], b3.at[0], up)
    b_down.wait_recv()
    add(p_b.at[zz(3), h, 96:192], b2.at[1])
    b_down2 = remote(p_b.at[zz(3), h], b3.at[1], down)

    for copy in m_copies:
        copy.wait_recv()
    total = m_part[here].astype(F32)
    for index in range(7):
        total = total + m_recv[index].astype(F32)
    m_own[...] = total.astype(BF16)
    gm[slot(0, 0)] = m_own[...]
    pair = {}

    def send(buf, dz, dh, device, rows=None):
        ref = buf.at[slot(dz, dh)] if rows is None else buf.at[slot(dz, dh), rows[0] : rows[1]]
        return remote(ref, ref, device)

    def share(name, buf, dz, dh, rows=None):
        pair[name] = send(buf, dz, dh, partner, rows)

    mf = send(gm, 0, 0, flip)
    mu = send(gm, 0, 0, up)
    md = send(gm, 0, 0, down)
    share(("gm", 0, 0, ""), gm, 0, 0)
    x_proj = tn(proj_ref[...], xall[col])

    conv_copy.wait()
    head = head_ref[...]
    for k in range(9):
        taps[k] = jnp.broadcast_to(
            jnp.sum(conv[k].astype(F32) * head, axis=1, keepdims=True), (128, 128)
        )
    lane = lax.broadcasted_iota(jnp.int32, (128, CH), 1)
    sub = lax.broadcasted_iota(jnp.int32, (128, CH), 0)
    taps[9] = jnp.broadcast_to(
        jnp.sum(jnp.where(lane == sub + first_channel, head, 0.0), axis=1, keepdims=True), (128, 128)
    )

    b_copies[0].wait_recv()
    a_flip.wait_recv()
    pre[:, :TA] = (
        p_a[z, h].astype(F32) + a2[0, h].astype(F32) + a2[1, h].astype(F32) + a3[...].astype(F32)
    )
    b_up2.wait_recv()
    b_down2.wait_recv()
    pre[:, TA:] = (
        p_b[z, h].astype(F32) + b1[z].astype(F32) + b3[0].astype(F32) + b3[1].astype(F32)
    )

    @pl.loop(0, TOK // 128)
    def _(t):
        at = pl.ds(pl.multiple_of(t * 128, 128), 128)
        value = pre[:, at]
        hid[:, at] = (value * cdf(value)).astype(BF16)

    @pl.loop(0, TOK // 256)
    def _(t):
        at = pl.ds(pl.multiple_of(t * 256, 256), 256)
        zc[:, at] = tn(m_own[...], hid[:, at])

    strip = pl.ds(pl.multiple_of(col * STRIP, STRIP), STRIP)
    zc[:, strip] = zc[:, strip] + x_proj

    z1[...] = zc[pl.ds(pl.multiple_of(other * 128, 128), 128), :].astype(BF16)
    z1_copy = remote(z1, z1_recv, partner)

    mine_a, mine_b = ga.at[slot(0, 0)], gb.at[slot(0, 0)]
    mf.wait_recv()
    mfu = send(gm, 0, 1, up)
    mfd = send(gm, 0, 1, down)
    share(("gm", 0, 1, ""), gm, 0, 1)
    top, low = (0, 96), (96, 192)

    @pl.loop(0, TB // 128)
    def _(t):
        at = pl.ds(pl.multiple_of(t * 128, 128), 128)
        mine_b[:, at] = slope(pre[:, pl.ds(pl.multiple_of(TA + t * 128, 128), 128)]).astype(BF16)

    z1_copy.wait_recv()
    z2[...] = (
        zc[pl.ds(pl.multiple_of(c * 128, 128), 128), :] + z1_recv[...].astype(F32)
    ).astype(BF16)
    z2_copies = []
    for index, (dz, dh) in enumerate(chip_peers):
        at = pl.multiple_of((zz(dz) * 2 + hh(dh)) * 16, 16)
        z2_copies.append(remote(z2.at[pl.ds(at, 16)], z2_recv.at[index], at_row(dz, dh, 0)))
    bu = send(gb, 0, 0, up)
    bd = send(gb, 0, 0, down)
    mu.wait_recv()
    mu2 = send(gm, 3, 0, up)
    share(("gm", 3, 0, ""), gm, 3, 0)
    md.wait_recv()
    share(("gm", 1, 0, ""), gm, 1, 0)
    share(("gb", 0, 0, ""), gb, 0, 0)

    @pl.loop(0, TA // 128)
    def _(t):
        at = pl.ds(pl.multiple_of(t * 128, 128), 128)
        mine_a[:, at] = slope(pre[:, at]).astype(BF16)

    fa = send(ga, 0, 0, flip)
    mfd.wait_recv()
    mfd2 = send(gm, 1, 1, down)
    share(("gm", 1, 1, ""), gm, 1, 1)
    mfu.wait_recv()
    share(("gm", 3, 1, ""), gm, 3, 1)
    share(("ga", 0, 0, ""), ga, 0, 0)
    mine = pl.ds(pl.multiple_of(here * 16, 16), 16)
    part = z2[mine, :].astype(F32)
    for index, copy in enumerate(z2_copies):
        copy.wait_recv()
        part = part + z2_recv[index].astype(F32)
    z3[col] = part.astype(BF16)
    z3_copies = [remote(z3.at[col], z3.at[col], at_col(*peer)) for peer in col_peers]
    au = send(ga, 0, 0, up)
    ad = send(ga, 0, 0, down)
    fb = send(gb, 0, 0, flip)
    bu.wait_recv()
    bu2 = send(gb, 3, 0, up, top)
    share(("gb", 3, 0, ""), gb, 3, 0)
    bd.wait_recv()
    bd2 = send(gb, 1, 0, down, low)
    share(("gb", 1, 0, ""), gb, 1, 0)
    for copy in z3_copies:
        copy.wait_recv()
    total = z3[0].astype(F32)
    for index in range(1, 8):
        total = total + z3[index].astype(F32)
    field[mine, :] = total.astype(BF16)
    z4_copies = [
        remote(field.at[mine], field.at[mine], at_row(dz, dh, 0)) for dz, dh in chip_peers
    ]
    f_m = send(gb, 3, 0, flip)
    f_p = send(gb, 1, 0, flip)
    fa.wait_recv()
    fau = send(ga, 0, 1, up)
    fad = send(ga, 0, 1, down)
    share(("ga", 0, 1, ""), ga, 0, 1)
    au.wait_recv()
    au2 = send(ga, 3, 0, up)
    share(("ga", 3, 0, ""), ga, 3, 0)
    ad.wait_recv()
    share(("ga", 1, 0, ""), ga, 1, 0)
    fb.wait_recv()
    share(("gb", 0, 1, ""), gb, 0, 1)
    bu2.wait_recv()
    f_top = send(gb, 2, 0, flip, top)
    share(("gb", 2, 0, "top"), gb, 2, 0, top)
    bd2.wait_recv()
    f_low = send(gb, 2, 0, flip, low)
    share(("gb", 2, 0, "low"), gb, 2, 0, low)
    mu2.wait_recv()
    share(("gm", 2, 0, ""), gm, 2, 0)
    mfd2.wait_recv()
    share(("gm", 2, 1, ""), gm, 2, 1)
    for copy in z4_copies:
        copy.wait_recv()

    token = lax.broadcasted_iota(jnp.int32, (1, TOK), 1)
    line, place = token >> 6, token & (GW - 1)

    def moved(values, di, dj):
        shift = di * GW + dj
        if shift:
            values = pltpu.roll(values, (-shift) % TOK, 1)
        inside = (
            (line + di >= 0) & (line + di < GH) & (place + dj >= 0) & (place + dj < GW)
        )
        return jnp.where(inside, values, 0.0)

    @pl.loop(0, TOK // 128)
    def _(t):
        at = pl.ds(pl.multiple_of(t * 128, 128), 128)
        value = field[:, at].astype(F32)
        act = (value * cdf(value)).astype(BF16).astype(F32)
        for k in range(9):
            shifted[k : k + 1, at] = jnp.sum(act * taps[k], axis=0, keepdims=True)
        shifted[9:10, at] = jnp.sum(value * taps[9], axis=0, keepdims=True)

    pred = shifted[9:10, :]
    for k in range(9):
        pred = pred + moved(shifted[k : k + 1, :], k // 3 - 1, k % 3 - 1)
    for index in range(8):
        rows_buf[index : index + 1, :] = pred[:, index * STRIP : (index + 1) * STRIP]
    pred_all[c] = rows_buf[...]
    pred_copy = remote(pred_all.at[c], pred_all.at[c], partner)
    fad.wait_recv()
    fad2 = send(ga, 1, 1, down)
    share(("ga", 1, 1, ""), ga, 1, 1)
    fau.wait_recv()
    share(("ga", 3, 1, ""), ga, 3, 1)

    @pl.loop(0, TOK // 128)
    def _(t):
        at = pl.ds(pl.multiple_of(t * 128, 128), 128)
        field_slope[:, at] = slope(field[:, at].astype(F32))

    valid = jnp.concatenate([st_col[index][2:3] for index in range(8)], axis=0)
    target = jnp.concatenate([st_col[index][3:4] for index in range(8)], axis=0)
    pred_copy.wait_recv()
    err = valid * (pred_all[0] + pred_all[1] - target)

    def whole(values):
        return jnp.sum(jnp.sum(values, axis=1, keepdims=True), axis=0, keepdims=True)

    count = whole(valid)
    mean_err = whole(err) / count
    loss_ref[0, 0] = jnp.sum(whole(err * err) / count - FOCUS * mean_err * mean_err)
    grad_pred = valid * (2.0 * err - 2.0 * FOCUS * mean_err)
    grad_pred = jnp.concatenate([grad_pred[index : index + 1] for index in range(8)], axis=1)
    for k in range(9):
        shifted[k : k + 1, :] = moved(grad_pred, 1 - k // 3, 1 - k % 3)
    shifted[9:10, :] = grad_pred

    @pl.loop(0, TOK // 128)
    def _(t):
        at = pl.ds(pl.multiple_of(t * 128, 128), 128)
        back = taps[0] * shifted[0:1, at]
        for k in range(1, 9):
            back = back + taps[k] * shifted[k : k + 1, at]
        gz[pl.ds(first_channel, 128), at] = (
            taps[9] * shifted[9:10, at] + field_slope[:, at] * back
        ).astype(BF16)

    half_z = gz.at[pl.ds(first_channel, 128)]
    gz_copy = remote(half_z, half_z, partner)

    second_channel = pl.multiple_of(other * 128, 128)
    gh_own[:, pl.ds(first_channel, 128)] = nt(hid[...], half_z[...]).astype(BF16)
    gz_copy.wait_recv()
    gh_own[:, pl.ds(second_channel, 128)] = nt(
        hid[...], gz[pl.ds(second_channel, 128), :]
    ).astype(BF16)
    local(gh_own, gh_out.at[own_rows(0, 0)])
    gh_flip = {0: remote(gh_own, gh_out.at[own_rows(0, 0)], flip)}
    gh_copies = {
        dz: remote(gh_own, gh_out.at[own_rows(0, 0)], at_row(dz, 0, 0)) for dz in (2, 1, 3)
    }
    gh_pair = [remote(gh_own, gh_out.at[own_rows(0, 0)], partner)]
    def ready(dz):
        for key, copy in pair.items():
            if key[1] == dz:
                copy.wait_recv()

    n_mine = n_t.at[pl.ds(feature_at, FEAT)]

    def column(dz):
        @pl.loop(0, 2)
        def _(core):
            base = core * 8 + zz(dz) * 2
            for half in (0, 1):
                rows = slice(half * OWN, (half + 1) * OWN)
                weights = gm[base + half]
                grad[rows, :TA] = (
                    mm(weights, gz[:, :TA]) * ga[base + half].astype(F32)
                ).astype(BF16)
                grad[rows, TA:] = (
                    mm(weights, gz[:, TA:]) * gb[base + half].astype(F32)
                ).astype(BF16)
            up_own[dz, core] = nt(n_mine[...], grad[...])
            at = pl.multiple_of(base * OWN, 2 * OWN)
            pltpu.make_async_copy(
                up_own.at[dz, core], up_out.at[:, pl.ds(at, 2 * OWN)], out_sems.at[dz, core]
            ).start()

    f_m.wait_recv()
    share(("gb", 3, 1, ""), gb, 3, 1)
    f_p.wait_recv()
    share(("gb", 1, 1, ""), gb, 1, 1)
    ready(0)
    column(0)
    f_top.wait_recv()
    share(("gb", 2, 1, "top"), gb, 2, 1, top)
    f_low.wait_recv()
    share(("gb", 2, 1, "low"), gb, 2, 1, low)
    ready(3)
    column(3)
    au2.wait_recv()
    share(("ga", 2, 0, ""), ga, 2, 0)
    ready(1)
    column(1)
    fad2.wait_recv()
    share(("ga", 2, 1, ""), ga, 2, 1)
    for dz, copy in gh_copies.items():
        copy.wait_recv()
        came = gh_out.at[own_rows(-dz, 0)]
        gh_flip[dz] = remote(came, came, flip)
        gh_pair.append(remote(came, came, partner))
    ready(2)
    column(2)

    for dz, copy in gh_flip.items():
        copy.wait_recv()
        came = gh_out.at[own_rows(-dz, 1)]
        gh_pair.append(remote(came, came, partner))
    for copy in gh_pair:
        copy.wait_recv()

    for dz in range(4):

        @pl.loop(0, 2)
        def _(core):
            at = pl.multiple_of((core * 8 + zz(dz) * 2) * OWN, 2 * OWN)
            pltpu.make_async_copy(
                up_own.at[dz, core], up_out.at[:, pl.ds(at, 2 * OWN)], out_sems.at[dz, core]
            ).wait()

    started[-1].wait()
    for copy in sent:
        copy.wait_send()


def weight_kernel(gh_hbm, proj_hbm, up_hbm, up_out, down_out, gh, proj, up, down, in_sems, out_sems):
    rows, lines = HID // N_DOWN, FEAT // N_UP

    def down_at(index):
        return pl.ds(index * rows, rows)

    def up_at(index):
        return pl.ds(index * lines, lines)

    proj_in = pltpu.make_async_copy(proj_hbm, proj, in_sems.at[0])
    gh_in = [
        pltpu.make_async_copy(gh_hbm.at[down_at(k)], gh.at[down_at(k)], in_sems.at[1 + k])
        for k in range(N_DOWN)
    ]
    up_in = [
        pltpu.make_async_copy(up_hbm.at[up_at(k)], up.at[up_at(k)], in_sems.at[1 + N_DOWN + k])
        for k in range(N_UP)
    ]
    for copy in [proj_in] + gh_in + up_in:
        copy.start()
    leaving = []
    proj_in.wait()
    for k in range(N_DOWN):
        gh_in[k].wait()
        down[down_at(k), :] = nt(gh[down_at(k), :], proj[...])
        leaving.append(
            pltpu.make_async_copy(down.at[down_at(k)], down_out.at[down_at(k)], out_sems.at[k])
        )
        leaving[-1].start()
    for k in range(N_UP):
        up_in[k].wait()
        leaving.append(
            pltpu.make_async_copy(up.at[up_at(k)], up_out.at[up_at(k)], out_sems.at[N_DOWN + k])
        )
        leaving[-1].start()
    for copy in leaving:
        copy.wait()


def on_device(tokens, ln_gain, w_up, w_down, proj, conv_kernel, head_weight, depth_mm, lidar_mask):
    vmem = pl.BlockSpec(memory_space=pltpu.VMEM)
    anywhere = pl.BlockSpec(memory_space=pl.ANY)
    up_held, grad_hidden, loss = pl.pallas_call(
        step_kernel,
        name="mlp_step",
        out_shape=[
            jax.ShapeDtypeStruct((FEAT, HID), F32),
            jax.ShapeDtypeStruct((HID, CH), BF16),
            jax.ShapeDtypeStruct((1, 1), F32),
        ],
        in_specs=[
            anywhere, vmem, anywhere, anywhere, anywhere, anywhere, vmem, anywhere, anywhere,
        ],
        out_specs=[anywhere, anywhere, pl.BlockSpec(memory_space=pltpu.SMEM)],
        scratch_shapes=[
            pltpu.VMEM((STRIP, FEAT), BF16),
            pltpu.VMEM((FEAT, HID), BF16),
            pltpu.VMEM((HID, FEAT), BF16),
            pltpu.VMEM((FEAT, CH), BF16),
            pltpu.VMEM((9, 128, CH), BF16),
            pltpu.VMEM((2, GW), jnp.int32),
            pltpu.VMEM((2, GW), jnp.int32),
            pltpu.VMEM((8, FEAT, STRIP), BF16),
            pltpu.VMEM((16, 8, STRIP), F32),
            pltpu.VMEM((8, 8, STRIP), F32),
            pltpu.VMEM((HALF, 2 * FEAT), BF16),
            pltpu.VMEM((HALF, FEAT), BF16),
            pltpu.VMEM((HALF, FEAT), BF16),
            pltpu.VMEM((FEAT, CH), BF16),
            pltpu.VMEM((2 * FEAT, TOK), BF16),
            pltpu.VMEM((8, OWN, CH), F32),
            pltpu.VMEM((8, OWN, CH), BF16),
            pltpu.VMEM((7, OWN, CH), BF16),
            pltpu.VMEM((OWN, CH), BF16),
            pltpu.VMEM((4, 2, OWN, TA), BF16),
            pltpu.VMEM((4, 2, OWN, TB), BF16),
            pltpu.VMEM((2, OWN, TA), BF16),
            pltpu.VMEM((2, 2, OWN, TA), BF16),
            pltpu.VMEM((OWN, TA), BF16),
            pltpu.VMEM((4, OWN, TB), BF16),
            pltpu.VMEM((2, OWN // 2, TB), BF16),
            pltpu.VMEM((2, OWN, TB), BF16),
            pltpu.VMEM((OWN, TOK), F32),
            pltpu.VMEM((OWN, TOK), BF16),
            pltpu.VMEM((CH, TOK), F32),
            pltpu.VMEM((128, TOK), BF16),
            pltpu.VMEM((128, TOK), BF16),
            pltpu.VMEM((128, TOK), BF16),
            pltpu.VMEM((7, 16, TOK), BF16),
            pltpu.VMEM((8, 16, TOK), BF16),
            pltpu.VMEM((10, 128, 128), F32),
            pltpu.VMEM((128, TOK), BF16),
            pltpu.VMEM((128, TOK), F32),
            pltpu.VMEM((16, TOK), F32),
            pltpu.VMEM((2, 8, STRIP), F32),
            pltpu.VMEM((8, STRIP), F32),
            pltpu.VMEM((CH, TOK), BF16),
            pltpu.VMEM((16, OWN, CH), BF16),
            pltpu.VMEM((16, OWN, TA), BF16),
            pltpu.VMEM((16, OWN, TB), BF16),
            pltpu.VMEM((OWN, CH), BF16),
            pltpu.VMEM((2 * OWN, TOK), BF16),
            pltpu.VMEM((4, 2, FEAT, 2 * OWN), F32),
            pltpu.SemaphoreType.DMA((N_SEMS,)),
            pltpu.SemaphoreType.DMA((N_SEMS,)),
            pltpu.SemaphoreType.DMA((9,)),
            pltpu.SemaphoreType.DMA((4, 2)),
        ],
        compiler_params=pltpu.CompilerParams(
            collective_id=0, has_side_effects=True, vmem_limit_bytes=60 * 2**20
        ),
        cost_estimate=pl.CostEstimate(flops=6 * 10**9, bytes_accessed=16 * 2**20, transcendentals=10**6),
    )(
        tokens, ln_gain, w_up, w_down, proj, conv_kernel.reshape(9, CH, CH),
        head_weight.reshape(1, CH), depth_mm, lidar_mask,
    )
    grad_up, grad_down = pl.pallas_call(
        weight_kernel,
        name="weight_grads",
        out_shape=[
            jax.ShapeDtypeStruct((FEAT, HID), F32),
            jax.ShapeDtypeStruct((HID, FEAT), F32),
        ],
        in_specs=[anywhere, anywhere, anywhere],
        out_specs=[anywhere, anywhere],
        scratch_shapes=[
            pltpu.VMEM((HID, CH), BF16),
            pltpu.VMEM((FEAT, CH), BF16),
            pltpu.VMEM((FEAT, HID), F32),
            pltpu.VMEM((HID, FEAT), F32),
            pltpu.SemaphoreType.DMA((1 + N_DOWN + N_UP,)),
            pltpu.SemaphoreType.DMA((N_DOWN + N_UP,)),
        ],
        compiler_params=pltpu.CompilerParams(vmem_limit_bytes=60 * 2**20),
        cost_estimate=pl.CostEstimate(flops=6 * 10**8, bytes_accessed=16 * 2**20, transcendentals=0),
    )(grad_hidden, proj, up_held)
    return (grad_up, grad_down, loss.reshape(()))


def solution(mesh):
    return jax.shard_map(
        on_device,
        mesh=mesh,
        in_specs=(
            P("col", "row"),
            P("row"),
            P("row", "col"),
            P("col", "row"),
            P("row", None),
            P(),
            P(),
            P("col", None),
            P("col", None),
        ),
        out_specs=(P("row", "col"), P("col", "row"), P()),
        check_vma=False,
    )
```

```python
import math

import jax
import jax.numpy as jnp
from jax import lax
from jax.experimental import pallas as pl
from jax.experimental.pallas import tpu as pltpu
from jax.sharding import PartitionSpec as P

MESH = pl.DeviceIdType.MESH
F32 = jnp.float32
BF16 = jnp.bfloat16

WIDTH = 6144
GW = 64
GH = 16
TOK = 1024
STRIP = 128
FEAT = 384
HID = 3072
HALF = 1536
OWN = 192
CH = 256
TA = 512
TB = TOK - TA
FOCUS = 0.85
EPS = 1e-06

ROOT_HALF = math.sqrt(0.5)
DENSITY = 1.0 / math.sqrt(2.0 * math.pi)

N_SEMS = 192
N_DOWN = 6
N_UP = 8


def cdf(v):
    return 0.5 * (1.0 + lax.erf(v * ROOT_HALF))


def slope(v):
    return cdf(v) + v * (DENSITY * jnp.exp(-0.5 * v * v))


def tn(a, b):
    return lax.dot_general(a, b, (((0,), (0,)), ((), ())), preferred_element_type=F32)


def nt(a, b):
    return lax.dot_general(a, b, (((1,), (1,)), ((), ())), preferred_element_type=F32)


def mm(a, b):
    return jnp.dot(a, b, preferred_element_type=F32)


def step_kernel(
    tok_hbm, gain_ref, wup_hbm, wdn_hbm, proj_hbm, conv_hbm, head_ref, depth_hbm, mask_hbm,
    up_out, gh_out, loss_ref,
    tok_ref, wup_ref, wdn, proj_ref, conv, depth_ref, mask_ref,
    xall, st_row, st_col, w_t, w_send, wd_peer, proj_peer, n_t, m_sum, m_part, m_recv, m_own,
    p_a, p_b, a1, a2, a3, b1, b2, b3, pre, hid, zc, z1, z1_recv, z2, z2_recv, z3,
    taps, field, field_slope, shifted, pred_all, rows_buf, gz, gm, ga, gb, gh_own, grad, up_own, send_sems, recv_sems, local_sems, out_sems,
):
    row, col = lax.axis_index("row"), lax.axis_index("col")
    z, h, c = row // 4, lax.rem(row // 2, 2), lax.rem(row, 2)
    used = [0]

    def zz(dz):
        return lax.rem(z + dz + 4, 4)

    def hh(dh):
        return lax.rem(h + dh, 2)

    def at_row(dz, dh, dc):
        return {"row": zz(dz) * 4 + hh(dh) * 2 + lax.rem(c + dc, 2)}

    def at_col(dl, dx):
        return {"col": lax.rem(col // 4 + dl, 2) * 4 + lax.rem(lax.rem(col, 4) + dx, 4)}

    def remote(src, dst, device):
        at = used[0]
        used[0] += 1
        copy = pltpu.make_async_remote_copy(
            src_ref=src, dst_ref=dst, send_sem=send_sems.at[at], recv_sem=recv_sems.at[at],
            device_id=device, device_id_type=MESH,
        )
        copy.start()
        sent.append(copy)
        return copy

    def slot(dz, dh):
        return c * 8 + zz(dz) * 2 + hh(dh)

    def own_rows(dz, dh):
        return pl.ds(pl.multiple_of(slot(dz, dh) * OWN, 64), OWN)

    sent = []
    row_peers = [
        (dz, dh, dc) for dz in (2, 1, 3, 0) for dh in (1, 0) for dc in (1, 0) if (dz, dh, dc) != (0, 0, 0)
    ]
    chip_peers = [(dz, dh) for dz in (2, 1, 3, 0) for dh in (1, 0) if (dz, dh) != (0, 0)]
    col_peers = [(dl, dx) for dl in (1, 0) for dx in (2, 1, 3, 0) if (dl, dx) != (0, 0)]
    partner = at_row(0, 0, 1)
    here = z * 2 + h
    other = 1 - c

    barrier = pltpu.get_barrier_semaphore()
    for peer in row_peers:
        pl.semaphore_signal(barrier, inc=1, device_id=at_row(*peer), device_id_type=MESH)
    for peer in col_peers:
        pl.semaphore_signal(barrier, inc=1, device_id=at_col(*peer), device_id_type=MESH)

    started = []

    def local(src, dst):
        copy = pltpu.make_async_copy(src, dst, local_sems.at[len(started)])
        copy.start()
        started.append(copy)
        return copy

    first_channel = pl.multiple_of(c * 128, 128)
    tok_copy = local(tok_hbm, tok_ref)
    proj_in = local(proj_hbm, proj_ref)
    wdn_copy = local(wdn_hbm, wdn)
    wup_copy = local(wup_hbm, wup_ref)
    depth_copy = local(depth_hbm, depth_ref)
    mask_copy = local(mask_hbm, mask_ref)
    conv_copy = local(conv_hbm.at[:, pl.ds(first_channel, 128), :], conv)

    tok_copy.wait()
    x_t = tok_ref[...].astype(F32).T
    xall[col] = x_t.astype(BF16)
    st_row[row] = jnp.concatenate(
        [
            jnp.sum(x_t, 0, keepdims=True),
            jnp.sum(x_t * x_t, 0, keepdims=True),
            jnp.zeros((6, STRIP), F32),
        ],
        axis=0,
    )
    own_half = pl.multiple_of(c * HALF, HALF)
    to_peer = pl.multiple_of(other * HALF, HALF)
    pl.semaphore_wait(barrier, len(row_peers) + len(col_peers))

    stat_copies = [remote(st_row.at[row], st_row.at[row], at_row(*peer)) for peer in row_peers]
    across = remote(xall.at[col], xall.at[col], at_col(1, 0))
    token_copies = [remote(xall.at[col], xall.at[col], at_col(0, dx)) for dx in (2, 1, 3)]
    proj_in.wait()
    wdn_copy.wait()
    wd_copy = remote(wdn.at[pl.ds(to_peer, HALF)], wd_peer, partner)
    proj_copy = remote(proj_ref, proj_peer, partner)

    @pl.loop(0, 8)
    def _(k):
        m_sum[k] = mm(wdn[pl.ds(pl.multiple_of(own_half + k * OWN, 64), OWN), :], proj_ref[...])

    across.wait_recv()
    came = xall.at[lax.rem(col + 4, 8)]
    token_copies += [remote(came, came, at_col(0, dx)) for dx in (2, 1, 3)]

    wd_copy.wait_recv()
    proj_copy.wait_recv()

    @pl.loop(0, 8)
    def _(k):
        more = mm(wd_peer[pl.ds(pl.multiple_of(k * OWN, 64), OWN), :], proj_peer[...])
        m_part[k] = (m_sum[k] + more).astype(BF16)

    m_copies = []
    for index, (dz, dh) in enumerate(chip_peers):
        m_copies.append(
            remote(m_part.at[zz(dz) * 2 + hh(dh)], m_recv.at[index], at_row(dz, dh, 0))
        )

    for copy in stat_copies:
        copy.wait_recv()
    total = st_row[0]
    for index in range(1, 16):
        total = total + st_row[index]
    mean = total[0:1] / WIDTH
    spread = total[1:2] / WIDTH - mean * mean
    depth_copy.wait()
    mask_copy.wait()
    depth = depth_ref[...].astype(F32)
    seen = mask_ref[...].astype(F32)
    st_col[col] = jnp.concatenate(
        [
            mean,
            lax.rsqrt(spread + EPS),
            jnp.concatenate([seen[0:1], seen[1:2]], axis=1),
            jnp.log(jnp.concatenate([depth[0:1], depth[1:2]], axis=1) * 0.001),
            jnp.zeros((4, STRIP), F32),
        ],
        axis=0,
    )
    norm_copies = [remote(st_col.at[col], st_col.at[col], at_col(*peer)) for peer in col_peers]

    feature_at = pl.multiple_of(c * FEAT, 128)
    wup_copy.wait()

    @pl.loop(0, HALF // 128)
    def _(i):
        at = pl.multiple_of(to_peer + i * 128, 128)
        w_send[pl.ds(pl.multiple_of(i * 128, 128), 128), :] = wup_ref[:, pl.ds(at, 128)].T

    w_copy = remote(w_send, w_t.at[:, pl.ds(feature_at, FEAT)], partner)

    @pl.loop(0, HALF // 128)
    def _(i):
        at = pl.multiple_of(own_half + i * 128, 128)
        w_t[pl.ds(pl.multiple_of(i * 128, 128), 128), pl.ds(feature_at, FEAT)] = wup_ref[:, pl.ds(at, 128)].T

    gain = jnp.broadcast_to(gain_ref[...].reshape(1, FEAT), (STRIP, FEAT)).T
    for copy in norm_copies:
        copy.wait_recv()
    for copy in token_copies:
        copy.wait_recv()

    n_copies = []
    for first in (0, 4):
        for index in range(first, first + 4):
            stats = st_col[index]
            n_t[pl.ds(feature_at, FEAT), index * STRIP : (index + 1) * STRIP] = (
                (xall[index].astype(F32) - stats[0:1]) * stats[1:2] * gain
            ).astype(BF16)
        half = n_t.at[pl.ds(feature_at, FEAT), first * STRIP : (first + 4) * STRIP]
        n_copies.append(remote(half, half, partner))
    w_copy.wait_recv()

    a_copies, b_copies = {}, {}

    def project(dz, into, first):
        base = pl.multiple_of(zz(dz) * 2 * OWN, 2 * OWN)

        @pl.loop(0, into.shape[3] // 256)
        def _(t):
            at = pl.multiple_of(t * 256, 256)
            both = mm(
                w_t[pl.ds(base, 2 * OWN), :], n_t[:, pl.ds(pl.multiple_of(first + at, 256), 256)]
            ).astype(BF16)
            into[zz(dz), 0, :, pl.ds(at, 256)] = both[:OWN]
            into[zz(dz), 1, :, pl.ds(at, 256)] = both[OWN:]

    up, down, flip = at_row(1, 0, 0), at_row(3, 0, 0), at_row(0, 1, 0)
    n_copies[0].wait_recv()
    project(2, p_a, 0)
    a_up = remote(p_a.at[zz(2), 0], a1.at[0], up)
    a_down = remote(p_a.at[zz(2), 1], a1.at[1], down)
    n_copies[1].wait_recv()

    def project_b(dz):
        project(dz, p_b, TA)
        b_copies[dz] = remote(p_b.at[zz(dz), 1 - h], b1.at[zz(dz)], flip)

    project_b(2)
    project(1, p_a, 0)
    a_up1 = remote(p_a.at[zz(1), 1], a2.at[0, 1], up)
    project(3, p_a, 0)
    a_down1 = remote(p_a.at[zz(3), 0], a2.at[1, 0], down)
    for dz in (1, 3, 0):
        project_b(dz)
    project(0, p_a, 0)

    def add(into, more):
        into[...] = (into[...].astype(F32) + more[...].astype(F32)).astype(BF16)

    a_up.wait_recv()
    add(p_a.at[zz(1), 0], a1.at[0])
    a_up2 = remote(p_a.at[zz(1), 0], a2.at[0, 0], up)
    a_down.wait_recv()
    add(p_a.at[zz(3), 1], a1.at[1])
    a_down2 = remote(p_a.at[zz(3), 1], a2.at[1, 1], down)

    b_copies[2].wait_recv()
    add(p_b.at[zz(2), h], b1.at[zz(2)])
    b_up = remote(p_b.at[zz(2), h, 0:96], b2.at[0], up)
    b_down = remote(p_b.at[zz(2), h, 96:192], b2.at[1], down)
    b_copies[1].wait_recv()
    add(p_b.at[zz(1), h], b1.at[zz(1)])
    b_copies[3].wait_recv()
    add(p_b.at[zz(3), h], b1.at[zz(3)])

    for copy in (a_up1, a_down1, a_up2, a_down2):
        copy.wait_recv()
    p_a[z, 1 - h] = (
        p_a[z, 1 - h].astype(F32) + a2[0, 1 - h].astype(F32) + a2[1, 1 - h].astype(F32)
    ).astype(BF16)
    a_flip = remote(p_a.at[z, 1 - h], a3, flip)

    b_up.wait_recv()
    add(p_b.at[zz(1), h, 0:96], b2.at[0])
    b_up2 = remote(p_b.at[zz(1), h], b3.at[0], up)
    b_down.wait_recv()
    add(p_b.at[zz(3), h, 96:192], b2.at[1])
    b_down2 = remote(p_b.at[zz(3), h], b3.at[1], down)

    for copy in m_copies:
        copy.wait_recv()
    total = m_part[here].astype(F32)
    for index in range(7):
        total = total + m_recv[index].astype(F32)
    m_own[...] = total.astype(BF16)
    gm[slot(0, 0)] = m_own[...]
    pair = {}

    def send(buf, dz, dh, device, rows=None):
        ref = buf.at[slot(dz, dh)] if rows is None else buf.at[slot(dz, dh), rows[0] : rows[1]]
        return remote(ref, ref, device)

    def share(name, buf, dz, dh, rows=None):
        pair[name] = send(buf, dz, dh, partner, rows)

    mf = send(gm, 0, 0, flip)
    mu = send(gm, 0, 0, up)
    md = send(gm, 0, 0, down)
    share(("gm", 0, 0, ""), gm, 0, 0)
    x_proj = tn(proj_ref[...], xall[col])

    conv_copy.wait()
    head = head_ref[...]
    for k in range(9):
        taps[k] = jnp.broadcast_to(
            jnp.sum(conv[k].astype(F32) * head, axis=1, keepdims=True), (128, 128)
        )
    lane = lax.broadcasted_iota(jnp.int32, (128, CH), 1)
    sub = lax.broadcasted_iota(jnp.int32, (128, CH), 0)
    taps[9] = jnp.broadcast_to(
        jnp.sum(jnp.where(lane == sub + first_channel, head, 0.0), axis=1, keepdims=True), (128, 128)
    )

    b_copies[0].wait_recv()
    a_flip.wait_recv()
    pre[:, :TA] = (
        p_a[z, h].astype(F32) + a2[0, h].astype(F32) + a2[1, h].astype(F32) + a3[...].astype(F32)
    )
    b_up2.wait_recv()
    b_down2.wait_recv()
    pre[:, TA:] = (
        p_b[z, h].astype(F32) + b1[z].astype(F32) + b3[0].astype(F32) + b3[1].astype(F32)
    )

    @pl.loop(0, TOK // 128)
    def _(t):
        at = pl.ds(pl.multiple_of(t * 128, 128), 128)
        value = pre[:, at]
        hid[:, at] = (value * cdf(value)).astype(BF16)

    @pl.loop(0, TOK // 256)
    def _(t):
        at = pl.ds(pl.multiple_of(t * 256, 256), 256)
        zc[:, at] = tn(m_own[...], hid[:, at])

    strip = pl.ds(pl.multiple_of(col * STRIP, STRIP), STRIP)
    zc[:, strip] = zc[:, strip] + x_proj

    z1[...] = zc[pl.ds(pl.multiple_of(other * 128, 128), 128), :].astype(BF16)
    z1_copy = remote(z1, z1_recv, partner)

    mine_a, mine_b = ga.at[slot(0, 0)], gb.at[slot(0, 0)]
    mf.wait_recv()
    mfu = send(gm, 0, 1, up)
    mfd = send(gm, 0, 1, down)
    share(("gm", 0, 1, ""), gm, 0, 1)
    top, low = (0, 96), (96, 192)

    @pl.loop(0, TB // 128)
    def _(t):
        at = pl.ds(pl.multiple_of(t * 128, 128), 128)
        mine_b[:, at] = slope(pre[:, pl.ds(pl.multiple_of(TA + t * 128, 128), 128)]).astype(BF16)

    z1_copy.wait_recv()
    z2[...] = (
        zc[pl.ds(pl.multiple_of(c * 128, 128), 128), :] + z1_recv[...].astype(F32)
    ).astype(BF16)
    z2_copies = []
    for index, (dz, dh) in enumerate(chip_peers):
        at = pl.multiple_of((zz(dz) * 2 + hh(dh)) * 16, 16)
        z2_copies.append(remote(z2.at[pl.ds(at, 16)], z2_recv.at[index], at_row(dz, dh, 0)))
    bu = send(gb, 0, 0, up)
    bd = send(gb, 0, 0, down)
    mu.wait_recv()
    mu2 = send(gm, 3, 0, up)
    share(("gm", 3, 0, ""), gm, 3, 0)
    md.wait_recv()
    share(("gm", 1, 0, ""), gm, 1, 0)
    share(("gb", 0, 0, ""), gb, 0, 0)

    @pl.loop(0, TA // 128)
    def _(t):
        at = pl.ds(pl.multiple_of(t * 128, 128), 128)
        mine_a[:, at] = slope(pre[:, at]).astype(BF16)

    fa = send(ga, 0, 0, flip)
    mfd.wait_recv()
    mfd2 = send(gm, 1, 1, down)
    share(("gm", 1, 1, ""), gm, 1, 1)
    mfu.wait_recv()
    share(("gm", 3, 1, ""), gm, 3, 1)
    share(("ga", 0, 0, ""), ga, 0, 0)
    mine = pl.ds(pl.multiple_of(here * 16, 16), 16)
    part = z2[mine, :].astype(F32)
    for index, copy in enumerate(z2_copies):
        copy.wait_recv()
        part = part + z2_recv[index].astype(F32)
    z3[col] = part.astype(BF16)
    z3_copies = [remote(z3.at[col], z3.at[col], at_col(*peer)) for peer in col_peers]
    au = send(ga, 0, 0, up)
    ad = send(ga, 0, 0, down)
    fb = send(gb, 0, 0, flip)
    bu.wait_recv()
    bu2 = send(gb, 3, 0, up, top)
    share(("gb", 3, 0, ""), gb, 3, 0)
    bd.wait_recv()
    bd2 = send(gb, 1, 0, down, low)
    share(("gb", 1, 0, ""), gb, 1, 0)
    for copy in z3_copies:
        copy.wait_recv()
    total = z3[0].astype(F32)
    for index in range(1, 8):
        total = total + z3[index].astype(F32)
    field[mine, :] = total.astype(BF16)
    z4_copies = [
        remote(field.at[mine], field.at[mine], at_row(dz, dh, 0)) for dz, dh in chip_peers
    ]
    f_m = send(gb, 3, 0, flip)
    f_p = send(gb, 1, 0, flip)
    fa.wait_recv()
    fau = send(ga, 0, 1, up)
    fad = send(ga, 0, 1, down)
    share(("ga", 0, 1, ""), ga, 0, 1)
    au.wait_recv()
    au2 = send(ga, 3, 0, up)
    share(("ga", 3, 0, ""), ga, 3, 0)
    ad.wait_recv()
    share(("ga", 1, 0, ""), ga, 1, 0)
    fb.wait_recv()
    share(("gb", 0, 1, ""), gb, 0, 1)
    bu2.wait_recv()
    f_top = send(gb, 2, 0, flip, top)
    share(("gb", 2, 0, "top"), gb, 2, 0, top)
    bd2.wait_recv()
    f_low = send(gb, 2, 0, flip, low)
    share(("gb", 2, 0, "low"), gb, 2, 0, low)
    mu2.wait_recv()
    share(("gm", 2, 0, ""), gm, 2, 0)
    mfd2.wait_recv()
    share(("gm", 2, 1, ""), gm, 2, 1)
    for copy in z4_copies:
        copy.wait_recv()

    token = lax.broadcasted_iota(jnp.int32, (1, TOK), 1)
    line, place = token >> 6, token & (GW - 1)

    def moved(values, di, dj):
        shift = di * GW + dj
        if shift:
            values = pltpu.roll(values, (-shift) % TOK, 1)
        inside = (
            (line + di >= 0) & (line + di < GH) & (place + dj >= 0) & (place + dj < GW)
        )
        return jnp.where(inside, values, 0.0)

    @pl.loop(0, TOK // 128)
    def _(t):
        at = pl.ds(pl.multiple_of(t * 128, 128), 128)
        value = field[:, at].astype(F32)
        act = (value * cdf(value)).astype(BF16).astype(F32)
        for k in range(9):
            shifted[k : k + 1, at] = jnp.sum(act * taps[k], axis=0, keepdims=True)
        shifted[9:10, at] = jnp.sum(value * taps[9], axis=0, keepdims=True)

    pred = shifted[9:10, :]
    for k in range(9):
        pred = pred + moved(shifted[k : k + 1, :], k // 3 - 1, k % 3 - 1)
    for index in range(8):
        rows_buf[index : index + 1, :] = pred[:, index * STRIP : (index + 1) * STRIP]
    pred_all[c] = rows_buf[...]
    pred_copy = remote(pred_all.at[c], pred_all.at[c], partner)

    @pl.loop(0, TOK // 128)
    def _(t):
        at = pl.ds(pl.multiple_of(t * 128, 128), 128)
        field_slope[:, at] = slope(field[:, at].astype(F32))

    valid = jnp.concatenate([st_col[index][2:3] for index in range(8)], axis=0)
    target = jnp.concatenate([st_col[index][3:4] for index in range(8)], axis=0)
    pred_copy.wait_recv()
    err = valid * (pred_all[0] + pred_all[1] - target)

    def whole(values):
        return jnp.sum(jnp.sum(values, axis=1, keepdims=True), axis=0, keepdims=True)

    count = whole(valid)
    mean_err = whole(err) / count
    loss_ref[0, 0] = jnp.sum(whole(err * err) / count - FOCUS * mean_err * mean_err)
    grad_pred = valid * (2.0 * err - 2.0 * FOCUS * mean_err)
    grad_pred = jnp.concatenate([grad_pred[index : index + 1] for index in range(8)], axis=1)
    for k in range(9):
        shifted[k : k + 1, :] = moved(grad_pred, 1 - k // 3, 1 - k % 3)
    shifted[9:10, :] = grad_pred

    @pl.loop(0, TOK // 128)
    def _(t):
        at = pl.ds(pl.multiple_of(t * 128, 128), 128)
        back = taps[0] * shifted[0:1, at]
        for k in range(1, 9):
            back = back + taps[k] * shifted[k : k + 1, at]
        gz[pl.ds(first_channel, 128), at] = (
            taps[9] * shifted[9:10, at] + field_slope[:, at] * back
        ).astype(BF16)

    half_z = gz.at[pl.ds(first_channel, 128)]
    gz_copy = remote(half_z, half_z, partner)
    fad.wait_recv()
    fad2 = send(ga, 1, 1, down)
    share(("ga", 1, 1, ""), ga, 1, 1)
    fau.wait_recv()
    share(("ga", 3, 1, ""), ga, 3, 1)

    second_channel = pl.multiple_of(other * 128, 128)
    gh_own[:, pl.ds(first_channel, 128)] = nt(hid[...], half_z[...]).astype(BF16)
    gz_copy.wait_recv()
    gh_own[:, pl.ds(second_channel, 128)] = nt(
        hid[...], gz[pl.ds(second_channel, 128), :]
    ).astype(BF16)
    local(gh_own, gh_out.at[own_rows(0, 0)])
    gh_copies = [
        remote(gh_own, gh_out.at[own_rows(0, 0)], at_row(dz, dh, 0)) for dz, dh in chip_peers
    ]
    gh_pair = [remote(gh_own, gh_out.at[own_rows(0, 0)], partner)]
    def ready(dz):
        for key, copy in pair.items():
            if key[1] == dz:
                copy.wait_recv()

    n_mine = n_t.at[pl.ds(feature_at, FEAT)]

    def column(dz):
        @pl.loop(0, 2)
        def _(core):
            base = core * 8 + zz(dz) * 2
            for half in (0, 1):
                rows = slice(half * OWN, (half + 1) * OWN)
                weights = gm[base + half]
                grad[rows, :TA] = (
                    mm(weights, gz[:, :TA]) * ga[base + half].astype(F32)
                ).astype(BF16)
                grad[rows, TA:] = (
                    mm(weights, gz[:, TA:]) * gb[base + half].astype(F32)
                ).astype(BF16)
            up_own[dz, core] = nt(n_mine[...], grad[...])
            at = pl.multiple_of(base * OWN, 2 * OWN)
            pltpu.make_async_copy(
                up_own.at[dz, core], up_out.at[:, pl.ds(at, 2 * OWN)], out_sems.at[dz, core]
            ).start()

    f_m.wait_recv()
    share(("gb", 3, 1, ""), gb, 3, 1)
    f_p.wait_recv()
    share(("gb", 1, 1, ""), gb, 1, 1)
    ready(0)
    column(0)
    f_top.wait_recv()
    share(("gb", 2, 1, "top"), gb, 2, 1, top)
    f_low.wait_recv()
    share(("gb", 2, 1, "low"), gb, 2, 1, low)
    ready(3)
    column(3)
    au2.wait_recv()
    share(("ga", 2, 0, ""), ga, 2, 0)
    ready(1)
    column(1)
    fad2.wait_recv()
    share(("ga", 2, 1, ""), ga, 2, 1)
    ready(2)
    column(2)

    for (dz, dh), copy in zip(chip_peers, gh_copies):
        copy.wait_recv()
        came = gh_out.at[own_rows(-dz, dh)]
        gh_pair.append(remote(came, came, partner))
    for copy in gh_pair:
        copy.wait_recv()

    for dz in range(4):

        @pl.loop(0, 2)
        def _(core):
            at = pl.multiple_of((core * 8 + zz(dz) * 2) * OWN, 2 * OWN)
            pltpu.make_async_copy(
                up_own.at[dz, core], up_out.at[:, pl.ds(at, 2 * OWN)], out_sems.at[dz, core]
            ).wait()

    started[-1].wait()
    for copy in sent:
        copy.wait_send()


def weight_kernel(gh_hbm, proj_hbm, up_hbm, up_out, down_out, gh, proj, up, down, in_sems, out_sems):
    rows, lines = HID // N_DOWN, FEAT // N_UP

    def down_at(index):
        return pl.ds(index * rows, rows)

    def up_at(index):
        return pl.ds(index * lines, lines)

    proj_in = pltpu.make_async_copy(proj_hbm, proj, in_sems.at[0])
    gh_in = [
        pltpu.make_async_copy(gh_hbm.at[down_at(k)], gh.at[down_at(k)], in_sems.at[1 + k])
        for k in range(N_DOWN)
    ]
    up_in = [
        pltpu.make_async_copy(up_hbm.at[up_at(k)], up.at[up_at(k)], in_sems.at[1 + N_DOWN + k])
        for k in range(N_UP)
    ]
    for copy in [proj_in] + gh_in + up_in:
        copy.start()
    leaving = []
    proj_in.wait()
    for k in range(N_DOWN):
        gh_in[k].wait()
        down[down_at(k), :] = nt(gh[down_at(k), :], proj[...])
        leaving.append(
            pltpu.make_async_copy(down.at[down_at(k)], down_out.at[down_at(k)], out_sems.at[k])
        )
        leaving[-1].start()
    for k in range(N_UP):
        up_in[k].wait()
        leaving.append(
            pltpu.make_async_copy(up.at[up_at(k)], up_out.at[up_at(k)], out_sems.at[N_DOWN + k])
        )
        leaving[-1].start()
    for copy in leaving:
        copy.wait()


def on_device(tokens, ln_gain, w_up, w_down, proj, conv_kernel, head_weight, depth_mm, lidar_mask):
    vmem = pl.BlockSpec(memory_space=pltpu.VMEM)
    anywhere = pl.BlockSpec(memory_space=pl.ANY)
    up_held, grad_hidden, loss = pl.pallas_call(
        step_kernel,
        name="mlp_step",
        out_shape=[
            jax.ShapeDtypeStruct((FEAT, HID), F32),
            jax.ShapeDtypeStruct((HID, CH), BF16),
            jax.ShapeDtypeStruct((1, 1), F32),
        ],
        in_specs=[
            anywhere, vmem, anywhere, anywhere, anywhere, anywhere, vmem, anywhere, anywhere,
        ],
        out_specs=[anywhere, anywhere, pl.BlockSpec(memory_space=pltpu.SMEM)],
        scratch_shapes=[
            pltpu.VMEM((STRIP, FEAT), BF16),
            pltpu.VMEM((FEAT, HID), BF16),
            pltpu.VMEM((HID, FEAT), BF16),
            pltpu.VMEM((FEAT, CH), BF16),
            pltpu.VMEM((9, 128, CH), BF16),
            pltpu.VMEM((2, GW), jnp.int32),
            pltpu.VMEM((2, GW), jnp.int32),
            pltpu.VMEM((8, FEAT, STRIP), BF16),
            pltpu.VMEM((16, 8, STRIP), F32),
            pltpu.VMEM((8, 8, STRIP), F32),
            pltpu.VMEM((HALF, 2 * FEAT), BF16),
            pltpu.VMEM((HALF, FEAT), BF16),
            pltpu.VMEM((HALF, FEAT), BF16),
            pltpu.VMEM((FEAT, CH), BF16),
            pltpu.VMEM((2 * FEAT, TOK), BF16),
            pltpu.VMEM((8, OWN, CH), F32),
            pltpu.VMEM((8, OWN, CH), BF16),
            pltpu.VMEM((7, OWN, CH), BF16),
            pltpu.VMEM((OWN, CH), BF16),
            pltpu.VMEM((4, 2, OWN, TA), BF16),
            pltpu.VMEM((4, 2, OWN, TB), BF16),
            pltpu.VMEM((2, OWN, TA), BF16),
            pltpu.VMEM((2, 2, OWN, TA), BF16),
            pltpu.VMEM((OWN, TA), BF16),
            pltpu.VMEM((4, OWN, TB), BF16),
            pltpu.VMEM((2, OWN // 2, TB), BF16),
            pltpu.VMEM((2, OWN, TB), BF16),
            pltpu.VMEM((OWN, TOK), F32),
            pltpu.VMEM((OWN, TOK), BF16),
            pltpu.VMEM((CH, TOK), F32),
            pltpu.VMEM((128, TOK), BF16),
            pltpu.VMEM((128, TOK), BF16),
            pltpu.VMEM((128, TOK), BF16),
            pltpu.VMEM((7, 16, TOK), BF16),
            pltpu.VMEM((8, 16, TOK), BF16),
            pltpu.VMEM((10, 128, 128), F32),
            pltpu.VMEM((128, TOK), BF16),
            pltpu.VMEM((128, TOK), F32),
            pltpu.VMEM((16, TOK), F32),
            pltpu.VMEM((2, 8, STRIP), F32),
            pltpu.VMEM((8, STRIP), F32),
            pltpu.VMEM((CH, TOK), BF16),
            pltpu.VMEM((16, OWN, CH), BF16),
            pltpu.VMEM((16, OWN, TA), BF16),
            pltpu.VMEM((16, OWN, TB), BF16),
            pltpu.VMEM((OWN, CH), BF16),
            pltpu.VMEM((2 * OWN, TOK), BF16),
            pltpu.VMEM((4, 2, FEAT, 2 * OWN), F32),
            pltpu.SemaphoreType.DMA((N_SEMS,)),
            pltpu.SemaphoreType.DMA((N_SEMS,)),
            pltpu.SemaphoreType.DMA((9,)),
            pltpu.SemaphoreType.DMA((4, 2)),
        ],
        compiler_params=pltpu.CompilerParams(
            collective_id=0, has_side_effects=True, vmem_limit_bytes=60 * 2**20
        ),
        cost_estimate=pl.CostEstimate(flops=6 * 10**9, bytes_accessed=16 * 2**20, transcendentals=10**6),
    )(
        tokens, ln_gain, w_up, w_down, proj, conv_kernel.reshape(9, CH, CH),
        head_weight.reshape(1, CH), depth_mm, lidar_mask,
    )
    grad_up, grad_down = pl.pallas_call(
        weight_kernel,
        name="weight_grads",
        out_shape=[
            jax.ShapeDtypeStruct((FEAT, HID), F32),
            jax.ShapeDtypeStruct((HID, FEAT), F32),
        ],
        in_specs=[anywhere, anywhere, anywhere],
        out_specs=[anywhere, anywhere],
        scratch_shapes=[
            pltpu.VMEM((HID, CH), BF16),
            pltpu.VMEM((FEAT, CH), BF16),
            pltpu.VMEM((FEAT, HID), F32),
            pltpu.VMEM((HID, FEAT), F32),
            pltpu.SemaphoreType.DMA((1 + N_DOWN + N_UP,)),
            pltpu.SemaphoreType.DMA((N_DOWN + N_UP,)),
        ],
        compiler_params=pltpu.CompilerParams(vmem_limit_bytes=60 * 2**20),
        cost_estimate=pl.CostEstimate(flops=6 * 10**8, bytes_accessed=16 * 2**20, transcendentals=0),
    )(grad_hidden, proj, up_held)
    return (grad_up, grad_down, loss.reshape(()))


def solution(mesh):
    return jax.shard_map(
        on_device,
        mesh=mesh,
        in_specs=(
            P("col", "row"),
            P("row"),
            P("row", "col"),
            P("col", "row"),
            P("row", None),
            P(),
            P(),
            P("col", None),
            P("col", None),
        ),
        out_specs=(P("row", "col"), P("col", "row"), P()),
        check_vma=False,
    )
```

```python
import math

import jax
import jax.numpy as jnp
from jax import lax
from jax.experimental import pallas as pl
from jax.experimental.pallas import tpu as pltpu
from jax.sharding import PartitionSpec as P

MESH = pl.DeviceIdType.MESH
F32 = jnp.float32
BF16 = jnp.bfloat16

WIDTH = 6144
GW = 64
GH = 16
TOK = 1024
STRIP = 128
FEAT = 384
HID = 3072
HALF = 1536
OWN = 192
CH = 256
TA = 512
TB = TOK - TA
FOCUS = 0.85
EPS = 1e-06

ROOT_HALF = math.sqrt(0.5)
DENSITY = 1.0 / math.sqrt(2.0 * math.pi)

N_SEMS = 192
N_DOWN = 6
N_UP = 8


def cdf(v):
    return 0.5 * (1.0 + lax.erf(v * ROOT_HALF))


def slope(v):
    return cdf(v) + v * (DENSITY * jnp.exp(-0.5 * v * v))


def tn(a, b):
    return lax.dot_general(a, b, (((0,), (0,)), ((), ())), preferred_element_type=F32)


def nt(a, b):
    return lax.dot_general(a, b, (((1,), (1,)), ((), ())), preferred_element_type=F32)


def mm(a, b):
    return jnp.dot(a, b, preferred_element_type=F32)


def step_kernel(
    tok_hbm, gain_ref, wup_hbm, wdn_hbm, proj_hbm, conv_hbm, head_ref, depth_hbm, mask_hbm,
    up_out, gh_out, loss_ref,
    tok_ref, wup_ref, wdn, proj_ref, conv, depth_ref, mask_ref,
    xall, st_row, st_col, w_t, w_send, wd_peer, proj_peer, n_t, m_sum, m_part, m_recv, m_own,
    p_a, p_b, a1, a2, a3, b1, b2, b3, pre, hid, zc, z1, z1_recv, z2, z2_recv, z3,
    taps, field, field_slope, shifted, pred_all, rows_buf, gz, gm, ga, gb, gh_own, grad, up_own, send_sems, recv_sems, local_sems, out_sems,
):
    row, col = lax.axis_index("row"), lax.axis_index("col")
    z, h, c = row // 4, lax.rem(row // 2, 2), lax.rem(row, 2)
    used = [0]

    def zz(dz):
        return lax.rem(z + dz + 4, 4)

    def hh(dh):
        return lax.rem(h + dh, 2)

    def at_row(dz, dh, dc):
        return {"row": zz(dz) * 4 + hh(dh) * 2 + lax.rem(c + dc, 2)}

    def at_col(dl, dx):
        return {"col": lax.rem(col // 4 + dl, 2) * 4 + lax.rem(lax.rem(col, 4) + dx, 4)}

    def remote(src, dst, device):
        at = used[0]
        used[0] += 1
        copy = pltpu.make_async_remote_copy(
            src_ref=src, dst_ref=dst, send_sem=send_sems.at[at], recv_sem=recv_sems.at[at],
            device_id=device, device_id_type=MESH,
        )
        copy.start()
        sent.append(copy)
        return copy

    def slot(dz, dh):
        return c * 8 + zz(dz) * 2 + hh(dh)

    def own_rows(dz, dh):
        return pl.ds(pl.multiple_of(slot(dz, dh) * OWN, 64), OWN)

    sent = []
    row_peers = [
        (dz, dh, dc) for dz in (2, 1, 3, 0) for dh in (1, 0) for dc in (1, 0) if (dz, dh, dc) != (0, 0, 0)
    ]
    chip_peers = [(dz, dh) for dz in (2, 1, 3, 0) for dh in (1, 0) if (dz, dh) != (0, 0)]
    col_peers = [(dl, dx) for dl in (1, 0) for dx in (2, 1, 3, 0) if (dl, dx) != (0, 0)]
    partner = at_row(0, 0, 1)
    here = z * 2 + h
    other = 1 - c

    barrier = pltpu.get_barrier_semaphore()
    for peer in row_peers:
        pl.semaphore_signal(barrier, inc=1, device_id=at_row(*peer), device_id_type=MESH)
    for peer in col_peers:
        pl.semaphore_signal(barrier, inc=1, device_id=at_col(*peer), device_id_type=MESH)

    started = []

    def local(src, dst):
        copy = pltpu.make_async_copy(src, dst, local_sems.at[len(started)])
        copy.start()
        started.append(copy)
        return copy

    first_channel = pl.multiple_of(c * 128, 128)
    tok_copy = local(tok_hbm, tok_ref)
    proj_in = local(proj_hbm, proj_ref)
    wdn_copy = local(wdn_hbm, wdn)
    wup_copy = local(wup_hbm, wup_ref)
    depth_copy = local(depth_hbm, depth_ref)
    mask_copy = local(mask_hbm, mask_ref)
    conv_copy = local(conv_hbm.at[:, pl.ds(first_channel, 128), :], conv)

    tok_copy.wait()
    x_t = tok_ref[...].astype(F32).T
    xall[col] = x_t.astype(BF16)
    st_row[row] = jnp.concatenate(
        [
            jnp.sum(x_t, 0, keepdims=True),
            jnp.sum(x_t * x_t, 0, keepdims=True),
            jnp.zeros((6, STRIP), F32),
        ],
        axis=0,
    )
    own_half = pl.multiple_of(c * HALF, HALF)
    to_peer = pl.multiple_of(other * HALF, HALF)
    pl.semaphore_wait(barrier, len(row_peers) + len(col_peers))

    stat_copies = [remote(st_row.at[row], st_row.at[row], at_row(*peer)) for peer in row_peers]
    across = remote(xall.at[col], xall.at[col], at_col(1, 0))
    token_copies = [remote(xall.at[col], xall.at[col], at_col(0, dx)) for dx in (2, 1, 3)]
    proj_in.wait()
    wdn_copy.wait()
    wd_copy = remote(wdn.at[pl.ds(to_peer, HALF)], wd_peer, partner)
    proj_copy = remote(proj_ref, proj_peer, partner)

    @pl.loop(0, 8)
    def _(k):
        m_sum[k] = mm(wdn[pl.ds(pl.multiple_of(own_half + k * OWN, 64), OWN), :], proj_ref[...])

    across.wait_recv()
    came = xall.at[lax.rem(col + 4, 8)]
    token_copies += [remote(came, came, at_col(0, dx)) for dx in (2, 1, 3)]

    wd_copy.wait_recv()
    proj_copy.wait_recv()

    @pl.loop(0, 8)
    def _(k):
        more = mm(wd_peer[pl.ds(pl.multiple_of(k * OWN, 64), OWN), :], proj_peer[...])
        m_part[k] = (m_sum[k] + more).astype(BF16)

    m_copies = []
    for index, (dz, dh) in enumerate(chip_peers):
        m_copies.append(
            remote(m_part.at[zz(dz) * 2 + hh(dh)], m_recv.at[index], at_row(dz, dh, 0))
        )

    for copy in stat_copies:
        copy.wait_recv()
    total = st_row[0]
    for index in range(1, 16):
        total = total + st_row[index]
    mean = total[0:1] / WIDTH
    spread = total[1:2] / WIDTH - mean * mean
    depth_copy.wait()
    mask_copy.wait()
    depth = depth_ref[...].astype(F32)
    seen = mask_ref[...].astype(F32)
    st_col[col] = jnp.concatenate(
        [
            mean,
            lax.rsqrt(spread + EPS),
            jnp.concatenate([seen[0:1], seen[1:2]], axis=1),
            jnp.log(jnp.concatenate([depth[0:1], depth[1:2]], axis=1) * 0.001),
            jnp.zeros((4, STRIP), F32),
        ],
        axis=0,
    )
    norm_copies = [remote(st_col.at[col], st_col.at[col], at_col(*peer)) for peer in col_peers]

    feature_at = pl.multiple_of(c * FEAT, 128)
    wup_copy.wait()

    @pl.loop(0, HALF // 128)
    def _(i):
        at = pl.multiple_of(to_peer + i * 128, 128)
        w_send[pl.ds(pl.multiple_of(i * 128, 128), 128), :] = wup_ref[:, pl.ds(at, 128)].T

    w_copy = remote(w_send, w_t.at[:, pl.ds(feature_at, FEAT)], partner)

    @pl.loop(0, HALF // 128)
    def _(i):
        at = pl.multiple_of(own_half + i * 128, 128)
        w_t[pl.ds(pl.multiple_of(i * 128, 128), 128), pl.ds(feature_at, FEAT)] = wup_ref[:, pl.ds(at, 128)].T

    gain = jnp.broadcast_to(gain_ref[...].reshape(1, FEAT), (STRIP, FEAT)).T
    for copy in norm_copies:
        copy.wait_recv()
    for copy in token_copies:
        copy.wait_recv()

    n_copies = []
    for first in (0, 4):
        for index in range(first, first + 4):
            stats = st_col[index]
            n_t[pl.ds(feature_at, FEAT), index * STRIP : (index + 1) * STRIP] = (
                (xall[index].astype(F32) - stats[0:1]) * stats[1:2] * gain
            ).astype(BF16)
        half = n_t.at[pl.ds(feature_at, FEAT), first * STRIP : (first + 4) * STRIP]
        n_copies.append(remote(half, half, partner))
    w_copy.wait_recv()

    a_copies, b_copies = {}, {}

    def project(dz, into, first):
        base = pl.multiple_of(zz(dz) * 2 * OWN, 2 * OWN)

        @pl.loop(0, into.shape[3] // 256)
        def _(t):
            at = pl.multiple_of(t * 256, 256)
            both = mm(
                w_t[pl.ds(base, 2 * OWN), :], n_t[:, pl.ds(pl.multiple_of(first + at, 256), 256)]
            ).astype(BF16)
            into[zz(dz), 0, :, pl.ds(at, 256)] = both[:OWN]
            into[zz(dz), 1, :, pl.ds(at, 256)] = both[OWN:]

    up, down, flip = at_row(1, 0, 0), at_row(3, 0, 0), at_row(0, 1, 0)
    n_copies[0].wait_recv()
    project(2, p_a, 0)
    a_up = remote(p_a.at[zz(2), 0], a1.at[0], up)
    a_down = remote(p_a.at[zz(2), 1], a1.at[1], down)
    n_copies[1].wait_recv()

    def project_b(dz):
        project(dz, p_b, TA)
        b_copies[dz] = remote(p_b.at[zz(dz), 1 - h], b1.at[zz(dz)], flip)

    project_b(2)
    project(1, p_a, 0)
    a_up1 = remote(p_a.at[zz(1), 1], a2.at[0, 1], up)
    project(3, p_a, 0)
    a_down1 = remote(p_a.at[zz(3), 0], a2.at[1, 0], down)
    for dz in (1, 3, 0):
        project_b(dz)
    project(0, p_a, 0)

    def add(into, more):
        into[...] = (into[...].astype(F32) + more[...].astype(F32)).astype(BF16)

    a_up.wait_recv()
    add(p_a.at[zz(1), 0], a1.at[0])
    a_up2 = remote(p_a.at[zz(1), 0], a2.at[0, 0], up)
    a_down.wait_recv()
    add(p_a.at[zz(3), 1], a1.at[1])
    a_down2 = remote(p_a.at[zz(3), 1], a2.at[1, 1], down)

    b_copies[2].wait_recv()
    add(p_b.at[zz(2), h], b1.at[zz(2)])
    b_up = remote(p_b.at[zz(2), h, 0:96], b2.at[0], up)
    b_down = remote(p_b.at[zz(2), h, 96:192], b2.at[1], down)
    b_copies[1].wait_recv()
    add(p_b.at[zz(1), h], b1.at[zz(1)])
    b_copies[3].wait_recv()
    add(p_b.at[zz(3), h], b1.at[zz(3)])

    for copy in (a_up1, a_down1, a_up2, a_down2):
        copy.wait_recv()
    p_a[z, 1 - h] = (
        p_a[z, 1 - h].astype(F32) + a2[0, 1 - h].astype(F32) + a2[1, 1 - h].astype(F32)
    ).astype(BF16)
    a_flip = remote(p_a.at[z, 1 - h], a3, flip)

    b_up.wait_recv()
    add(p_b.at[zz(1), h, 0:96], b2.at[0])
    b_up2 = remote(p_b.at[zz(1), h], b3.at[0], up)
    b_down.wait_recv()
    add(p_b.at[zz(3), h, 96:192], b2.at[1])
    b_down2 = remote(p_b.at[zz(3), h], b3.at[1], down)

    for copy in m_copies:
        copy.wait_recv()
    total = m_part[here].astype(F32)
    for index in range(7):
        total = total + m_recv[index].astype(F32)
    m_own[...] = total.astype(BF16)
    gm[slot(0, 0)] = m_own[...]
    pair = {}

    def send(buf, dz, dh, device, rows=None):
        ref = buf.at[slot(dz, dh)] if rows is None else buf.at[slot(dz, dh), rows[0] : rows[1]]
        return remote(ref, ref, device)

    def share(name, buf, dz, dh, rows=None):
        pair[name] = send(buf, dz, dh, partner, rows)

    mf = send(gm, 0, 0, flip)
    mu = send(gm, 0, 0, up)
    md = send(gm, 0, 0, down)
    share(("gm", 0, 0, ""), gm, 0, 0)
    zc[...] = jnp.zeros_like(zc)
    zc[:, pl.ds(pl.multiple_of(col * STRIP, STRIP), STRIP)] = tn(proj_ref[...], xall[col])

    conv_copy.wait()
    head = head_ref[...]
    for k in range(9):
        taps[k] = jnp.broadcast_to(
            jnp.sum(conv[k].astype(F32) * head, axis=1, keepdims=True), (128, 128)
        )
    lane = lax.broadcasted_iota(jnp.int32, (128, CH), 1)
    sub = lax.broadcasted_iota(jnp.int32, (128, CH), 0)
    taps[9] = jnp.broadcast_to(
        jnp.sum(jnp.where(lane == sub + first_channel, head, 0.0), axis=1, keepdims=True), (128, 128)
    )

    mine_a, mine_b = ga.at[slot(0, 0)], gb.at[slot(0, 0)]

    def hidden(part):
        @pl.loop(0, TA // 256)
        def _(t):
            at = pl.ds(pl.multiple_of(part * TA + t * 256, 256), 256)
            value = pre[:, at]
            value = (value * cdf(value)).astype(BF16)
            hid[:, at] = value
            zc[:, at] = zc[:, at] + tn(m_own[...], value)

    a_flip.wait_recv()
    pre[:, :TA] = (
        p_a[z, h].astype(F32) + a2[0, h].astype(F32) + a2[1, h].astype(F32) + a3[...].astype(F32)
    )
    hidden(0)

    @pl.loop(0, TA // 128)
    def _(t):
        at = pl.ds(pl.multiple_of(t * 128, 128), 128)
        mine_a[:, at] = slope(pre[:, at]).astype(BF16)

    fa = send(ga, 0, 0, flip)

    b_copies[0].wait_recv()
    b_up2.wait_recv()
    b_down2.wait_recv()
    pre[:, TA:] = (
        p_b[z, h].astype(F32) + b1[z].astype(F32) + b3[0].astype(F32) + b3[1].astype(F32)
    )
    hidden(1)

    z1[...] = zc[pl.ds(pl.multiple_of(other * 128, 128), 128), :].astype(BF16)
    z1_copy = remote(z1, z1_recv, partner)

    mf.wait_recv()
    mfu = send(gm, 0, 1, up)
    mfd = send(gm, 0, 1, down)
    share(("gm", 0, 1, ""), gm, 0, 1)
    top, low = (0, 96), (96, 192)

    @pl.loop(0, TB // 128)
    def _(t):
        at = pl.ds(pl.multiple_of(t * 128, 128), 128)
        mine_b[:, at] = slope(pre[:, pl.ds(pl.multiple_of(TA + t * 128, 128), 128)]).astype(BF16)

    z1_copy.wait_recv()
    z2[...] = (
        zc[pl.ds(pl.multiple_of(c * 128, 128), 128), :] + z1_recv[...].astype(F32)
    ).astype(BF16)
    z2_copies = []
    for index, (dz, dh) in enumerate(chip_peers):
        at = pl.multiple_of((zz(dz) * 2 + hh(dh)) * 16, 16)
        z2_copies.append(remote(z2.at[pl.ds(at, 16)], z2_recv.at[index], at_row(dz, dh, 0)))
    bu = send(gb, 0, 0, up)
    bd = send(gb, 0, 0, down)
    mu.wait_recv()
    mu2 = send(gm, 3, 0, up)
    share(("gm", 3, 0, ""), gm, 3, 0)
    md.wait_recv()
    share(("gm", 1, 0, ""), gm, 1, 0)
    share(("gb", 0, 0, ""), gb, 0, 0)

    mfd.wait_recv()
    mfd2 = send(gm, 1, 1, down)
    share(("gm", 1, 1, ""), gm, 1, 1)
    mfu.wait_recv()
    share(("gm", 3, 1, ""), gm, 3, 1)
    share(("ga", 0, 0, ""), ga, 0, 0)
    mine = pl.ds(pl.multiple_of(here * 16, 16), 16)
    part = z2[mine, :].astype(F32)
    for index, copy in enumerate(z2_copies):
        copy.wait_recv()
        part = part + z2_recv[index].astype(F32)
    z3[col] = part.astype(BF16)
    z3_copies = [remote(z3.at[col], z3.at[col], at_col(*peer)) for peer in col_peers]
    au = send(ga, 0, 0, up)
    ad = send(ga, 0, 0, down)
    fb = send(gb, 0, 0, flip)
    bu.wait_recv()
    bu2 = send(gb, 3, 0, up, top)
    share(("gb", 3, 0, ""), gb, 3, 0)
    bd.wait_recv()
    bd2 = send(gb, 1, 0, down, low)
    share(("gb", 1, 0, ""), gb, 1, 0)
    for copy in z3_copies:
        copy.wait_recv()
    total = z3[0].astype(F32)
    for index in range(1, 8):
        total = total + z3[index].astype(F32)
    field[mine, :] = total.astype(BF16)
    z4_copies = [
        remote(field.at[mine], field.at[mine], at_row(dz, dh, 0)) for dz, dh in chip_peers
    ]
    f_m = send(gb, 3, 0, flip)
    f_p = send(gb, 1, 0, flip)
    fa.wait_recv()
    fau = send(ga, 0, 1, up)
    fad = send(ga, 0, 1, down)
    share(("ga", 0, 1, ""), ga, 0, 1)
    au.wait_recv()
    au2 = send(ga, 3, 0, up)
    share(("ga", 3, 0, ""), ga, 3, 0)
    ad.wait_recv()
    share(("ga", 1, 0, ""), ga, 1, 0)
    fb.wait_recv()
    share(("gb", 0, 1, ""), gb, 0, 1)
    bu2.wait_recv()
    f_top = send(gb, 2, 0, flip, top)
    share(("gb", 2, 0, "top"), gb, 2, 0, top)
    bd2.wait_recv()
    f_low = send(gb, 2, 0, flip, low)
    share(("gb", 2, 0, "low"), gb, 2, 0, low)
    mu2.wait_recv()
    share(("gm", 2, 0, ""), gm, 2, 0)
    mfd2.wait_recv()
    share(("gm", 2, 1, ""), gm, 2, 1)
    for copy in z4_copies:
        copy.wait_recv()

    token = lax.broadcasted_iota(jnp.int32, (1, TOK), 1)
    line, place = token >> 6, token & (GW - 1)

    def moved(values, di, dj):
        shift = di * GW + dj
        if shift:
            values = pltpu.roll(values, (-shift) % TOK, 1)
        inside = (
            (line + di >= 0) & (line + di < GH) & (place + dj >= 0) & (place + dj < GW)
        )
        return jnp.where(inside, values, 0.0)

    @pl.loop(0, TOK // 128)
    def _(t):
        at = pl.ds(pl.multiple_of(t * 128, 128), 128)
        value = field[:, at].astype(F32)
        act = (value * cdf(value)).astype(BF16).astype(F32)
        for k in range(9):
            shifted[k : k + 1, at] = jnp.sum(act * taps[k], axis=0, keepdims=True)
        shifted[9:10, at] = jnp.sum(value * taps[9], axis=0, keepdims=True)

    pred = shifted[9:10, :]
    for k in range(9):
        pred = pred + moved(shifted[k : k + 1, :], k // 3 - 1, k % 3 - 1)
    for index in range(8):
        rows_buf[index : index + 1, :] = pred[:, index * STRIP : (index + 1) * STRIP]
    pred_all[c] = rows_buf[...]
    pred_copy = remote(pred_all.at[c], pred_all.at[c], partner)
    fad.wait_recv()
    fad2 = send(ga, 1, 1, down)
    share(("ga", 1, 1, ""), ga, 1, 1)
    fau.wait_recv()
    share(("ga", 3, 1, ""), ga, 3, 1)

    @pl.loop(0, TOK // 128)
    def _(t):
        at = pl.ds(pl.multiple_of(t * 128, 128), 128)
        field_slope[:, at] = slope(field[:, at].astype(F32))

    valid = jnp.concatenate([st_col[index][2:3] for index in range(8)], axis=0)
    target = jnp.concatenate([st_col[index][3:4] for index in range(8)], axis=0)
    pred_copy.wait_recv()
    err = valid * (pred_all[0] + pred_all[1] - target)

    def whole(values):
        return jnp.sum(jnp.sum(values, axis=1, keepdims=True), axis=0, keepdims=True)

    count = whole(valid)
    mean_err = whole(err) / count
    loss_ref[0, 0] = jnp.sum(whole(err * err) / count - FOCUS * mean_err * mean_err)
    grad_pred = valid * (2.0 * err - 2.0 * FOCUS * mean_err)
    grad_pred = jnp.concatenate([grad_pred[index : index + 1] for index in range(8)], axis=1)
    for k in range(9):
        shifted[k : k + 1, :] = moved(grad_pred, 1 - k // 3, 1 - k % 3)
    shifted[9:10, :] = grad_pred

    @pl.loop(0, TOK // 128)
    def _(t):
        at = pl.ds(pl.multiple_of(t * 128, 128), 128)
        back = taps[0] * shifted[0:1, at]
        for k in range(1, 9):
            back = back + taps[k] * shifted[k : k + 1, at]
        gz[pl.ds(first_channel, 128), at] = (
            taps[9] * shifted[9:10, at] + field_slope[:, at] * back
        ).astype(BF16)

    half_z = gz.at[pl.ds(first_channel, 128)]
    gz_copy = remote(half_z, half_z, partner)

    second_channel = pl.multiple_of(other * 128, 128)
    gh_own[:, pl.ds(first_channel, 128)] = nt(hid[...], half_z[...]).astype(BF16)
    gz_copy.wait_recv()
    gh_own[:, pl.ds(second_channel, 128)] = nt(
        hid[...], gz[pl.ds(second_channel, 128), :]
    ).astype(BF16)
    local(gh_own, gh_out.at[own_rows(0, 0)])
    gh_copies = [
        remote(gh_own, gh_out.at[own_rows(0, 0)], at_row(dz, dh, 0)) for dz, dh in chip_peers
    ]
    gh_pair = [remote(gh_own, gh_out.at[own_rows(0, 0)], partner)]
    def ready(dz):
        for key, copy in pair.items():
            if key[1] == dz:
                copy.wait_recv()

    n_mine = n_t.at[pl.ds(feature_at, FEAT)]

    def column(dz):
        @pl.loop(0, 2)
        def _(core):
            base = core * 8 + zz(dz) * 2
            for half in (0, 1):
                rows = slice(half * OWN, (half + 1) * OWN)
                weights = gm[base + half]
                grad[rows, :TA] = (
                    mm(weights, gz[:, :TA]) * ga[base + half].astype(F32)
                ).astype(BF16)
                grad[rows, TA:] = (
                    mm(weights, gz[:, TA:]) * gb[base + half].astype(F32)
                ).astype(BF16)
            up_own[dz, core] = nt(n_mine[...], grad[...])
            at = pl.multiple_of(base * OWN, 2 * OWN)
            pltpu.make_async_copy(
                up_own.at[dz, core], up_out.at[:, pl.ds(at, 2 * OWN)], out_sems.at[dz, core]
            ).start()

    f_m.wait_recv()
    share(("gb", 3, 1, ""), gb, 3, 1)
    f_p.wait_recv()
    share(("gb", 1, 1, ""), gb, 1, 1)
    ready(0)
    column(0)
    f_top.wait_recv()
    share(("gb", 2, 1, "top"), gb, 2, 1, top)
    f_low.wait_recv()
    share(("gb", 2, 1, "low"), gb, 2, 1, low)
    ready(3)
    column(3)
    au2.wait_recv()
    share(("ga", 2, 0, ""), ga, 2, 0)
    ready(1)
    column(1)
    fad2.wait_recv()
    share(("ga", 2, 1, ""), ga, 2, 1)
    ready(2)
    column(2)

    for (dz, dh), copy in zip(chip_peers, gh_copies):
        copy.wait_recv()
        came = gh_out.at[own_rows(-dz, dh)]
        gh_pair.append(remote(came, came, partner))
    for copy in gh_pair:
        copy.wait_recv()

    for dz in range(4):

        @pl.loop(0, 2)
        def _(core):
            at = pl.multiple_of((core * 8 + zz(dz) * 2) * OWN, 2 * OWN)
            pltpu.make_async_copy(
                up_own.at[dz, core], up_out.at[:, pl.ds(at, 2 * OWN)], out_sems.at[dz, core]
            ).wait()

    started[-1].wait()
    for copy in sent:
        copy.wait_send()


def weight_kernel(gh_hbm, proj_hbm, up_hbm, up_out, down_out, gh, proj, up, down, in_sems, out_sems):
    rows, lines = HID // N_DOWN, FEAT // N_UP

    def down_at(index):
        return pl.ds(index * rows, rows)

    def up_at(index):
        return pl.ds(index * lines, lines)

    proj_in = pltpu.make_async_copy(proj_hbm, proj, in_sems.at[0])
    gh_in = [
        pltpu.make_async_copy(gh_hbm.at[down_at(k)], gh.at[down_at(k)], in_sems.at[1 + k])
        for k in range(N_DOWN)
    ]
    up_in = [
        pltpu.make_async_copy(up_hbm.at[up_at(k)], up.at[up_at(k)], in_sems.at[1 + N_DOWN + k])
        for k in range(N_UP)
    ]
    for copy in [proj_in] + gh_in + up_in:
        copy.start()
    leaving = []
    proj_in.wait()
    for k in range(N_DOWN):
        gh_in[k].wait()
        down[down_at(k), :] = nt(gh[down_at(k), :], proj[...])
        leaving.append(
            pltpu.make_async_copy(down.at[down_at(k)], down_out.at[down_at(k)], out_sems.at[k])
        )
        leaving[-1].start()
    for k in range(N_UP):
        up_in[k].wait()
        leaving.append(
            pltpu.make_async_copy(up.at[up_at(k)], up_out.at[up_at(k)], out_sems.at[N_DOWN + k])
        )
        leaving[-1].start()
    for copy in leaving:
        copy.wait()


def on_device(tokens, ln_gain, w_up, w_down, proj, conv_kernel, head_weight, depth_mm, lidar_mask):
    vmem = pl.BlockSpec(memory_space=pltpu.VMEM)
    anywhere = pl.BlockSpec(memory_space=pl.ANY)
    up_held, grad_hidden, loss = pl.pallas_call(
        step_kernel,
        name="mlp_step",
        out_shape=[
            jax.ShapeDtypeStruct((FEAT, HID), F32),
            jax.ShapeDtypeStruct((HID, CH), BF16),
            jax.ShapeDtypeStruct((1, 1), F32),
        ],
        in_specs=[
            anywhere, vmem, anywhere, anywhere, anywhere, anywhere, vmem, anywhere, anywhere,
        ],
        out_specs=[anywhere, anywhere, pl.BlockSpec(memory_space=pltpu.SMEM)],
        scratch_shapes=[
            pltpu.VMEM((STRIP, FEAT), BF16),
            pltpu.VMEM((FEAT, HID), BF16),
            pltpu.VMEM((HID, FEAT), BF16),
            pltpu.VMEM((FEAT, CH), BF16),
            pltpu.VMEM((9, 128, CH), BF16),
            pltpu.VMEM((2, GW), jnp.int32),
            pltpu.VMEM((2, GW), jnp.int32),
            pltpu.VMEM((8, FEAT, STRIP), BF16),
            pltpu.VMEM((16, 8, STRIP), F32),
            pltpu.VMEM((8, 8, STRIP), F32),
            pltpu.VMEM((HALF, 2 * FEAT), BF16),
            pltpu.VMEM((HALF, FEAT), BF16),
            pltpu.VMEM((HALF, FEAT), BF16),
            pltpu.VMEM((FEAT, CH), BF16),
            pltpu.VMEM((2 * FEAT, TOK), BF16),
            pltpu.VMEM((8, OWN, CH), F32),
            pltpu.VMEM((8, OWN, CH), BF16),
            pltpu.VMEM((7, OWN, CH), BF16),
            pltpu.VMEM((OWN, CH), BF16),
            pltpu.VMEM((4, 2, OWN, TA), BF16),
            pltpu.VMEM((4, 2, OWN, TB), BF16),
            pltpu.VMEM((2, OWN, TA), BF16),
            pltpu.VMEM((2, 2, OWN, TA), BF16),
            pltpu.VMEM((OWN, TA), BF16),
            pltpu.VMEM((4, OWN, TB), BF16),
            pltpu.VMEM((2, OWN // 2, TB), BF16),
            pltpu.VMEM((2, OWN, TB), BF16),
            pltpu.VMEM((OWN, TOK), F32),
            pltpu.VMEM((OWN, TOK), BF16),
            pltpu.VMEM((CH, TOK), F32),
            pltpu.VMEM((128, TOK), BF16),
            pltpu.VMEM((128, TOK), BF16),
            pltpu.VMEM((128, TOK), BF16),
            pltpu.VMEM((7, 16, TOK), BF16),
            pltpu.VMEM((8, 16, TOK), BF16),
            pltpu.VMEM((10, 128, 128), F32),
            pltpu.VMEM((128, TOK), BF16),
            pltpu.VMEM((128, TOK), F32),
            pltpu.VMEM((16, TOK), F32),
            pltpu.VMEM((2, 8, STRIP), F32),
            pltpu.VMEM((8, STRIP), F32),
            pltpu.VMEM((CH, TOK), BF16),
            pltpu.VMEM((16, OWN, CH), BF16),
            pltpu.VMEM((16, OWN, TA), BF16),
            pltpu.VMEM((16, OWN, TB), BF16),
            pltpu.VMEM((OWN, CH), BF16),
            pltpu.VMEM((2 * OWN, TOK), BF16),
            pltpu.VMEM((4, 2, FEAT, 2 * OWN), F32),
            pltpu.SemaphoreType.DMA((N_SEMS,)),
            pltpu.SemaphoreType.DMA((N_SEMS,)),
            pltpu.SemaphoreType.DMA((9,)),
            pltpu.SemaphoreType.DMA((4, 2)),
        ],
        compiler_params=pltpu.CompilerParams(
            collective_id=0, has_side_effects=True, vmem_limit_bytes=60 * 2**20
        ),
        cost_estimate=pl.CostEstimate(flops=6 * 10**9, bytes_accessed=16 * 2**20, transcendentals=10**6),
    )(
        tokens, ln_gain, w_up, w_down, proj, conv_kernel.reshape(9, CH, CH),
        head_weight.reshape(1, CH), depth_mm, lidar_mask,
    )
    grad_up, grad_down = pl.pallas_call(
        weight_kernel,
        name="weight_grads",
        out_shape=[
            jax.ShapeDtypeStruct((FEAT, HID), F32),
            jax.ShapeDtypeStruct((HID, FEAT), F32),
        ],
        in_specs=[anywhere, anywhere, anywhere],
        out_specs=[anywhere, anywhere],
        scratch_shapes=[
            pltpu.VMEM((HID, CH), BF16),
            pltpu.VMEM((FEAT, CH), BF16),
            pltpu.VMEM((FEAT, HID), F32),
            pltpu.VMEM((HID, FEAT), F32),
            pltpu.SemaphoreType.DMA((1 + N_DOWN + N_UP,)),
            pltpu.SemaphoreType.DMA((N_DOWN + N_UP,)),
        ],
        compiler_params=pltpu.CompilerParams(vmem_limit_bytes=60 * 2**20),
        cost_estimate=pl.CostEstimate(flops=6 * 10**8, bytes_accessed=16 * 2**20, transcendentals=0),
    )(grad_hidden, proj, up_held)
    return (grad_up, grad_down, loss.reshape(()))


def solution(mesh):
    return jax.shard_map(
        on_device,
        mesh=mesh,
        in_specs=(
            P("col", "row"),
            P("row"),
            P("row", "col"),
            P("col", "row"),
            P("row", None),
            P(),
            P(),
            P("col", None),
            P("col", None),
        ),
        out_specs=(P("row", "col"), P("col", "row"), P()),
        check_vma=False,
    )
```
